128 devices in a mesh: px: 16 (over z, y), py: 8 (over x, core).
Axes of the slice: x: 4, y: 4, z: 4, core: 2. Of those that a mesh axis runs over, the one named last changes fastest.
Arguments:
- right_side: float32 [4, 5, 5, 5, 32, 16, 128], P(None, None, None, None, 'px', 'py'), may hold values from -6 to 6
- first_guess: float32 [4, 5, 5, 5, 32, 16, 128], P(None, None, None, None, 'px', 'py'), may hold values from -6 to 6
- coefficient: float32 [32, 16, 128], P('px', 'py'), may hold values from 0.2 to 2
- modal_basis: float32 [5, 5], replicated, may hold values from -1 to 1, as said below
- modal_values: float32 [5], replicated, may hold values from 0.5 to 4
- patch_inverse: float32 [256, 256], replicated, may hold values from -0.018 to 0.018
- patch_elements: int32 [65536, 8], P(('px', 'py')), may hold values from 0 to 65535, as said below
- patch_mask: int32 [65536, 8], P(('px', 'py')), may hold values from 0 to 1, as said below
Outputs:
- solution: float32 [4, 5, 5, 5, 32, 16, 128], P(None, None, None, None, 'px', 'py')
The draws below stay inside these ranges and needn't reach their ends.
Inputs may be any that keep to these rules, and one draw needn't show every extreme that they name: `modal_basis`: an orthogonal matrix. `patch_elements`: element number e = (x 16 + y) * 128 + z. Row r belongs to block b = r // 512 with bx = b // 8 and by = b % 8; every slot of the row, live or padded, names an element with bx * 2 - 1 <= x <= bx * 2 + 2 and by * 2 - 1 <= y <= by * 2 + 2. The live slots of a row name distinct elements that share one mesh vertex. `patch_mask`: padded slots belong to patches of vertices on the boundary of the grid.
All inputs are finite; a program needn't handle non-finite values.
Results may differ from the reference program's by a relative error of at most 0.0001.
Values sent between devices are 32-bit elements; how exact they have to be, the bound alone decides.
A program may use at most 64 MiB of HBM per device.

```python
import math
import jax
import jax.numpy as jnp
from jax import lax

NP = 5
FIELDS = 4
EX = 2
EY = 2
EZ = 128
NEX = 32
NEY = 16
PVEC = 256


def draw_modal_basis(key, part):
    basis_key = jax.random.fold_in(key, 3)
    raw_matrix = jax.random.normal(basis_key, (NP, NP), jnp.float32)
    factor_q, factor_r = jnp.linalg.qr(raw_matrix)
    return factor_q.astype(jnp.float32)


def patch_layout(key):
    base_key = jax.random.fold_in(key, 11)
    key_shift_one, key_shift_two, key_rows, key_slots = jax.random.split(base_key, 4)
    blocks_first = NEX // EX
    blocks_second = NEY // EY
    blocks_all = blocks_first * blocks_second
    per_block = EX * EY * EZ
    shift_first = jax.random.randint(key_shift_one, (EZ,), 0, 2).reshape(1, 1, 1, 1, EZ, 1)
    shift_second = jax.random.randint(key_shift_two, (EZ,), 0, 2).reshape(1, 1, 1, 1, EZ, 1)
    block_first = jnp.arange(blocks_first).reshape(blocks_first, 1, 1, 1, 1, 1)
    block_second = jnp.arange(blocks_second).reshape(1, blocks_second, 1, 1, 1, 1)
    local_first = jnp.arange(EX).reshape(1, 1, EX, 1, 1, 1)
    local_second = jnp.arange(EY).reshape(1, 1, 1, EY, 1, 1)
    local_third = jnp.arange(EZ).reshape(1, 1, 1, 1, EZ, 1)
    slot_id = jnp.arange(8).reshape(1, 1, 1, 1, 1, 8)
    vertex_first = block_first * EX + local_first + shift_first
    vertex_second = block_second * EY + local_second + shift_second
    cell_first = vertex_first - 1 + slot_id // 4
    cell_second = vertex_second - 1 + slot_id // 2 % 2
    cell_third = local_third - 1 + slot_id % 2
    inside = (cell_first >= 0) & (cell_first < NEX) & (cell_second >= 0) & (cell_second < NEY)
    inside = inside & (cell_third >= 0) & (cell_third < EZ)
    element_ids = (jnp.clip(cell_first, 0, NEX - 1) * NEY + jnp.clip(cell_second, 0, NEY - 1)) * EZ
    element_ids = element_ids + jnp.clip(cell_third, 0, EZ - 1)
    full_shape = (blocks_first, blocks_second, EX, EY, EZ, 8)
    element_ids = jnp.broadcast_to(element_ids, full_shape).reshape(blocks_all, per_block, 8)
    inside = jnp.broadcast_to(inside, full_shape).reshape(blocks_all, per_block, 8).astype(jnp.int32)

    def shuffle_rows(row_key):
        return jax.random.permutation(row_key, per_block)
    row_order = jax.vmap(shuffle_rows)(jax.random.split(key_rows, blocks_all))
    element_ids = jnp.take_along_axis(element_ids, row_order[:, :, None], axis=1)
    inside = jnp.take_along_axis(inside, row_order[:, :, None], axis=1)
    scores = jax.random.randint(key_slots, (blocks_all, per_block, 8), 0, 1 << 20) * 8 + jnp.arange(8)
    slot_order = jnp.argsort(scores, axis=-1)
    element_ids = jnp.take_along_axis(element_ids, slot_order, axis=-1)
    inside = jnp.take_along_axis(inside, slot_order, axis=-1)
    return (element_ids.reshape(blocks_all * per_block, 8).astype(jnp.int32), inside.reshape(blocks_all * per_block, 8).astype(jnp.int32))


def draw_patch_elements(key, part):
    return patch_layout(key)[0]


def draw_patch_mask(key, part):
    return patch_layout(key)[1]


def level_of(own_key, shape, shards, least, high):
    def one(axis_at, shards_of):
        heights = jax.random.uniform(jax.random.fold_in(jax.random.fold_in(own_key, 6), axis_at), (shards_of,), jnp.float32, least / len(shards), high / len(shards))
        return jnp.repeat(jnp.exp(heights), shape[axis_at] // shards_of).reshape((-1,) + (1,) * (len(shape) - axis_at - 1))

    gain = one(*shards[0])
    for cut in shards[1:]:
        gain = gain * one(*cut)
    return gain


def normal_values(rng, shape, width, limit, shards=(), kind=jnp.bfloat16):
    level = level_of(rng, shape, shards, -0.22, 0.18) if shards else 1.0
    drawn = jax.random.normal(rng, shape, jnp.float32) * width * level
    return jnp.minimum(jnp.maximum(drawn, -limit), limit).astype(kind)


def setup_inputs(seed: int = 0) -> dict:
    streams_of = jax.random.split(jax.random.key(seed), 9)
    right_side = normal_values(streams_of[0], (FIELDS, NP, NP, NP, NEX, NEY, EZ), 1.0, 6.0, ((4, 16), (5, 8)), jnp.float32)
    first_guess = normal_values(streams_of[1], (FIELDS, NP, NP, NP, NEX, NEY, EZ), 1.0, 6.0, ((4, 16), (5, 8)), jnp.float32)
    coefficient = jnp.clip(jnp.exp(math.log(2.0) - 2.3025851 * jax.random.uniform(streams_of[2], (NEX, NEY, EZ), jnp.float32) ** level_of(streams_of[2], (NEX, NEY, EZ), ((0, 16), (1, 8)), -0.2, 0.2)), 0.2, 2.0)
    modal_basis = draw_modal_basis(jax.random.fold_in(streams_of[8], 71), 0)
    modal_values = jnp.clip(jnp.exp(jax.random.uniform(streams_of[4], (NP,), jnp.float32, math.log(0.5), math.log(4.0))), 0.5, 4.0)
    patch_inverse = normal_values(streams_of[5], (PVEC, PVEC), 0.003, 0.018, (), jnp.float32)
    patch_elements = draw_patch_elements(jax.random.fold_in(streams_of[8], 71), 0)
    patch_mask = draw_patch_mask(jax.random.fold_in(streams_of[8], 71), 0)
    return dict(right_side=right_side, first_guess=first_guess, coefficient=coefficient, modal_basis=modal_basis, modal_values=modal_values, patch_inverse=patch_inverse, patch_elements=patch_elements, patch_mask=patch_mask)


MASS_SHIFT = 1.0
FACE_PENALTY = 0.5
DAMPING = 0.8
PRECISE = lax.Precision.HIGHEST
PATTERNS = ('ai,fijkxyz->fajkxyz', 'bj,fijkxyz->fibkxyz', 'ck,fijkxyz->fijcxyz')

def linear_table():
    root = math.sqrt(3.0 / 7.0)
    points = jnp.array([-1.0, -root, 0.0, root, 1.0], dtype=jnp.float32)
    return jnp.stack([(1.0 - points) * 0.5, (1.0 + points) * 0.5], axis=1)

def apply_all(matrix, vector):
    for pattern in PATTERNS:
        vector = jnp.einsum(pattern, matrix, vector, precision=PRECISE)
    return vector

def stiffness(matrix, vector):
    result = jnp.zeros_like(vector)
    for pattern in PATTERNS:
        result = result + jnp.einsum(pattern, matrix, vector, precision=PRECISE)
    return result

def leading(layer_data, dimension):
    extent = layer_data.shape[dimension]
    kept_part = lax.slice_in_dim(layer_data, 1, extent, axis=dimension)
    rim_zeros = jnp.zeros_like(lax.slice_in_dim(layer_data, 0, 1, axis=dimension))
    return jnp.concatenate([kept_part, rim_zeros], axis=dimension)

def trailing(layer_data, dimension):
    extent = layer_data.shape[dimension]
    kept_part = lax.slice_in_dim(layer_data, 0, extent - 1, axis=dimension)
    rim_zeros = jnp.zeros_like(lax.slice_in_dim(layer_data, 0, 1, axis=dimension))
    return jnp.concatenate([rim_zeros, kept_part], axis=dimension)

def add_couplings(vector, upper_first, lower_first, upper_second, lower_second):
    top_node = vector.shape[1] - 1
    upper_third = leading(vector[:, :, :, 0], 5)
    lower_third = trailing(vector[:, :, :, top_node], 5)
    coupled = jnp.zeros_like(vector)
    coupled = coupled.at[:, top_node].add(upper_first)
    coupled = coupled.at[:, 0].add(lower_first)
    coupled = coupled.at[:, :, top_node].add(upper_second)
    coupled = coupled.at[:, :, 0].add(lower_second)
    coupled = coupled.at[:, :, :, top_node].add(upper_third)
    coupled = coupled.at[:, :, :, 0].add(lower_third)
    return coupled

def operate(vector, coefficient, stiff_matrix):
    top_node = vector.shape[1] - 1
    coupled = add_couplings(vector, leading(vector[:, 0], 3), trailing(vector[:, top_node], 3), leading(vector[:, :, 0], 4), trailing(vector[:, :, top_node], 4))
    return coefficient * stiffness(stiff_matrix, vector) + MASS_SHIFT * vector - FACE_PENALTY * coupled

def schwarz(coarse, patch_inverse, patch_elements, patch_mask):
    count_values = coarse.shape[0]
    flattened = coarse.reshape(count_values, -1)
    column = patch_elements.T
    alive_slots = patch_mask.T.astype(jnp.float32)
    gathered = jnp.take(flattened, column, axis=1) * alive_slots
    solved = jnp.dot(patch_inverse, gathered.reshape(count_values * column.shape[0], -1), precision=PRECISE)
    solved = solved.reshape(gathered.shape) * alive_slots
    spread = jnp.zeros_like(flattened).at[:, column.reshape(-1)].add(solved.reshape(count_values, -1))
    return spread.reshape(coarse.shape)

def reference(right_side, first_guess, coefficient, modal_basis, modal_values, patch_inverse, patch_elements, patch_mask):
    stiff_matrix = jnp.dot(modal_basis * modal_values[None, :], modal_basis.T, precision=PRECISE)
    spectrum = modal_values[:, None, None] + modal_values[None, :, None] + modal_values[None, None, :]
    inverse_diag = 1.0 / (coefficient[None, None, None, None] * spectrum[None, :, :, :, None, None, None] + MASS_SHIFT)

    def smooth(remainder):
        return apply_all(modal_basis, apply_all(modal_basis.T, remainder) * inverse_diag)
    table = linear_table()
    residual = right_side - operate(first_guess, coefficient, stiff_matrix)
    solution = first_guess + DAMPING * smooth(residual)
    residual = right_side - operate(solution, coefficient, stiff_matrix)
    restricted = apply_all(table.T, residual)
    coarse = restricted.reshape((-1,) + restricted.shape[4:])
    correction = schwarz(coarse, patch_inverse, patch_elements, patch_mask)
    solution = solution + apply_all(table, correction.reshape(restricted.shape))
    residual = right_side - operate(solution, coefficient, stiff_matrix)
    return solution + DAMPING * smooth(residual)
```

```python
import math

import jax
import jax.numpy as jnp
import numpy as np
from jax import lax
from jax.experimental import pallas as pl
from jax.experimental.pallas import tpu as pltpu
from jax.sharding import PartitionSpec as P

MESH = pl.DeviceIdType.MESH
F32 = jnp.float32
BF16 = jnp.bfloat16
DIRS = ((1, 0), (-1, 0), (0, 1), (0, -1), (1, 1), (1, -1), (-1, 1), (-1, -1))
LANES = 512


def linear_values():
    root = np.float32(math.sqrt(3.0 / 7.0))
    points = np.array([-1.0, -root, 0.0, root, 1.0], np.float32)
    half = np.float32(0.5)
    return (1 - points) * half, (1 + points) * half


def column_table():
    table = np.full((8, 640), 7, np.int32)
    table[3] = 9

    def put(column, i, j, k, f=9):
        table[0:4, column] = (i, j, k, f)

    for n in range(125):
        put(n, n // 25, n // 5 % 5, n % 5)
    for g in range(25):
        u, v = g // 5, g % 5
        put(128 + g, 4, u, v)
        put(160 + g, 0, u, v)
        put(192 + u * 8 + v, u, 4, v)
        put(232 + u * 8 + v, u, 0, v)
        put(272 + g, u, v, 4)
        put(304 + g, u, v, 0)
    for r in range(32):
        a, b, f, c = r // 16, r // 8 % 2, r // 2 % 4, r % 2
        for copy in range(3):
            put(384 + 32 * copy + r, 5 + a, 5 + b, 5 + c, f)
        put(512 + 64 + r, 5 + a, 5 + b, 4 if c == 0 else 0, f)
    for r in range(16):
        h, f, c = r // 8, r // 2 % 4, r % 2
        put(512 + r, 4, 5 + h, 5 + c, f)
        put(528 + r, 0, 5 + h, 5 + c, f)
        put(544 + r, 5 + h, 4, 5 + c, f)
        put(560 + r, 5 + h, 0, 5 + c, f)
    return table


def split(value):
    high = value.astype(BF16)
    return high, (value - high.astype(F32)).astype(BF16)


def dot(a, b):
    return lax.dot_general(a, b, (((1,), (0,)), ((), ())), preferred_element_type=F32)


def dot_nt(a, b):
    return lax.dot_general(a, b, (((1,), (1,)), ((), ())), preferred_element_type=F32)


def mm3(ah, al, x):
    xh, xl = split(x)
    return dot(ah, xh) + dot(ah, xl) + dot(al, xh)


def iota(shape, dim):
    return lax.broadcasted_iota(jnp.int32, shape, dim)


def a_half(v, a):
    return v[16 * a : 16 * a + 16]


def b_half(v, b):
    return jnp.concatenate([v[8 * b : 8 * b + 8], v[16 + 8 * b : 24 + 8 * b]], axis=0)


def add_a(v, a, h):
    parts = [v[0:16], v[16:32]]
    parts[a] = parts[a] + h
    return jnp.concatenate(parts, axis=0)


def add_b(v, b, h):
    parts = [v[0:8], v[8:16], v[16:24], v[24:32]]
    parts[b] = parts[b] + h[0:8]
    parts[2 + b] = parts[2 + b] + h[8:16]
    return jnp.concatenate(parts, axis=0)


def rows_to(v, rows):
    return jnp.concatenate([v, jnp.zeros((rows - v.shape[0], v.shape[1]), v.dtype)], axis=0)


def from_next(v):
    lane = iota(v.shape, 1)
    return jnp.where(lane == 127, 0.0, pltpu.roll(v, 127, 1))


def from_previous(v):
    lane = iota(v.shape, 1)
    return jnp.where(lane == 0, 0.0, pltpu.roll(v, 1, 1))


def by_column(fn, v):
    return jnp.concatenate([fn(v[:, 128 * c : 128 * c + 128]) for c in range(4)], axis=1)


def kernel(
    nx, ny,
    xa, xx, xy, xz, ba, coef_h, ub, mv, pinv_h, pe_h, pm_h, tab_h,
    out_h,
    xin, bin_, nfx, nfy, nfz, coef, pinv, pe, pm, tab,
    bt_h, bt_l, bte_h, bte_l, bb_h, bb_l, fb_h, fb_l,
    qc_h, qc_l, qf_h, qf_l, tc, tf_h, tf_l, mi_h, mi_l,
    xhat, bhat, dinv, oh, xs_h, xs_l, ts_h, ts_l,
    cp, gath, wh, wl, ans, ap, vv,
    sx, sy, rx, ry, fz, s2, r2, s3, r3, outv,
    lsem, ssem1, rsem1, ssemf, rsemf, ssem2, rsem2, ssem3, rsem3,
):
    px, py = lax.axis_index("px"), lax.axis_index("py")

    def peer(dx, dy):
        return (lax.rem(px + dx + nx, nx), lax.rem(py + dy + ny, ny))

    local = []

    def load(src, dst):
        copy = pltpu.make_async_copy(src, dst, lsem.at[len(local)])
        copy.start()
        local.append(copy)

    load(tab_h, tab)
    load(coef_h, coef)
    load(xa.at[:, :, 0, :], xin)
    load(ba.at[:, :, 0, :], bin_)
    load(pe_h, pe)
    load(pm_h, pm)
    load(pinv_h, pinv)
    load(xx.at[:, 0, :, 1, 0, :], nfx.at[0, :, :, pl.ds(0, 256)])
    load(xx.at[:, 4, :, 0, 0, :], nfx.at[1, :, :, pl.ds(256, 256)])
    for x in range(2):
        load(xy.at[:, :, 0, :, x, 1, 0, :], nfy.at[0, :, :, :, pl.ds(256 * x, 128)])
        load(xy.at[:, :, 4, :, x, 0, 0, :], nfy.at[1, :, :, :, pl.ds(256 * x + 128, 128)])
    load(xz.at[:, :, 0, 0, :], nfz.at[0])
    load(xz.at[:, :, 4, 0, :], nfz.at[1])

    barrier = pltpu.get_barrier_semaphore()
    for dx, dy in DIRS:
        pl.semaphore_signal(barrier, inc=1, device_id=peer(dx, dy), device_id_type=MESH)
    pl.semaphore_wait(barrier, 8)

    sent = []

    def send(src, dst, ssem, rsem, to):
        copy = pltpu.make_async_remote_copy(
            src_ref=src, dst_ref=dst, send_sem=ssem, recv_sem=rsem, device_id=to, device_id_type=MESH
        )
        copy.start()
        sent.append(copy)
        return copy

    first = [
        send(xx.at[:, 4, :, 1, 0, :], nfx.at[1, :, :, pl.ds(0, 256)], ssem1.at[0], rsem1.at[0], peer(1, 0)),
        send(xx.at[:, 0, :, 0, 0, :], nfx.at[0, :, :, pl.ds(256, 256)], ssem1.at[1], rsem1.at[1], peer(-1, 0)),
    ]
    for x in range(2):
        first.append(
            send(xy.at[:, :, 4, :, x, 1, 0, :], nfy.at[1, :, :, :, pl.ds(256 * x, 128)],
                 ssem1.at[2 + 2 * x], rsem1.at[2 + 2 * x], peer(0, 1))
        )
        first.append(
            send(xy.at[:, :, 0, :, x, 0, 0, :], nfy.at[0, :, :, :, pl.ds(256 * x + 128, 128)],
                 ssem1.at[3 + 2 * x], rsem1.at[3 + 2 * x], peer(0, -1))
        )

    basis = [[ub[p, q] for q in range(5)] for p in range(5)]
    for weights in linear_values():
        basis.append([sum(float(weights[i]) * basis[i][q] for i in range(5)) for q in range(5)])
    spectrum = [mv[q] for q in range(5)]
    local[0].wait()
    local[1].wait()

    def mode_index(shape):
        row = iota(shape, 0)
        i = (row * 41) >> 10
        rest = row - 25 * i
        j = (rest * 13) >> 6
        return i, j, rest - 5 * j

    def block(start):
        modes = mode_index((128, 128))
        result = None
        for d in range(3):
            index = tab[d : d + 1, start : start + 128]
            hits = [index == p for p in range(7)]
            grown = jnp.zeros((128, 128), F32)
            for q in range(5):
                line = jnp.zeros((1, 128), F32)
                for p in range(7):
                    line = jnp.where(hits[p], basis[p][q], line)
                grown = jnp.where(modes[d] == q, line, grown)
            result = grown if result is None else result * grown
        return result

    nodes = block(0)
    bt_h[...], bt_l[...] = split(nodes)
    bb_h[...], bb_l[...] = split(nodes.T)
    for part in range(2):
        faces = block(128 + 128 * part)
        span = pl.ds(128 * part, 128)
        bte_h[:, span], bte_l[:, span] = split(faces)
        fb_h[span, :], fb_l[span, :] = split(faces.T)
    field = tab[3:4, 384:512]
    coarse_block = block(384)
    copy_of = iota((128, 128), 1)
    for f in range(4):
        part = jnp.where(field == f, coarse_block, 0.0)
        high, low = split(part)
        tc[pl.ds(128 * f, 128), :] = jnp.where(copy_of < 64, high.astype(F32), low.astype(F32)).astype(BF16)
        turned = part.T
        qc_h[:, pl.ds(128 * f, 128)], qc_l[:, pl.ds(128 * f, 128)] = split(turned[0:32])
    field = tab[3:4, 512:640]
    face_block = block(512)
    for f in range(4):
        part = jnp.where(field == f, face_block, 0.0)
        tf_h[pl.ds(128 * f, 128), :], tf_l[pl.ds(128 * f, 128), :] = split(part)
        turned = part.T
        qf_h[:, pl.ds(128 * f, 128)], qf_l[:, pl.ds(128 * f, 128)] = split(turned[0:96])

    modes = mode_index((128, 128))
    total = jnp.zeros((128, 128), F32)
    for d in range(3):
        for q in range(5):
            total = jnp.where(modes[d] == q, total + spectrum[q], total)

    def diagonal(c):
        return total * coef[c : c + 1, :] + 1.0

    for c in range(4):
        dinv[:, pl.ds(128 * c, 128)] = 1.0 / diagonal(c)

    local[2].wait()
    local[3].wait()
    for f in range(4):
        xhat[f] = mm3(bt_h[...], bt_l[...], rows_to(xin[f], 128))
        bhat[f] = mm3(bt_h[...], bt_l[...], rows_to(bin_[f], 128))

    local[4].wait()
    local[5].wait()
    elements = pe[...]
    alive = pm[...] != 0
    at_x = (elements >> 11) - 2 * px + 1
    at_y = ((elements >> 7) & 15) - 2 * py + 1
    at_z = elements & 127

    def least(v, most):
        return jnp.minimum(jnp.min(jnp.where(alive, v, most), axis=0, keepdims=True), most)

    low_x, low_y, low_z = least(at_x, 2), least(at_y, 2), least(at_z, 126)
    key = (low_x * 3 + low_y) * 128 + low_z
    place = (at_x - low_x) * 4 + (at_y - low_y) * 2 + (at_z - low_z)
    place = jnp.where(alive, place, 99)
    vertex = iota((128, LANES), 0)
    for v in range(9):
        oh[pl.ds(128 * v, 128), :] = jnp.where(vertex + 128 * v == key, 1.0, 0.0).astype(BF16)

    local[6].wait()
    r = iota((256, 256), 0)
    source = (((r >> 1) & 3) * 8 + ((r >> 4) & 1) * 4 + ((r >> 3) & 1) * 2 + (r & 1)) * 8 + (r >> 5)
    order = jnp.where(iota((256, 256), 1) == source, 1.0, 0.0).astype(BF16)
    for piece, target in zip(split(pinv[...]), (mi_h, mi_l)):
        target[...] = dot_nt(dot(order, piece).astype(BF16), order).astype(BF16)

    has = {
        (1, 0): jnp.where(px < nx - 1, 1.0, 0.0),
        (-1, 0): jnp.where(px > 0, 1.0, 0.0),
        (0, 1): jnp.where(py < ny - 1, 1.0, 0.0),
        (0, -1): jnp.where(py > 0, 1.0, 0.0),
    }
    lane = iota((1, LANES), 1)
    upper_x = jnp.where(lane >= 256, has[(1, 0)], 1.0)
    lower_x = jnp.where(lane < 256, has[(-1, 0)], 1.0)
    upper_y = jnp.where(((lane >> 7) & 1) == 1, has[(0, 1)], 1.0)
    lower_y = jnp.where(((lane >> 7) & 1) == 0, has[(0, -1)], 1.0)

    for copy in local[7:]:
        copy.wait()
    for copy in first:
        copy.wait_recv()

    for f in range(4):
        parts = [
            rows_to(nfx[0, f], 32) * upper_x,
            rows_to(nfx[1, f], 32) * lower_x,
        ]
        parts += [rows_to(nfy[0, f, i], 8) * upper_y for i in range(5)]
        parts += [rows_to(nfy[1, f, i], 8) * lower_y for i in range(5)]
        parts.append(by_column(from_next, rows_to(nfz[0, f], 32)))
        parts.append(by_column(from_previous, rows_to(nfz[1, f], 32)))
        parts.append(jnp.zeros((48, LANES), F32))
        around = mm3(bte_h[...], bte_l[...], jnp.concatenate(parts, axis=0))
        loaded = bhat[f] + 0.5 * around
        x0 = xhat[f]
        x1 = 0.2 * x0 + 0.8 * (dinv[...] * loaded)
        diag = jnp.concatenate([diagonal(c) for c in range(4)], axis=1)
        rest = bhat[f] - 0.2 * (diag * x0) - 0.8 * loaded
        xhat[f] = x1
        rows = pl.ds(128 * f, 128)
        xs_h[rows, :], xs_l[rows, :] = split(x1)
        ts_h[rows, :], ts_l[rows, :] = split(rest)

    inner = dot(qc_h[...], ts_h[...]) + dot(qc_h[...], ts_l[...]) + dot(qc_l[...], ts_h[...])
    rim = 0.5 * (dot(qf_h[...], xs_h[...]) + dot(qf_h[...], xs_l[...]) + dot(qf_l[...], xs_h[...]))
    up_row = ((iota((32, 128), 0) & 1) == 1)

    def rim_of(start, size, c):
        return rim[start : start + size, 128 * c : 128 * c + 128]

    own = {}
    for x in range(2):
        for y in range(2):
            c = 2 * x + y
            v = inner[:, 128 * c : 128 * c + 128]
            faces = rim_of(64, 32, c)
            v = v + jnp.where(up_row, from_next(faces), from_previous(faces))
            v = add_a(v, 0, rim_of(0, 16, y)) if x == 1 else add_a(v, 1, rim_of(16, 16, 2 + y))
            v = add_b(v, 0, rim_of(32, 16, 2 * x)) if y == 1 else add_b(v, 1, rim_of(48, 16, 2 * x + 1))
            own[(x, y)] = v
    hx = {(1, y): rim_of(0, 16, 2 + y) for y in range(2)} | {(-1, y): rim_of(16, 16, y) for y in range(2)}
    hy = {(1, x): rim_of(32, 16, 2 * x + 1) for x in range(2)} | {(-1, x): rim_of(48, 16, 2 * x) for x in range(2)}

    def edge(d):
        return 1 if d == 1 else 0

    def exchange(blocks, sbuf, rbuf, ssem, rsem):
        copies = []
        for n, (dx, dy) in enumerate(DIRS):
            at = 0
            for v in blocks(dx, dy):
                sbuf[n, pl.ds(at, v.shape[0]), :] = v
                at += v.shape[0]
            copies.append(
                send(sbuf.at[n, pl.ds(0, at)], rbuf.at[n, pl.ds(0, at)], ssem.at[n], rsem.at[n], peer(dx, dy))
            )
        return copies

    def residual_blocks(dx, dy):
        x, y = edge(dx), edge(dy)
        if dy == 0:
            return [own[(x, 0)], own[(x, 1)], hx[(dx, 0)], hx[(dx, 1)], hy[(1, x)], hy[(-1, x)]]
        if dx == 0:
            return [own[(0, y)], own[(1, y)], hy[(dy, 0)], hy[(dy, 1)], hx[(1, y)], hx[(-1, y)]]
        return [own[(x, y)], hx[(dx, y)], hy[(dy, x)]]

    second = exchange(residual_blocks, s2, r2, ssem2, rsem2)

    for f in range(4):
        rows = pl.ds(128 * f, 128)
        for part in range(2):
            span = pl.ds(128 * part, 128)
            faces = (
                dot(fb_h[span, :], xs_h[rows, :])
                + dot(fb_h[span, :], xs_l[rows, :])
                + dot(fb_l[span, :], xs_h[rows, :])
            )
            fz[f, span, :] = faces
        sx[0, f] = fz[f, 0:32, 256:512]
        sx[1, f] = fz[f, 32:64, 0:256]
        for x in range(2):
            sy[0, f, :, pl.ds(128 * x, 128)] = fz[f, 64:104, 256 * x + 128 : 256 * x + 256]
            sy[1, f, :, pl.ds(128 * x, 128)] = fz[f, 104:144, 256 * x : 256 * x + 128]
    whole = [
        send(sx.at[0], rx.at[0], ssemf.at[0], rsemf.at[0], peer(1, 0)),
        send(sx.at[1], rx.at[1], ssemf.at[1], rsemf.at[1], peer(-1, 0)),
        send(sy.at[0], ry.at[0], ssemf.at[2], rsemf.at[2], peer(0, 1)),
        send(sy.at[1], ry.at[1], ssemf.at[3], rsemf.at[3], peer(0, -1)),
    ]

    def sender_is_there(dx, dy):
        there = 1.0
        if dx:
            there = there * has[(-dx, 0)]
        if dy:
            there = there * has[(0, -dy)]
        return there

    for copy in second:
        copy.wait_recv()
    field_of = {}

    def put(at, v):
        field_of[at] = field_of[at] + v if at in field_of else v

    for at, v in own.items():
        put(at, v)
    late = []
    for y in range(2):
        late += [("a", 0, (2, y), hx[(1, y)]), ("a", 1, (-1, y), hx[(-1, y)])]
        late += [("b", 0, (y, 2), hy[(1, y)]), ("b", 1, (y, -1), hy[(-1, y)])]
    for n, (dx, dy) in enumerate(DIRS):
        x, y = edge(dx), edge(dy)
        there = sender_is_there(dx, dy)
        side_a, side_b = (0 if dx == 1 else 1), (0 if dy == 1 else 1)
        if dy == 0:
            for t in range(2):
                put((x - 2 * dx, t), r2[n, 32 * t : 32 * t + 32, :])
                late.append(("a", side_a, (x - dx, t), r2[n, 64 + 16 * t : 80 + 16 * t, :] * there))
            late.append(("b", 0, (x - 2 * dx, 2), r2[n, 96:112, :] * there))
            late.append(("b", 1, (x - 2 * dx, -1), r2[n, 112:128, :] * there))
        elif dx == 0:
            for t in range(2):
                put((t, y - 2 * dy), r2[n, 32 * t : 32 * t + 32, :])
                late.append(("b", side_b, (t, y - dy), r2[n, 64 + 16 * t : 80 + 16 * t, :] * there))
            late.append(("a", 0, (2, y - 2 * dy), r2[n, 96:112, :] * there))
            late.append(("a", 1, (-1, y - 2 * dy), r2[n, 112:128, :] * there))
        else:
            put((x - 2 * dx, y - 2 * dy), r2[n, 0:32, :])
            late.append(("a", side_a, (x - dx, y - 2 * dy), r2[n, 32:48, :] * there))
            late.append(("b", side_b, (x - 2 * dx, y - dy), r2[n, 48:64, :] * there))
    for kind, side, at, v in late:
        field_of[at] = add_a(field_of[at], side, v) if kind == "a" else add_b(field_of[at], side, v)

    for (x, y), v in field_of.items():
        moved = pltpu.roll(v, 127, 1)
        for z, value in enumerate((v, moved)):
            pieces = split(value)
            for sx_, sy_ in ((0, 0), (0, 1), (1, 0), (1, 1)):
                vx, vy = x + 1 - sx_, y + 1 - sy_
                if 0 <= vx <= 2 and 0 <= vy <= 2:
                    p = sx_ * 4 + sy_ * 2 + z
                    for t in range(2):
                        cp[pl.ds(256 * t + 32 * p, 32), pl.ds(128 * (3 * vx + vy), 128)] = pieces[t]
    gath[...] = dot(cp[pl.ds(0, 256), :], oh[...]) + dot(cp[pl.ds(256, 256), :], oh[...])
    for s in range(8):
        slot = jnp.broadcast_to(place[s : s + 1, :], (32, LANES))
        value = jnp.zeros((32, LANES), F32)
        for p in range(8):
            value = jnp.where(slot == p, gath[pl.ds(32 * p, 32), :], value)
        rows = pl.ds(32 * s, 32)
        wh[rows, :], wl[rows, :] = split(value)
    ans[...] = dot(mi_h[...], wh[...]) + dot(mi_h[...], wl[...]) + dot(mi_l[...], wh[...])
    for p in range(8):
        value = jnp.zeros((32, LANES), F32)
        for s in range(8):
            slot = jnp.broadcast_to(place[s : s + 1, :], (32, LANES))
            value = jnp.where(slot == p, ans[pl.ds(32 * s, 32), :], value)
        ap[pl.ds(32 * p, 32), :], ap[pl.ds(256 + 32 * p, 32), :] = split(value)
    vv[...] = dot_nt(ap[pl.ds(0, 256), :], oh[...]) + dot_nt(ap[pl.ds(256, 256), :], oh[...])
    spread = {}
    for x in range(-1, 3):
        for y in range(-1, 3):
            sums = [None, None]
            for sx_, sy_ in ((0, 0), (0, 1), (1, 0), (1, 1)):
                vx, vy = x + 1 - sx_, y + 1 - sy_
                if 0 <= vx <= 2 and 0 <= vy <= 2:
                    for z in range(2):
                        p = sx_ * 4 + sy_ * 2 + z
                        v = vv[pl.ds(32 * p, 32), pl.ds(128 * (3 * vx + vy), 128)]
                        sums[z] = v if sums[z] is None else sums[z] + v
            spread[(x, y)] = sums[0] + pltpu.roll(sums[1], 1, 1)

    def correction_blocks(dx, dy):
        x, y = edge(dx), edge(dy)
        if dy == 0:
            return [
                spread[(x + dx, 0)], spread[(x + dx, 1)], a_half(spread[(x, 0)], x), a_half(spread[(x, 1)], x),
                b_half(spread[(x + dx, 2)], 0), b_half(spread[(x + dx, -1)], 1),
            ]
        if dx == 0:
            return [
                spread[(0, y + dy)], spread[(1, y + dy)], b_half(spread[(0, y)], y), b_half(spread[(1, y)], y),
                a_half(spread[(2, y + dy)], 0), a_half(spread[(-1, y + dy)], 1),
            ]
        return [spread[(x + dx, y + dy)], a_half(spread[(x, y + dy)], x), b_half(spread[(x + dx, y)], y)]

    third = exchange(correction_blocks, s3, r3, ssem3, rsem3)

    for copy in whole:
        copy.wait_recv()
    for f in range(4):
        x_up = jnp.concatenate([fz[f, 32:64, 256:512], rx[1, f]], axis=1) * upper_x
        x_down = jnp.concatenate([rx[0, f], fz[f, 0:32, 0:256]], axis=1) * lower_x
        y_up, y_down = [], []
        for x in range(2):
            y_up += [fz[f, 104:144, 256 * x + 128 : 256 * x + 256], ry[1, f, :, 128 * x : 128 * x + 128]]
            y_down += [ry[0, f, :, 128 * x : 128 * x + 128], fz[f, 64:104, 256 * x : 256 * x + 128]]
        parts = [
            x_up, x_down,
            jnp.concatenate(y_up, axis=1) * upper_y,
            jnp.concatenate(y_down, axis=1) * lower_y,
            by_column(from_next, fz[f, 176:208, :]),
            by_column(from_previous, fz[f, 144:176, :]),
            jnp.zeros((48, LANES), F32),
        ]
        around = mm3(bte_h[...], bte_l[...], jnp.concatenate(parts, axis=0))
        xhat[f] = 0.2 * xhat[f] + 0.8 * (dinv[...] * (bhat[f] + 0.5 * around))

    for copy in third:
        copy.wait_recv()
    fixed = {at: spread[at] for at in own}
    near_x = {(2, y): a_half(spread[(2, y)], 0) for y in range(2)} | {
        (-1, y): a_half(spread[(-1, y)], 1) for y in range(2)
    }
    near_y = {(x, 2): b_half(spread[(x, 2)], 0) for x in range(2)} | {
        (x, -1): b_half(spread[(x, -1)], 1) for x in range(2)
    }
    for n, (dx, dy) in enumerate(DIRS):
        x, y = edge(dx), edge(dy)
        if dy == 0:
            for t in range(2):
                fixed[(x - dx, t)] += r3[n, 32 * t : 32 * t + 32, :]
                near_x[(x - 2 * dx, t)] += r3[n, 64 + 16 * t : 80 + 16 * t, :]
            near_y[(x - dx, 2)] += r3[n, 96:112, :]
            near_y[(x - dx, -1)] += r3[n, 112:128, :]
        elif dx == 0:
            for t in range(2):
                fixed[(t, y - dy)] += r3[n, 32 * t : 32 * t + 32, :]
                near_y[(t, y - 2 * dy)] += r3[n, 64 + 16 * t : 80 + 16 * t, :]
            near_x[(2, y - dy)] += r3[n, 96:112, :]
            near_x[(-1, y - dy)] += r3[n, 112:128, :]
        else:
            fixed[(x - dx, y - dy)] += r3[n, 0:32, :]
            near_x[(x - 2 * dx, y - dy)] += r3[n, 32:48, :]
            near_y[(x - dx, y - 2 * dy)] += r3[n, 48:64, :]

    columns, rims = [], []
    for x in range(2):
        for y in range(2):
            v = fixed[(x, y)]
            columns.append(v)
            rims.append(
                jnp.concatenate(
                    [
                        a_half(fixed[(1, y)], 0) if x == 0 else near_x[(2, y)] * has[(1, 0)],
                        a_half(fixed[(0, y)], 1) if x == 1 else near_x[(-1, y)] * has[(-1, 0)],
                        b_half(fixed[(x, 1)], 0) if y == 0 else near_y[(x, 2)] * has[(0, 1)],
                        b_half(fixed[(x, 0)], 1) if y == 1 else near_y[(x, -1)] * has[(0, -1)],
                        jnp.where(up_row, from_previous(v), from_next(v)),
                        jnp.zeros((32, 128), F32),
                    ],
                    axis=0,
                )
            )
    ch, cl = split(jnp.concatenate(columns, axis=1))
    stacked = jnp.concatenate([ch, cl, ch, jnp.zeros((32, LANES), BF16)], axis=0)
    rh, rl = split(jnp.concatenate(rims, axis=1))
    for f in range(4):
        rows = pl.ds(128 * f, 128)
        direct = dot(tc[rows, :], stacked)
        coupled = dot(tf_h[rows, :], rh) + dot(tf_h[rows, :], rl) + dot(tf_l[rows, :], rh)
        final = xhat[f] + 0.2 * direct + 0.4 * (dinv[...] * coupled)
        outv[f] = mm3(bb_h[...], bb_l[...], final)[0:125]
    done = pltpu.make_async_copy(outv, out_h.at[:, :, 0, :], lsem.at[len(local)])
    done.start()
    for copy in sent:
        copy.wait_send()
    done.wait()


def solution(mesh):
    nx, ny = mesh.shape["px"], mesh.shape["py"]
    table = column_table()

    def per_device(
        right_side, first_guess, coefficient, modal_basis, modal_values, patch_inverse, patch_elements, patch_mask
    ):
        any_ = pl.BlockSpec(memory_space=pl.ANY)
        smem = pl.BlockSpec(memory_space=pltpu.SMEM)

        def body(*refs):
            kernel(nx, ny, *refs)

        def f32(*shape):
            return pltpu.VMEM(shape, F32)

        def b16(*shape):
            return pltpu.VMEM(shape, BF16)

        dma = pltpu.SemaphoreType.DMA
        out = pl.pallas_call(
            body,
            out_shape=jax.ShapeDtypeStruct((4, 125, 1, 512), F32),
            in_specs=[any_] * 6 + [smem] * 2 + [any_] * 4,
            out_specs=any_,
            scratch_shapes=[
                f32(4, 125, 512), f32(4, 125, 512), f32(2, 4, 25, 512), f32(2, 4, 5, 5, 512), f32(2, 4, 25, 512),
                f32(4, 128), f32(256, 256), pltpu.VMEM((8, 512), jnp.int32), pltpu.VMEM((8, 512), jnp.int32),
                pltpu.VMEM((8, 640), jnp.int32),
                b16(128, 128), b16(128, 128), b16(128, 256), b16(128, 256), b16(128, 128), b16(128, 128),
                b16(256, 128), b16(256, 128),
                b16(32, 512), b16(32, 512), b16(96, 512), b16(96, 512),
                b16(512, 128), b16(512, 128), b16(512, 128), b16(256, 256), b16(256, 256),
                f32(4, 128, 512), f32(4, 128, 512), f32(128, 512), b16(1152, 512),
                b16(512, 512), b16(512, 512), b16(512, 512), b16(512, 512),
                b16(512, 1152), f32(256, 512), b16(256, 512), b16(256, 512), f32(256, 512), b16(512, 512),
                f32(256, 1152),
                f32(2, 4, 32, 256), f32(2, 4, 40, 256), f32(2, 4, 32, 256), f32(2, 4, 40, 256), f32(4, 256, 512),
                f32(8, 128, 128), f32(8, 128, 128), f32(8, 128, 128), f32(8, 128, 128), f32(4, 125, 512),
                dma((16,)), dma((6,)), dma((6,)), dma((4,)), dma((4,)), dma((8,)), dma((8,)), dma((8,)), dma((8,)),
            ],
            compiler_params=pltpu.CompilerParams(
                collective_id=0, has_side_effects=True, vmem_limit_bytes=48 * 1024 * 1024
            ),
        )(
            first_guess.reshape(4, 125, 1, 512),
            first_guess.reshape(4, 5, 25, 2, 1, 256),
            first_guess.reshape(4, 5, 5, 5, 2, 2, 1, 128),
            first_guess.reshape(4, 25, 5, 1, 512),
            right_side.reshape(4, 125, 1, 512),
            coefficient.reshape(4, 128),
            modal_basis,
            modal_values,
            patch_inverse,
            patch_elements.T,
            patch_mask.T,
            jnp.asarray(table),
        )
        return out.reshape(4, 5, 5, 5, 2, 2, 128)

    grid = P(None, None, None, None, "px", "py", None)
    rows = P(("px", "py"), None)
    return jax.shard_map(
        per_device,
        mesh=mesh,
        in_specs=(grid, grid, P("px", "py", None), P(), P(), P(), rows, rows),
        out_specs=grid,
        check_vma=False,
    )
```

```python
import math

import jax
import jax.numpy as jnp
import numpy as np
from jax import lax
from jax.experimental import pallas as pl
from jax.experimental.pallas import tpu as pltpu
from jax.sharding import PartitionSpec as P

MESH = pl.DeviceIdType.MESH
F32 = jnp.float32
BF16 = jnp.bfloat16
DIRS = ((1, 0), (-1, 0), (0, 1), (0, -1), (1, 1), (1, -1), (-1, 1), (-1, -1))
LANES = 512


def linear_values():
    root = np.float32(math.sqrt(3.0 / 7.0))
    points = np.array([-1.0, -root, 0.0, root, 1.0], np.float32)
    half = np.float32(0.5)
    return (1 - points) * half, (1 + points) * half


def column_table():
    table = np.full((8, 640), 7, np.int32)
    table[3] = 9

    def put(column, i, j, k, f=9):
        table[0:4, column] = (i, j, k, f)

    for n in range(125):
        put(n, n // 25, n // 5 % 5, n % 5)
    for g in range(25):
        u, v = g // 5, g % 5
        put(128 + g, 4, u, v)
        put(160 + g, 0, u, v)
        put(192 + u * 8 + v, u, 4, v)
        put(232 + u * 8 + v, u, 0, v)
        put(272 + g, u, v, 4)
        put(304 + g, u, v, 0)
    for r in range(32):
        a, b, f, c = r // 16, r // 8 % 2, r // 2 % 4, r % 2
        for copy in range(3):
            put(384 + 32 * copy + r, 5 + a, 5 + b, 5 + c, f)
        put(512 + 64 + r, 5 + a, 5 + b, 4 if c == 0 else 0, f)
    for r in range(16):
        h, f, c = r // 8, r // 2 % 4, r % 2
        put(512 + r, 4, 5 + h, 5 + c, f)
        put(528 + r, 0, 5 + h, 5 + c, f)
        put(544 + r, 5 + h, 4, 5 + c, f)
        put(560 + r, 5 + h, 0, 5 + c, f)
    return table


def split(value):
    high = value.astype(BF16)
    return high, (value - high.astype(F32)).astype(BF16)


def dot(a, b):
    return lax.dot_general(a, b, (((1,), (0,)), ((), ())), preferred_element_type=F32)


def dot_nt(a, b):
    return lax.dot_general(a, b, (((1,), (1,)), ((), ())), preferred_element_type=F32)


def mm3(ah, al, x):
    xh, xl = split(x)
    return dot(ah, xh) + dot(ah, xl) + dot(al, xh)


def iota(shape, dim):
    return lax.broadcasted_iota(jnp.int32, shape, dim)


def a_half(v, a):
    return v[16 * a : 16 * a + 16]


def b_half(v, b):
    return jnp.concatenate([v[8 * b : 8 * b + 8], v[16 + 8 * b : 24 + 8 * b]], axis=0)


def add_a(v, a, h):
    parts = [v[0:16], v[16:32]]
    parts[a] = parts[a] + h
    return jnp.concatenate(parts, axis=0)


def add_b(v, b, h):
    parts = [v[0:8], v[8:16], v[16:24], v[24:32]]
    parts[b] = parts[b] + h[0:8]
    parts[2 + b] = parts[2 + b] + h[8:16]
    return jnp.concatenate(parts, axis=0)


def rows_to(v, rows):
    return jnp.concatenate([v, jnp.zeros((rows - v.shape[0], v.shape[1]), v.dtype)], axis=0)


def from_next(v):
    lane = iota(v.shape, 1)
    return jnp.where(lane == 127, 0.0, pltpu.roll(v, 127, 1))


def from_previous(v):
    lane = iota(v.shape, 1)
    return jnp.where(lane == 0, 0.0, pltpu.roll(v, 1, 1))


def by_column(fn, v):
    return jnp.concatenate([fn(v[:, 128 * c : 128 * c + 128]) for c in range(4)], axis=1)


def kernel(
    nx, ny,
    xa, xx, xy, xz, ba, coef_h, ub_h, mv_h, pinv_h, pe_h, pm_h, tab_h,
    outv,
    ub, mv, xin, bin_, nfx, nfy, nfz, coef, pinv, pe, pm, tab,
    bt_h, bt_l, bte_h, bte_l, bb_h, bb_l, fb_h, fb_l,
    qc_h, qc_l, qf_h, qf_l, tc, tf_h, tf_l, mi_h, mi_l,
    xhat, bhat, dinv, oh, xs_h, xs_l, ts_h, ts_l,
    cp, gath, wh, wl, ans, ap, vv,
    sx, sy, rx, ry, fz, s2, r2, s3, r3,
    lsem, ssem1, rsem1, ssemf, rsemf, ssem2, rsem2, ssem3, rsem3,
):
    px, py = lax.axis_index("px"), lax.axis_index("py")

    def peer(dx, dy):
        return (lax.rem(px + dx + nx, nx), lax.rem(py + dy + ny, ny))

    local = []

    def load(src, dst):
        copy = pltpu.make_async_copy(src, dst, lsem.at[len(local)])
        copy.start()
        local.append(copy)

    load(tab_h, tab)
    load(coef_h, coef)
    load(ub_h, ub)
    load(mv_h, mv)
    load(xa.at[:, :, 0, :], xin)
    load(ba.at[:, :, 0, :], bin_)
    load(pe_h, pe)
    load(pm_h, pm)
    load(pinv_h, pinv)
    load(xx.at[:, 0, :, 1, 0, :], nfx.at[0, :, :, pl.ds(0, 256)])
    load(xx.at[:, 4, :, 0, 0, :], nfx.at[1, :, :, pl.ds(256, 256)])
    for x in range(2):
        load(xy.at[:, :, 0, :, x, 1, 0, :], nfy.at[0, :, :, :, pl.ds(256 * x, 128)])
        load(xy.at[:, :, 4, :, x, 0, 0, :], nfy.at[1, :, :, :, pl.ds(256 * x + 128, 128)])
    load(xz.at[:, :, 0, 0, :], nfz.at[0])
    load(xz.at[:, :, 4, 0, :], nfz.at[1])

    barrier = pltpu.get_barrier_semaphore()
    for dx, dy in DIRS:
        pl.semaphore_signal(barrier, inc=1, device_id=peer(dx, dy), device_id_type=MESH)
    pl.semaphore_wait(barrier, 8)

    sent = []

    def send(src, dst, ssem, rsem, to):
        copy = pltpu.make_async_remote_copy(
            src_ref=src, dst_ref=dst, send_sem=ssem, recv_sem=rsem, device_id=to, device_id_type=MESH
        )
        copy.start()
        sent.append(copy)
        return copy

    first = [
        send(xx.at[:, 4, :, 1, 0, :], nfx.at[1, :, :, pl.ds(0, 256)], ssem1.at[0], rsem1.at[0], peer(1, 0)),
        send(xx.at[:, 0, :, 0, 0, :], nfx.at[0, :, :, pl.ds(256, 256)], ssem1.at[1], rsem1.at[1], peer(-1, 0)),
    ]
    for x in range(2):
        first.append(
            send(xy.at[:, :, 4, :, x, 1, 0, :], nfy.at[1, :, :, :, pl.ds(256 * x, 128)],
                 ssem1.at[2 + 2 * x], rsem1.at[2 + 2 * x], peer(0, 1))
        )
        first.append(
            send(xy.at[:, :, 0, :, x, 0, 0, :], nfy.at[0, :, :, :, pl.ds(256 * x + 128, 128)],
                 ssem1.at[3 + 2 * x], rsem1.at[3 + 2 * x], peer(0, -1))
        )

    for copy in local[0:4]:
        copy.wait()
    basis = [[ub[p, q] for q in range(5)] for p in range(5)]
    for weights in linear_values():
        basis.append([sum(float(weights[i]) * basis[i][q] for i in range(5)) for q in range(5)])
    spectrum = [mv[q] for q in range(5)]

    def mode_index(shape):
        row = iota(shape, 0)
        i = (row * 41) >> 10
        rest = row - 25 * i
        j = (rest * 13) >> 6
        return i, j, rest - 5 * j

    def block(start):
        modes = mode_index((128, 128))
        result = None
        for d in range(3):
            index = tab[d : d + 1, start : start + 128]
            hits = [index == p for p in range(7)]
            grown = jnp.zeros((128, 128), F32)
            for q in range(5):
                line = jnp.zeros((1, 128), F32)
                for p in range(7):
                    line = jnp.where(hits[p], basis[p][q], line)
                grown = jnp.where(modes[d] == q, line, grown)
            result = grown if result is None else result * grown
        return result

    nodes = block(0)
    bt_h[...], bt_l[...] = split(nodes)
    bb_h[...], bb_l[...] = split(nodes.T)
    for part in range(2):
        faces = block(128 + 128 * part)
        span = pl.ds(128 * part, 128)
        bte_h[:, span], bte_l[:, span] = split(faces)
        fb_h[span, :], fb_l[span, :] = split(faces.T)
    field = tab[3:4, 384:512]
    coarse_block = block(384)
    copy_of = iota((128, 128), 1)
    for f in range(4):
        part = jnp.where(field == f, coarse_block, 0.0)
        high, low = split(part)
        tc[pl.ds(128 * f, 128), :] = jnp.where(copy_of < 64, high.astype(F32), low.astype(F32)).astype(BF16)
        turned = part.T
        qc_h[:, pl.ds(128 * f, 128)], qc_l[:, pl.ds(128 * f, 128)] = split(turned[0:32])
    field = tab[3:4, 512:640]
    face_block = block(512)
    for f in range(4):
        part = jnp.where(field == f, face_block, 0.0)
        tf_h[pl.ds(128 * f, 128), :], tf_l[pl.ds(128 * f, 128), :] = split(part)
        turned = part.T
        qf_h[:, pl.ds(128 * f, 128)], qf_l[:, pl.ds(128 * f, 128)] = split(turned[0:96])

    modes = mode_index((128, 128))
    total = jnp.zeros((128, 128), F32)
    for d in range(3):
        for q in range(5):
            total = jnp.where(modes[d] == q, total + spectrum[q], total)

    def diagonal(c):
        return total * coef[c : c + 1, :] + 1.0

    for c in range(4):
        dinv[:, pl.ds(128 * c, 128)] = 1.0 / diagonal(c)

    local[4].wait()
    local[5].wait()
    for f in range(4):
        xhat[f] = mm3(bt_h[...], bt_l[...], rows_to(xin[f], 128))
        bhat[f] = mm3(bt_h[...], bt_l[...], rows_to(bin_[f], 128))

    local[6].wait()
    local[7].wait()
    elements = pe[...]
    alive = pm[...] != 0
    at_x = (elements >> 11) - 2 * px + 1
    at_y = ((elements >> 7) & 15) - 2 * py + 1
    at_z = elements & 127

    def least(v, most):
        return jnp.minimum(jnp.min(jnp.where(alive, v, most), axis=0, keepdims=True), most)

    low_x, low_y, low_z = least(at_x, 2), least(at_y, 2), least(at_z, 126)
    key = (low_x * 3 + low_y) * 128 + low_z
    place = (at_x - low_x) * 4 + (at_y - low_y) * 2 + (at_z - low_z)
    place = jnp.where(alive, place, 99)
    vertex = iota((128, LANES), 0)
    for v in range(9):
        oh[pl.ds(128 * v, 128), :] = jnp.where(vertex + 128 * v == key, 1.0, 0.0).astype(BF16)

    local[8].wait()
    r = iota((256, 256), 0)
    source = (((r >> 1) & 3) * 8 + ((r >> 4) & 1) * 4 + ((r >> 3) & 1) * 2 + (r & 1)) * 8 + (r >> 5)
    order = jnp.where(iota((256, 256), 1) == source, 1.0, 0.0).astype(BF16)
    for piece, target in zip(split(pinv[...]), (mi_h, mi_l)):
        target[...] = dot_nt(dot(order, piece).astype(BF16), order).astype(BF16)

    has = {
        (1, 0): jnp.where(px < nx - 1, 1.0, 0.0),
        (-1, 0): jnp.where(px > 0, 1.0, 0.0),
        (0, 1): jnp.where(py < ny - 1, 1.0, 0.0),
        (0, -1): jnp.where(py > 0, 1.0, 0.0),
    }
    lane = iota((1, LANES), 1)
    upper_x = jnp.where(lane >= 256, has[(1, 0)], 1.0)
    lower_x = jnp.where(lane < 256, has[(-1, 0)], 1.0)
    upper_y = jnp.where(((lane >> 7) & 1) == 1, has[(0, 1)], 1.0)
    lower_y = jnp.where(((lane >> 7) & 1) == 0, has[(0, -1)], 1.0)

    for copy in local[9:]:
        copy.wait()
    for copy in first:
        copy.wait_recv()

    for f in range(4):
        parts = [
            rows_to(nfx[0, f], 32) * upper_x,
            rows_to(nfx[1, f], 32) * lower_x,
        ]
        parts += [rows_to(nfy[0, f, i], 8) * upper_y for i in range(5)]
        parts += [rows_to(nfy[1, f, i], 8) * lower_y for i in range(5)]
        parts.append(by_column(from_next, rows_to(nfz[0, f], 32)))
        parts.append(by_column(from_previous, rows_to(nfz[1, f], 32)))
        parts.append(jnp.zeros((48, LANES), F32))
        around = mm3(bte_h[...], bte_l[...], jnp.concatenate(parts, axis=0))
        loaded = bhat[f] + 0.5 * around
        x0 = xhat[f]
        x1 = 0.2 * x0 + 0.8 * (dinv[...] * loaded)
        diag = jnp.concatenate([diagonal(c) for c in range(4)], axis=1)
        rest = bhat[f] - 0.2 * (diag * x0) - 0.8 * loaded
        xhat[f] = x1
        rows = pl.ds(128 * f, 128)
        xs_h[rows, :], xs_l[rows, :] = split(x1)
        ts_h[rows, :], ts_l[rows, :] = split(rest)

    inner = dot(qc_h[...], ts_h[...]) + dot(qc_h[...], ts_l[...]) + dot(qc_l[...], ts_h[...])
    rim = 0.5 * (dot(qf_h[...], xs_h[...]) + dot(qf_h[...], xs_l[...]) + dot(qf_l[...], xs_h[...]))
    up_row = ((iota((32, 128), 0) & 1) == 1)

    def rim_of(start, size, c):
        return rim[start : start + size, 128 * c : 128 * c + 128]

    own = {}
    for x in range(2):
        for y in range(2):
            c = 2 * x + y
            v = inner[:, 128 * c : 128 * c + 128]
            faces = rim_of(64, 32, c)
            v = v + jnp.where(up_row, from_next(faces), from_previous(faces))
            v = add_a(v, 0, rim_of(0, 16, y)) if x == 1 else add_a(v, 1, rim_of(16, 16, 2 + y))
            v = add_b(v, 0, rim_of(32, 16, 2 * x)) if y == 1 else add_b(v, 1, rim_of(48, 16, 2 * x + 1))
            own[(x, y)] = v
    hx = {(1, y): rim_of(0, 16, 2 + y) for y in range(2)} | {(-1, y): rim_of(16, 16, y) for y in range(2)}
    hy = {(1, x): rim_of(32, 16, 2 * x + 1) for x in range(2)} | {(-1, x): rim_of(48, 16, 2 * x) for x in range(2)}

    def edge(d):
        return 1 if d == 1 else 0

    def exchange(blocks, sbuf, rbuf, ssem, rsem):
        copies = []
        for n, (dx, dy) in enumerate(DIRS):
            at = 0
            for v in blocks(dx, dy):
                sbuf[n, pl.ds(at, v.shape[0]), :] = v
                at += v.shape[0]
            copies.append(
                send(sbuf.at[n, pl.ds(0, at)], rbuf.at[n, pl.ds(0, at)], ssem.at[n], rsem.at[n], peer(dx, dy))
            )
        return copies

    def residual_blocks(dx, dy):
        x, y = edge(dx), edge(dy)
        if dy == 0:
            return [own[(x, 0)], own[(x, 1)], hx[(dx, 0)], hx[(dx, 1)], hy[(1, x)], hy[(-1, x)]]
        if dx == 0:
            return [own[(0, y)], own[(1, y)], hy[(dy, 0)], hy[(dy, 1)], hx[(1, y)], hx[(-1, y)]]
        return [own[(x, y)], hx[(dx, y)], hy[(dy, x)]]

    second = exchange(residual_blocks, s2, r2, ssem2, rsem2)

    for f in range(4):
        rows = pl.ds(128 * f, 128)
        for part in range(2):
            span = pl.ds(128 * part, 128)
            faces = (
                dot(fb_h[span, :], xs_h[rows, :])
                + dot(fb_h[span, :], xs_l[rows, :])
                + dot(fb_l[span, :], xs_h[rows, :])
            )
            fz[f, span, :] = faces
        sx[0, f] = fz[f, 0:32, 256:512]
        sx[1, f] = fz[f, 32:64, 0:256]
        for x in range(2):
            sy[0, f, :, pl.ds(128 * x, 128)] = fz[f, 64:104, 256 * x + 128 : 256 * x + 256]
            sy[1, f, :, pl.ds(128 * x, 128)] = fz[f, 104:144, 256 * x : 256 * x + 128]
    whole = [
        send(sx.at[0], rx.at[0], ssemf.at[0], rsemf.at[0], peer(1, 0)),
        send(sx.at[1], rx.at[1], ssemf.at[1], rsemf.at[1], peer(-1, 0)),
        send(sy.at[0], ry.at[0], ssemf.at[2], rsemf.at[2], peer(0, 1)),
        send(sy.at[1], ry.at[1], ssemf.at[3], rsemf.at[3], peer(0, -1)),
    ]

    def sender_is_there(dx, dy):
        there = 1.0
        if dx:
            there = there * has[(-dx, 0)]
        if dy:
            there = there * has[(0, -dy)]
        return there

    for copy in second:
        copy.wait_recv()
    field_of = {}

    def put(at, v):
        field_of[at] = field_of[at] + v if at in field_of else v

    for at, v in own.items():
        put(at, v)
    late = []
    for y in range(2):
        late += [("a", 0, (2, y), hx[(1, y)]), ("a", 1, (-1, y), hx[(-1, y)])]
        late += [("b", 0, (y, 2), hy[(1, y)]), ("b", 1, (y, -1), hy[(-1, y)])]
    for n, (dx, dy) in enumerate(DIRS):
        x, y = edge(dx), edge(dy)
        there = sender_is_there(dx, dy)
        side_a, side_b = (0 if dx == 1 else 1), (0 if dy == 1 else 1)
        if dy == 0:
            for t in range(2):
                put((x - 2 * dx, t), r2[n, 32 * t : 32 * t + 32, :])
                late.append(("a", side_a, (x - dx, t), r2[n, 64 + 16 * t : 80 + 16 * t, :] * there))
            late.append(("b", 0, (x - 2 * dx, 2), r2[n, 96:112, :] * there))
            late.append(("b", 1, (x - 2 * dx, -1), r2[n, 112:128, :] * there))
        elif dx == 0:
            for t in range(2):
                put((t, y - 2 * dy), r2[n, 32 * t : 32 * t + 32, :])
                late.append(("b", side_b, (t, y - dy), r2[n, 64 + 16 * t : 80 + 16 * t, :] * there))
            late.append(("a", 0, (2, y - 2 * dy), r2[n, 96:112, :] * there))
            late.append(("a", 1, (-1, y - 2 * dy), r2[n, 112:128, :] * there))
        else:
            put((x - 2 * dx, y - 2 * dy), r2[n, 0:32, :])
            late.append(("a", side_a, (x - dx, y - 2 * dy), r2[n, 32:48, :] * there))
            late.append(("b", side_b, (x - 2 * dx, y - dy), r2[n, 48:64, :] * there))
    for kind, side, at, v in late:
        field_of[at] = add_a(field_of[at], side, v) if kind == "a" else add_b(field_of[at], side, v)

    for (x, y), v in field_of.items():
        moved = pltpu.roll(v, 127, 1)
        for z, value in enumerate((v, moved)):
            pieces = split(value)
            for sx_, sy_ in ((0, 0), (0, 1), (1, 0), (1, 1)):
                vx, vy = x + 1 - sx_, y + 1 - sy_
                if 0 <= vx <= 2 and 0 <= vy <= 2:
                    p = sx_ * 4 + sy_ * 2 + z
                    for t in range(2):
                        cp[pl.ds(256 * t + 32 * p, 32), pl.ds(128 * (3 * vx + vy), 128)] = pieces[t]
    gath[...] = dot(cp[pl.ds(0, 256), :], oh[...]) + dot(cp[pl.ds(256, 256), :], oh[...])
    for s in range(8):
        slot = jnp.broadcast_to(place[s : s + 1, :], (32, LANES))
        value = jnp.zeros((32, LANES), F32)
        for p in range(8):
            value = jnp.where(slot == p, gath[pl.ds(32 * p, 32), :], value)
        rows = pl.ds(32 * s, 32)
        wh[rows, :], wl[rows, :] = split(value)
    ans[...] = dot(mi_h[...], wh[...]) + dot(mi_h[...], wl[...]) + dot(mi_l[...], wh[...])
    for p in range(8):
        value = jnp.zeros((32, LANES), F32)
        for s in range(8):
            slot = jnp.broadcast_to(place[s : s + 1, :], (32, LANES))
            value = jnp.where(slot == p, ans[pl.ds(32 * s, 32), :], value)
        ap[pl.ds(32 * p, 32), :], ap[pl.ds(256 + 32 * p, 32), :] = split(value)
    vv[...] = dot_nt(ap[pl.ds(0, 256), :], oh[...]) + dot_nt(ap[pl.ds(256, 256), :], oh[...])
    spread = {}
    for x in range(-1, 3):
        for y in range(-1, 3):
            sums = [None, None]
            for sx_, sy_ in ((0, 0), (0, 1), (1, 0), (1, 1)):
                vx, vy = x + 1 - sx_, y + 1 - sy_
                if 0 <= vx <= 2 and 0 <= vy <= 2:
                    for z in range(2):
                        p = sx_ * 4 + sy_ * 2 + z
                        v = vv[pl.ds(32 * p, 32), pl.ds(128 * (3 * vx + vy), 128)]
                        sums[z] = v if sums[z] is None else sums[z] + v
            spread[(x, y)] = sums[0] + pltpu.roll(sums[1], 1, 1)

    def correction_blocks(dx, dy):
        x, y = edge(dx), edge(dy)
        if dy == 0:
            return [
                spread[(x + dx, 0)], spread[(x + dx, 1)], a_half(spread[(x, 0)], x), a_half(spread[(x, 1)], x),
                b_half(spread[(x + dx, 2)], 0), b_half(spread[(x + dx, -1)], 1),
            ]
        if dx == 0:
            return [
                spread[(0, y + dy)], spread[(1, y + dy)], b_half(spread[(0, y)], y), b_half(spread[(1, y)], y),
                a_half(spread[(2, y + dy)], 0), a_half(spread[(-1, y + dy)], 1),
            ]
        return [spread[(x + dx, y + dy)], a_half(spread[(x, y + dy)], x), b_half(spread[(x + dx, y)], y)]

    third = exchange(correction_blocks, s3, r3, ssem3, rsem3)

    for copy in whole:
        copy.wait_recv()
    for f in range(4):
        x_up = jnp.concatenate([fz[f, 32:64, 256:512], rx[1, f]], axis=1) * upper_x
        x_down = jnp.concatenate([rx[0, f], fz[f, 0:32, 0:256]], axis=1) * lower_x
        y_up, y_down = [], []
        for x in range(2):
            y_up += [fz[f, 104:144, 256 * x + 128 : 256 * x + 256], ry[1, f, :, 128 * x : 128 * x + 128]]
            y_down += [ry[0, f, :, 128 * x : 128 * x + 128], fz[f, 64:104, 256 * x : 256 * x + 128]]
        parts = [
            x_up, x_down,
            jnp.concatenate(y_up, axis=1) * upper_y,
            jnp.concatenate(y_down, axis=1) * lower_y,
            by_column(from_next, fz[f, 176:208, :]),
            by_column(from_previous, fz[f, 144:176, :]),
            jnp.zeros((48, LANES), F32),
        ]
        around = mm3(bte_h[...], bte_l[...], jnp.concatenate(parts, axis=0))
        xhat[f] = 0.2 * xhat[f] + 0.8 * (dinv[...] * (bhat[f] + 0.5 * around))

    for copy in third:
        copy.wait_recv()
    fixed = {at: spread[at] for at in own}
    near_x = {(2, y): a_half(spread[(2, y)], 0) for y in range(2)} | {
        (-1, y): a_half(spread[(-1, y)], 1) for y in range(2)
    }
    near_y = {(x, 2): b_half(spread[(x, 2)], 0) for x in range(2)} | {
        (x, -1): b_half(spread[(x, -1)], 1) for x in range(2)
    }
    for n, (dx, dy) in enumerate(DIRS):
        x, y = edge(dx), edge(dy)
        if dy == 0:
            for t in range(2):
                fixed[(x - dx, t)] += r3[n, 32 * t : 32 * t + 32, :]
                near_x[(x - 2 * dx, t)] += r3[n, 64 + 16 * t : 80 + 16 * t, :]
            near_y[(x - dx, 2)] += r3[n, 96:112, :]
            near_y[(x - dx, -1)] += r3[n, 112:128, :]
        elif dx == 0:
            for t in range(2):
                fixed[(t, y - dy)] += r3[n, 32 * t : 32 * t + 32, :]
                near_y[(t, y - 2 * dy)] += r3[n, 64 + 16 * t : 80 + 16 * t, :]
            near_x[(2, y - dy)] += r3[n, 96:112, :]
            near_x[(-1, y - dy)] += r3[n, 112:128, :]
        else:
            fixed[(x - dx, y - dy)] += r3[n, 0:32, :]
            near_x[(x - 2 * dx, y - dy)] += r3[n, 32:48, :]
            near_y[(x - dx, y - 2 * dy)] += r3[n, 48:64, :]

    columns, rims = [], []
    for x in range(2):
        for y in range(2):
            v = fixed[(x, y)]
            columns.append(v)
            rims.append(
                jnp.concatenate(
                    [
                        a_half(fixed[(1, y)], 0) if x == 0 else near_x[(2, y)] * has[(1, 0)],
                        a_half(fixed[(0, y)], 1) if x == 1 else near_x[(-1, y)] * has[(-1, 0)],
                        b_half(fixed[(x, 1)], 0) if y == 0 else near_y[(x, 2)] * has[(0, 1)],
                        b_half(fixed[(x, 0)], 1) if y == 1 else near_y[(x, -1)] * has[(0, -1)],
                        jnp.where(up_row, from_previous(v), from_next(v)),
                        jnp.zeros((32, 128), F32),
                    ],
                    axis=0,
                )
            )
    ch, cl = split(jnp.concatenate(columns, axis=1))
    stacked = jnp.concatenate([ch, cl, ch, jnp.zeros((32, LANES), BF16)], axis=0)
    rh, rl = split(jnp.concatenate(rims, axis=1))
    for f in range(4):
        rows = pl.ds(128 * f, 128)
        direct = dot(tc[rows, :], stacked)
        coupled = dot(tf_h[rows, :], rh) + dot(tf_h[rows, :], rl) + dot(tf_l[rows, :], rh)
        final = xhat[f] + 0.2 * direct + 0.4 * (dinv[...] * coupled)
        value = mm3(bb_h[...], bb_l[...], final)
        for c in range(4):
            outv[pl.ds(500 * f + c, 125, stride=4), :] = value[0:125, 128 * c : 128 * c + 128]
    for copy in sent:
        copy.wait_send()


def solution(mesh):
    nx, ny = mesh.shape["px"], mesh.shape["py"]
    table = column_table()

    def per_device(
        right_side, first_guess, coefficient, modal_basis, modal_values, patch_inverse, patch_elements, patch_mask
    ):
        hbm = pl.BlockSpec(memory_space=pltpu.HBM)

        def body(*refs):
            kernel(nx, ny, *refs)

        def f32(*shape):
            return pltpu.VMEM(shape, F32)

        def b16(*shape):
            return pltpu.VMEM(shape, BF16)

        def in_hbm(array):
            return pltpu.with_memory_space_constraint(array, pltpu.HBM)

        dma = pltpu.SemaphoreType.DMA
        out = pl.pallas_call(
            body,
            out_shape=pltpu.VMEM((2000, 128), F32),
            in_specs=[hbm] * 12,
            out_specs=pl.BlockSpec(memory_space=pltpu.VMEM),
            scratch_shapes=[
                pltpu.SMEM((5, 5), F32), pltpu.SMEM((5,), F32),
                f32(4, 125, 512), f32(4, 125, 512), f32(2, 4, 25, 512), f32(2, 4, 5, 5, 512), f32(2, 4, 25, 512),
                f32(4, 128), f32(256, 256), pltpu.VMEM((8, 512), jnp.int32), pltpu.VMEM((8, 512), jnp.int32),
                pltpu.VMEM((8, 640), jnp.int32),
                b16(128, 128), b16(128, 128), b16(128, 256), b16(128, 256), b16(128, 128), b16(128, 128),
                b16(256, 128), b16(256, 128),
                b16(32, 512), b16(32, 512), b16(96, 512), b16(96, 512),
                b16(512, 128), b16(512, 128), b16(512, 128), b16(256, 256), b16(256, 256),
                f32(4, 128, 512), f32(4, 128, 512), f32(128, 512), b16(1152, 512),
                b16(512, 512), b16(512, 512), b16(512, 512), b16(512, 512),
                b16(512, 1152), f32(256, 512), b16(256, 512), b16(256, 512), f32(256, 512), b16(512, 512),
                f32(256, 1152),
                f32(2, 4, 32, 256), f32(2, 4, 40, 256), f32(2, 4, 32, 256), f32(2, 4, 40, 256), f32(4, 256, 512),
                f32(8, 128, 128), f32(8, 128, 128), f32(8, 128, 128), f32(8, 128, 128),
                dma((20,)), dma((6,)), dma((6,)), dma((4,)), dma((4,)), dma((8,)), dma((8,)), dma((8,)), dma((8,)),
            ],
            compiler_params=pltpu.CompilerParams(
                collective_id=0, has_side_effects=True, vmem_limit_bytes=60 * 1024 * 1024
            ),
        )(
            in_hbm(first_guess.reshape(4, 125, 1, 512)),
            in_hbm(first_guess.reshape(4, 5, 25, 2, 1, 256)),
            in_hbm(first_guess.reshape(4, 5, 5, 5, 2, 2, 1, 128)),
            in_hbm(first_guess.reshape(4, 25, 5, 1, 512)),
            in_hbm(right_side.reshape(4, 125, 1, 512)),
            in_hbm(coefficient.reshape(4, 128)),
            in_hbm(modal_basis),
            in_hbm(modal_values),
            in_hbm(patch_inverse),
            in_hbm(patch_elements.T),
            in_hbm(patch_mask.T),
            in_hbm(jnp.asarray(table)),
        )
        return out.reshape(4, 5, 5, 5, 2, 2, 128)

    grid = P(None, None, None, None, "px", "py", None)
    rows = P(("px", "py"), None)
    return jax.shard_map(
        per_device,
        mesh=mesh,
        in_specs=(grid, grid, P("px", "py", None), P(), P(), P(), rows, rows),
        out_specs=grid,
        check_vma=False,
    )
```

```python
import math

import jax
import jax.numpy as jnp
import numpy as np
from jax import lax
from jax.experimental import pallas as pl
from jax.experimental.pallas import tpu as pltpu
from jax.sharding import PartitionSpec as P

MESH = pl.DeviceIdType.MESH
F32 = jnp.float32
BF16 = jnp.bfloat16
DIRS = ((1, 0), (-1, 0), (0, 1), (0, -1), (1, 1), (1, -1), (-1, 1), (-1, -1))
LANES = 512


def linear_values():
    root = np.float32(math.sqrt(3.0 / 7.0))
    points = np.array([-1.0, -root, 0.0, root, 1.0], np.float32)
    half = np.float32(0.5)
    return (1 - points) * half, (1 + points) * half


def column_table():
    table = np.full((8, 640), 7, np.int32)
    table[3] = 9

    def put(column, i, j, k, f=9):
        table[0:4, column] = (i, j, k, f)

    for n in range(125):
        put(n, n // 25, n // 5 % 5, n % 5)
    for g in range(25):
        u, v = g // 5, g % 5
        put(128 + g, 4, u, v)
        put(160 + g, 0, u, v)
        put(192 + u * 8 + v, u, 4, v)
        put(232 + u * 8 + v, u, 0, v)
        put(272 + g, u, v, 4)
        put(304 + g, u, v, 0)
    for r in range(32):
        a, b, f, c = r // 16, r // 8 % 2, r // 2 % 4, r % 2
        for copy in range(3):
            put(384 + 32 * copy + r, 5 + a, 5 + b, 5 + c, f)
        put(512 + 64 + r, 5 + a, 5 + b, 4 if c == 0 else 0, f)
    for r in range(16):
        h, f, c = r // 8, r // 2 % 4, r % 2
        put(512 + r, 4, 5 + h, 5 + c, f)
        put(528 + r, 0, 5 + h, 5 + c, f)
        put(544 + r, 5 + h, 4, 5 + c, f)
        put(560 + r, 5 + h, 0, 5 + c, f)
    return table


def split(value):
    high = value.astype(BF16)
    return high, (value - high.astype(F32)).astype(BF16)


def dot(a, b):
    return lax.dot_general(a, b, (((1,), (0,)), ((), ())), preferred_element_type=F32)


def dot_nt(a, b):
    return lax.dot_general(a, b, (((1,), (1,)), ((), ())), preferred_element_type=F32)


def mm3(ah, al, x):
    xh, xl = split(x)
    return dot(ah, xh) + dot(ah, xl) + dot(al, xh)


def iota(shape, dim):
    return lax.broadcasted_iota(jnp.int32, shape, dim)


def a_half(v, a):
    return v[16 * a : 16 * a + 16]


def b_half(v, b):
    return jnp.concatenate([v[8 * b : 8 * b + 8], v[16 + 8 * b : 24 + 8 * b]], axis=0)


def add_a(v, a, h):
    parts = [v[0:16], v[16:32]]
    parts[a] = parts[a] + h
    return jnp.concatenate(parts, axis=0)


def add_b(v, b, h):
    parts = [v[0:8], v[8:16], v[16:24], v[24:32]]
    parts[b] = parts[b] + h[0:8]
    parts[2 + b] = parts[2 + b] + h[8:16]
    return jnp.concatenate(parts, axis=0)


def rows_to(v, rows):
    return jnp.concatenate([v, jnp.zeros((rows - v.shape[0], v.shape[1]), v.dtype)], axis=0)


def from_next(v):
    lane = iota(v.shape, 1)
    return jnp.where(lane == 127, 0.0, pltpu.roll(v, 127, 1))


def from_previous(v):
    lane = iota(v.shape, 1)
    return jnp.where(lane == 0, 0.0, pltpu.roll(v, 1, 1))


def by_column(fn, v):
    return jnp.concatenate([fn(v[:, 128 * c : 128 * c + 128]) for c in range(4)], axis=1)


def kernel(
    nx, ny,
    xa, xx, xy, xz, ba, coef_h, ub_h, mv_h, pinv_h, pe_h, pm_h, tab_h,
    outv,
    ub, mv, xin, bin_, nfx, nfy, nfz, coef, pinv, pe, pm, tab,
    bt_h, bt_l, bte_h, bte_l, bb_h, bb_l, fb_h, fb_l,
    qc_h, qc_l, qf_h, qf_l, tc, tf_h, tf_l, mi_h, mi_l,
    xhat, bhat, dinv, oh, xs_h, xs_l, ts_h, ts_l,
    cp, gath, wh, wl, ans, ap, vv,
    sx, sy, rx, ry, fz, s2, r2, s3, r3,
    lsem, ssem1, rsem1, ssemf, rsemf, ssem2, rsem2, ssem3, rsem3,
):
    px, py = lax.axis_index("px"), lax.axis_index("py")

    def peer(dx, dy):
        return (lax.rem(px + dx + nx, nx), lax.rem(py + dy + ny, ny))

    inside = {(1, 0): px < nx - 1, (-1, 0): px > 0, (0, 1): py < ny - 1, (0, -1): py > 0}

    def exists(dx, dy):
        if dx == 0 or dy == 0:
            return inside[(dx, dy)]
        return inside[(dx, 0)] & inside[(0, dy)]

    def unless(condition):
        return pl.when(jnp.logical_not(condition))

    local = []

    def load(src, dst):
        copy = pltpu.make_async_copy(src, dst, lsem.at[len(local)])
        copy.start()
        local.append(copy)

    load(tab_h, tab)
    load(coef_h, coef)
    load(ub_h, ub)
    load(mv_h, mv)
    load(xa.at[:, :, 0, :], xin)
    load(ba.at[:, :, 0, :], bin_)
    load(pe_h, pe)
    load(pm_h, pm)
    load(pinv_h, pinv)
    load(xx.at[:, 0, :, 1, 0, :], nfx.at[0, :, :, pl.ds(0, 256)])
    load(xx.at[:, 4, :, 0, 0, :], nfx.at[1, :, :, pl.ds(256, 256)])
    for x in range(2):
        load(xy.at[:, :, 0, :, x, 1, 0, :], nfy.at[0, :, :, :, pl.ds(256 * x, 128)])
        load(xy.at[:, :, 4, :, x, 0, 0, :], nfy.at[1, :, :, :, pl.ds(256 * x + 128, 128)])
    load(xz.at[:, :, 0, 0, :], nfz.at[0])
    load(xz.at[:, :, 4, 0, :], nfz.at[1])

    barrier = pltpu.get_barrier_semaphore()
    greeted = 0
    for dx, dy in DIRS:
        greeted = greeted + jnp.where(exists(dx, dy), 1, 0)

        @pl.when(exists(dx, dy))
        def _():
            pl.semaphore_signal(barrier, inc=1, device_id=peer(dx, dy), device_id_type=MESH)

    @unless(inside[(1, 0)])
    def _():
        nfx[0, :, :, 256:512] = jnp.zeros((4, 25, 256), F32)
        rx[1] = jnp.zeros((4, 32, 256), F32)

    @unless(inside[(-1, 0)])
    def _():
        nfx[1, :, :, 0:256] = jnp.zeros((4, 25, 256), F32)
        rx[0] = jnp.zeros((4, 32, 256), F32)

    @unless(inside[(0, 1)])
    def _():
        for x in range(2):
            nfy[0, :, :, :, 256 * x + 128 : 256 * x + 256] = jnp.zeros((4, 5, 5, 128), F32)
        ry[1] = jnp.zeros((4, 40, 256), F32)

    @unless(inside[(0, -1)])
    def _():
        for x in range(2):
            nfy[1, :, :, :, 256 * x : 256 * x + 128] = jnp.zeros((4, 5, 5, 128), F32)
        ry[0] = jnp.zeros((4, 40, 256), F32)

    for n, (dx, dy) in enumerate(DIRS):

        @unless(exists(-dx, -dy))
        def _():
            r2[n] = jnp.zeros((128, 128), F32)
            r3[n] = jnp.zeros((128, 128), F32)

    pl.semaphore_wait(barrier, greeted)

    sent = []

    def send(src, dst, ssem, rsem, dx, dy):
        copy = pltpu.make_async_remote_copy(
            src_ref=src, dst_ref=dst, send_sem=ssem, recv_sem=rsem, device_id=peer(dx, dy), device_id_type=MESH
        )

        @pl.when(exists(dx, dy))
        def _():
            copy.start()

        sent.append((copy, dx, dy))
        return sent[-1]

    def receive(copies):
        for copy, dx, dy in copies:

            @pl.when(exists(-dx, -dy))
            def _():
                copy.wait_recv()

    first = [
        send(xx.at[:, 4, :, 1, 0, :], nfx.at[1, :, :, pl.ds(0, 256)], ssem1.at[0], rsem1.at[0], 1, 0),
        send(xx.at[:, 0, :, 0, 0, :], nfx.at[0, :, :, pl.ds(256, 256)], ssem1.at[1], rsem1.at[1], -1, 0),
    ]
    for x in range(2):
        first.append(
            send(xy.at[:, :, 4, :, x, 1, 0, :], nfy.at[1, :, :, :, pl.ds(256 * x, 128)],
                 ssem1.at[2 + 2 * x], rsem1.at[2 + 2 * x], 0, 1)
        )
        first.append(
            send(xy.at[:, :, 0, :, x, 0, 0, :], nfy.at[0, :, :, :, pl.ds(256 * x + 128, 128)],
                 ssem1.at[3 + 2 * x], rsem1.at[3 + 2 * x], 0, -1)
        )

    for copy in local[0:4]:
        copy.wait()
    basis = [[ub[p, q] for q in range(5)] for p in range(5)]
    for weights in linear_values():
        basis.append([sum(float(weights[i]) * basis[i][q] for i in range(5)) for q in range(5)])
    spectrum = [mv[q] for q in range(5)]

    def mode_index(shape):
        row = iota(shape, 0)
        i = (row * 41) >> 10
        rest = row - 25 * i
        j = (rest * 13) >> 6
        return i, j, rest - 5 * j

    def block(start):
        modes = mode_index((128, 128))
        result = None
        for d in range(3):
            index = tab[d : d + 1, start : start + 128]
            hits = [index == p for p in range(7)]
            grown = jnp.zeros((128, 128), F32)
            for q in range(5):
                line = jnp.zeros((1, 128), F32)
                for p in range(7):
                    line = jnp.where(hits[p], basis[p][q], line)
                grown = jnp.where(modes[d] == q, line, grown)
            result = grown if result is None else result * grown
        return result

    nodes = block(0)
    bt_h[...], bt_l[...] = split(nodes)
    bb_h[...], bb_l[...] = split(nodes.T)
    for part in range(2):
        faces = block(128 + 128 * part)
        span = pl.ds(128 * part, 128)
        bte_h[:, span], bte_l[:, span] = split(faces)
        fb_h[span, :], fb_l[span, :] = split(faces.T)
    field = tab[3:4, 384:512]
    coarse_block = block(384)
    copy_of = iota((128, 128), 1)
    for f in range(4):
        part = jnp.where(field == f, coarse_block, 0.0)
        high, low = split(part)
        tc[pl.ds(128 * f, 128), :] = jnp.where(copy_of < 64, high.astype(F32), low.astype(F32)).astype(BF16)
        turned = part.T
        qc_h[:, pl.ds(128 * f, 128)], qc_l[:, pl.ds(128 * f, 128)] = split(turned[0:32])
    field = tab[3:4, 512:640]
    face_block = block(512)
    for f in range(4):
        part = jnp.where(field == f, face_block, 0.0)
        tf_h[pl.ds(128 * f, 128), :], tf_l[pl.ds(128 * f, 128), :] = split(part)
        turned = part.T
        qf_h[:, pl.ds(128 * f, 128)], qf_l[:, pl.ds(128 * f, 128)] = split(turned[0:96])

    modes = mode_index((128, 128))
    total = jnp.zeros((128, 128), F32)
    for d in range(3):
        for q in range(5):
            total = jnp.where(modes[d] == q, total + spectrum[q], total)

    def diagonal(c):
        return total * coef[c : c + 1, :] + 1.0

    for c in range(4):
        dinv[:, pl.ds(128 * c, 128)] = 1.0 / diagonal(c)

    local[4].wait()
    local[5].wait()
    for f in range(4):
        xhat[f] = mm3(bt_h[...], bt_l[...], rows_to(xin[f], 128))
        bhat[f] = mm3(bt_h[...], bt_l[...], rows_to(bin_[f], 128))

    local[6].wait()
    local[7].wait()
    elements = pe[...]
    alive = pm[...] != 0
    at_x = (elements >> 11) - 2 * px + 1
    at_y = ((elements >> 7) & 15) - 2 * py + 1
    at_z = elements & 127

    def least(v, most):
        return jnp.minimum(jnp.min(jnp.where(alive, v, most), axis=0, keepdims=True), most)

    low_x, low_y, low_z = least(at_x, 2), least(at_y, 2), least(at_z, 126)
    key = (low_x * 3 + low_y) * 128 + low_z
    place = (at_x - low_x) * 4 + (at_y - low_y) * 2 + (at_z - low_z)
    place = jnp.where(alive, place, 99)
    vertex = iota((128, LANES), 0)
    for v in range(9):
        oh[pl.ds(128 * v, 128), :] = jnp.where(vertex + 128 * v == key, 1.0, 0.0).astype(BF16)

    local[8].wait()
    r = iota((256, 256), 0)
    source = (((r >> 1) & 3) * 8 + ((r >> 4) & 1) * 4 + ((r >> 3) & 1) * 2 + (r & 1)) * 8 + (r >> 5)
    order = jnp.where(iota((256, 256), 1) == source, 1.0, 0.0).astype(BF16)
    for piece, target in zip(split(pinv[...]), (mi_h, mi_l)):
        target[...] = dot_nt(dot(order, piece).astype(BF16), order).astype(BF16)

    for copy in local[9:]:
        copy.wait()
    receive(first)

    for f in range(4):
        parts = [
            rows_to(nfx[0, f], 32),
            rows_to(nfx[1, f], 32),
        ]
        parts += [rows_to(nfy[0, f, i], 8) for i in range(5)]
        parts += [rows_to(nfy[1, f, i], 8) for i in range(5)]
        parts.append(by_column(from_next, rows_to(nfz[0, f], 32)))
        parts.append(by_column(from_previous, rows_to(nfz[1, f], 32)))
        parts.append(jnp.zeros((48, LANES), F32))
        around = mm3(bte_h[...], bte_l[...], jnp.concatenate(parts, axis=0))
        loaded = bhat[f] + 0.5 * around
        x0 = xhat[f]
        x1 = 0.2 * x0 + 0.8 * (dinv[...] * loaded)
        diag = jnp.concatenate([diagonal(c) for c in range(4)], axis=1)
        rest = bhat[f] - 0.2 * (diag * x0) - 0.8 * loaded
        xhat[f] = x1
        rows = pl.ds(128 * f, 128)
        xs_h[rows, :], xs_l[rows, :] = split(x1)
        ts_h[rows, :], ts_l[rows, :] = split(rest)

    inner = dot(qc_h[...], ts_h[...]) + dot(qc_h[...], ts_l[...]) + dot(qc_l[...], ts_h[...])
    rim = 0.5 * (dot(qf_h[...], xs_h[...]) + dot(qf_h[...], xs_l[...]) + dot(qf_l[...], xs_h[...]))
    up_row = ((iota((32, 128), 0) & 1) == 1)

    def rim_of(start, size, c):
        return rim[start : start + size, 128 * c : 128 * c + 128]

    own = {}
    for x in range(2):
        for y in range(2):
            c = 2 * x + y
            v = inner[:, 128 * c : 128 * c + 128]
            faces = rim_of(64, 32, c)
            v = v + jnp.where(up_row, from_next(faces), from_previous(faces))
            v = add_a(v, 0, rim_of(0, 16, y)) if x == 1 else add_a(v, 1, rim_of(16, 16, 2 + y))
            v = add_b(v, 0, rim_of(32, 16, 2 * x)) if y == 1 else add_b(v, 1, rim_of(48, 16, 2 * x + 1))
            own[(x, y)] = v
    hx = {(1, y): rim_of(0, 16, 2 + y) for y in range(2)} | {(-1, y): rim_of(16, 16, y) for y in range(2)}
    hy = {(1, x): rim_of(32, 16, 2 * x + 1) for x in range(2)} | {(-1, x): rim_of(48, 16, 2 * x) for x in range(2)}

    def edge(d):
        return 1 if d == 1 else 0

    def exchange(blocks, sbuf, rbuf, ssem, rsem):
        copies = []
        for n, (dx, dy) in enumerate(DIRS):
            at = 0
            for v in blocks(dx, dy):
                sbuf[n, pl.ds(at, v.shape[0]), :] = v
                at += v.shape[0]
            copies.append(
                send(sbuf.at[n, pl.ds(0, at)], rbuf.at[n, pl.ds(0, at)], ssem.at[n], rsem.at[n], dx, dy)
            )
        return copies

    def residual_blocks(dx, dy):
        x, y = edge(dx), edge(dy)
        if dy == 0:
            return [own[(x, 0)], own[(x, 1)], hx[(dx, 0)], hx[(dx, 1)], hy[(1, x)], hy[(-1, x)]]
        if dx == 0:
            return [own[(0, y)], own[(1, y)], hy[(dy, 0)], hy[(dy, 1)], hx[(1, y)], hx[(-1, y)]]
        return [own[(x, y)], hx[(dx, y)], hy[(dy, x)]]

    second = exchange(residual_blocks, s2, r2, ssem2, rsem2)

    for f in range(4):
        rows = pl.ds(128 * f, 128)
        for part in range(2):
            span = pl.ds(128 * part, 128)
            faces = (
                dot(fb_h[span, :], xs_h[rows, :])
                + dot(fb_h[span, :], xs_l[rows, :])
                + dot(fb_l[span, :], xs_h[rows, :])
            )
            fz[f, span, :] = faces
        sx[0, f] = fz[f, 0:32, 256:512]
        sx[1, f] = fz[f, 32:64, 0:256]
        for x in range(2):
            sy[0, f, :, pl.ds(128 * x, 128)] = fz[f, 64:104, 256 * x + 128 : 256 * x + 256]
            sy[1, f, :, pl.ds(128 * x, 128)] = fz[f, 104:144, 256 * x : 256 * x + 128]
    whole = [
        send(sx.at[0], rx.at[0], ssemf.at[0], rsemf.at[0], 1, 0),
        send(sx.at[1], rx.at[1], ssemf.at[1], rsemf.at[1], -1, 0),
        send(sy.at[0], ry.at[0], ssemf.at[2], rsemf.at[2], 0, 1),
        send(sy.at[1], ry.at[1], ssemf.at[3], rsemf.at[3], 0, -1),
    ]

    receive(second)
    field_of = {}

    def put(at, v):
        field_of[at] = field_of[at] + v if at in field_of else v

    for at, v in own.items():
        put(at, v)
    late = []
    for y in range(2):
        late += [("a", 0, (2, y), hx[(1, y)]), ("a", 1, (-1, y), hx[(-1, y)])]
        late += [("b", 0, (y, 2), hy[(1, y)]), ("b", 1, (y, -1), hy[(-1, y)])]
    for n, (dx, dy) in enumerate(DIRS):
        x, y = edge(dx), edge(dy)
        side_a, side_b = (0 if dx == 1 else 1), (0 if dy == 1 else 1)
        if dy == 0:
            for t in range(2):
                put((x - 2 * dx, t), r2[n, 32 * t : 32 * t + 32, :])
                late.append(("a", side_a, (x - dx, t), r2[n, 64 + 16 * t : 80 + 16 * t, :]))
            late.append(("b", 0, (x - 2 * dx, 2), r2[n, 96:112, :]))
            late.append(("b", 1, (x - 2 * dx, -1), r2[n, 112:128, :]))
        elif dx == 0:
            for t in range(2):
                put((t, y - 2 * dy), r2[n, 32 * t : 32 * t + 32, :])
                late.append(("b", side_b, (t, y - dy), r2[n, 64 + 16 * t : 80 + 16 * t, :]))
            late.append(("a", 0, (2, y - 2 * dy), r2[n, 96:112, :]))
            late.append(("a", 1, (-1, y - 2 * dy), r2[n, 112:128, :]))
        else:
            put((x - 2 * dx, y - 2 * dy), r2[n, 0:32, :])
            late.append(("a", side_a, (x - dx, y - 2 * dy), r2[n, 32:48, :]))
            late.append(("b", side_b, (x - 2 * dx, y - dy), r2[n, 48:64, :]))
    for kind, side, at, v in late:
        field_of[at] = add_a(field_of[at], side, v) if kind == "a" else add_b(field_of[at], side, v)

    for (x, y), v in field_of.items():
        moved = pltpu.roll(v, 127, 1)
        for z, value in enumerate((v, moved)):
            pieces = split(value)
            for sx_, sy_ in ((0, 0), (0, 1), (1, 0), (1, 1)):
                vx, vy = x + 1 - sx_, y + 1 - sy_
                if 0 <= vx <= 2 and 0 <= vy <= 2:
                    p = sx_ * 4 + sy_ * 2 + z
                    for t in range(2):
                        cp[pl.ds(256 * t + 32 * p, 32), pl.ds(128 * (3 * vx + vy), 128)] = pieces[t]
    gath[...] = dot(cp[pl.ds(0, 256), :], oh[...]) + dot(cp[pl.ds(256, 256), :], oh[...])
    for s in range(8):
        slot = jnp.broadcast_to(place[s : s + 1, :], (32, LANES))
        value = jnp.zeros((32, LANES), F32)
        for p in range(8):
            value = jnp.where(slot == p, gath[pl.ds(32 * p, 32), :], value)
        rows = pl.ds(32 * s, 32)
        wh[rows, :], wl[rows, :] = split(value)
    ans[...] = dot(mi_h[...], wh[...]) + dot(mi_h[...], wl[...]) + dot(mi_l[...], wh[...])
    for p in range(8):
        value = jnp.zeros((32, LANES), F32)
        for s in range(8):
            slot = jnp.broadcast_to(place[s : s + 1, :], (32, LANES))
            value = jnp.where(slot == p, ans[pl.ds(32 * s, 32), :], value)
        ap[pl.ds(32 * p, 32), :], ap[pl.ds(256 + 32 * p, 32), :] = split(value)
    vv[...] = dot_nt(ap[pl.ds(0, 256), :], oh[...]) + dot_nt(ap[pl.ds(256, 256), :], oh[...])
    spread = {}
    for x in range(-1, 3):
        for y in range(-1, 3):
            sums = [None, None]
            for sx_, sy_ in ((0, 0), (0, 1), (1, 0), (1, 1)):
                vx, vy = x + 1 - sx_, y + 1 - sy_
                if 0 <= vx <= 2 and 0 <= vy <= 2:
                    for z in range(2):
                        p = sx_ * 4 + sy_ * 2 + z
                        v = vv[pl.ds(32 * p, 32), pl.ds(128 * (3 * vx + vy), 128)]
                        sums[z] = v if sums[z] is None else sums[z] + v
            spread[(x, y)] = sums[0] + pltpu.roll(sums[1], 1, 1)

    def correction_blocks(dx, dy):
        x, y = edge(dx), edge(dy)
        if dy == 0:
            return [
                spread[(x + dx, 0)], spread[(x + dx, 1)], a_half(spread[(x, 0)], x), a_half(spread[(x, 1)], x),
                b_half(spread[(x + dx, 2)], 0), b_half(spread[(x + dx, -1)], 1),
            ]
        if dx == 0:
            return [
                spread[(0, y + dy)], spread[(1, y + dy)], b_half(spread[(0, y)], y), b_half(spread[(1, y)], y),
                a_half(spread[(2, y + dy)], 0), a_half(spread[(-1, y + dy)], 1),
            ]
        return [spread[(x + dx, y + dy)], a_half(spread[(x, y + dy)], x), b_half(spread[(x + dx, y)], y)]

    third = exchange(correction_blocks, s3, r3, ssem3, rsem3)

    receive(whole)
    for f in range(4):
        x_up = jnp.concatenate([fz[f, 32:64, 256:512], rx[1, f]], axis=1)
        x_down = jnp.concatenate([rx[0, f], fz[f, 0:32, 0:256]], axis=1)
        y_up, y_down = [], []
        for x in range(2):
            y_up += [fz[f, 104:144, 256 * x + 128 : 256 * x + 256], ry[1, f, :, 128 * x : 128 * x + 128]]
            y_down += [ry[0, f, :, 128 * x : 128 * x + 128], fz[f, 64:104, 256 * x : 256 * x + 128]]
        parts = [
            x_up, x_down,
            jnp.concatenate(y_up, axis=1),
            jnp.concatenate(y_down, axis=1),
            by_column(from_next, fz[f, 176:208, :]),
            by_column(from_previous, fz[f, 144:176, :]),
            jnp.zeros((48, LANES), F32),
        ]
        around = mm3(bte_h[...], bte_l[...], jnp.concatenate(parts, axis=0))
        xhat[f] = 0.2 * xhat[f] + 0.8 * (dinv[...] * (bhat[f] + 0.5 * around))

    receive(third)
    fixed = {at: spread[at] for at in own}
    near_x = {(2, y): a_half(spread[(2, y)], 0) for y in range(2)} | {
        (-1, y): a_half(spread[(-1, y)], 1) for y in range(2)
    }
    near_y = {(x, 2): b_half(spread[(x, 2)], 0) for x in range(2)} | {
        (x, -1): b_half(spread[(x, -1)], 1) for x in range(2)
    }
    for n, (dx, dy) in enumerate(DIRS):
        x, y = edge(dx), edge(dy)
        if dy == 0:
            for t in range(2):
                fixed[(x - dx, t)] += r3[n, 32 * t : 32 * t + 32, :]
                near_x[(x - 2 * dx, t)] += r3[n, 64 + 16 * t : 80 + 16 * t, :]
            near_y[(x - dx, 2)] += r3[n, 96:112, :]
            near_y[(x - dx, -1)] += r3[n, 112:128, :]
        elif dx == 0:
            for t in range(2):
                fixed[(t, y - dy)] += r3[n, 32 * t : 32 * t + 32, :]
                near_y[(t, y - 2 * dy)] += r3[n, 64 + 16 * t : 80 + 16 * t, :]
            near_x[(2, y - dy)] += r3[n, 96:112, :]
            near_x[(-1, y - dy)] += r3[n, 112:128, :]
        else:
            fixed[(x - dx, y - dy)] += r3[n, 0:32, :]
            near_x[(x - 2 * dx, y - dy)] += r3[n, 32:48, :]
            near_y[(x - dx, y - 2 * dy)] += r3[n, 48:64, :]

    columns, rims = [], []
    for x in range(2):
        for y in range(2):
            v = fixed[(x, y)]
            columns.append(v)
            rims.append(
                jnp.concatenate(
                    [
                        a_half(fixed[(1, y)], 0) if x == 0 else near_x[(2, y)],
                        a_half(fixed[(0, y)], 1) if x == 1 else near_x[(-1, y)],
                        b_half(fixed[(x, 1)], 0) if y == 0 else near_y[(x, 2)],
                        b_half(fixed[(x, 0)], 1) if y == 1 else near_y[(x, -1)],
                        jnp.where(up_row, from_previous(v), from_next(v)),
                        jnp.zeros((32, 128), F32),
                    ],
                    axis=0,
                )
            )
    ch, cl = split(jnp.concatenate(columns, axis=1))
    stacked = jnp.concatenate([ch, cl, ch, jnp.zeros((32, LANES), BF16)], axis=0)
    rh, rl = split(jnp.concatenate(rims, axis=1))
    for f in range(4):
        rows = pl.ds(128 * f, 128)
        direct = dot(tc[rows, :], stacked)
        coupled = dot(tf_h[rows, :], rh) + dot(tf_h[rows, :], rl) + dot(tf_l[rows, :], rh)
        final = xhat[f] + 0.2 * direct + 0.4 * (dinv[...] * coupled)
        value = mm3(bb_h[...], bb_l[...], final)
        for c in range(4):
            outv[pl.ds(500 * f + c, 125, stride=4), :] = value[0:125, 128 * c : 128 * c + 128]
    for copy, dx, dy in sent:

        @pl.when(exists(dx, dy))
        def _():
            copy.wait_send()


def solution(mesh):
    nx, ny = mesh.shape["px"], mesh.shape["py"]
    table = column_table()

    def per_device(
        right_side, first_guess, coefficient, modal_basis, modal_values, patch_inverse, patch_elements, patch_mask
    ):
        hbm = pl.BlockSpec(memory_space=pltpu.HBM)

        def body(*refs):
            kernel(nx, ny, *refs)

        def f32(*shape):
            return pltpu.VMEM(shape, F32)

        def b16(*shape):
            return pltpu.VMEM(shape, BF16)

        def in_hbm(array):
            return pltpu.with_memory_space_constraint(array, pltpu.HBM)

        dma = pltpu.SemaphoreType.DMA
        out = pl.pallas_call(
            body,
            out_shape=pltpu.VMEM((2000, 128), F32),
            in_specs=[hbm] * 12,
            out_specs=pl.BlockSpec(memory_space=pltpu.VMEM),
            scratch_shapes=[
                pltpu.SMEM((5, 5), F32), pltpu.SMEM((5,), F32),
                f32(4, 125, 512), f32(4, 125, 512), f32(2, 4, 25, 512), f32(2, 4, 5, 5, 512), f32(2, 4, 25, 512),
                f32(4, 128), f32(256, 256), pltpu.VMEM((8, 512), jnp.int32), pltpu.VMEM((8, 512), jnp.int32),
                pltpu.VMEM((8, 640), jnp.int32),
                b16(128, 128), b16(128, 128), b16(128, 256), b16(128, 256), b16(128, 128), b16(128, 128),
                b16(256, 128), b16(256, 128),
                b16(32, 512), b16(32, 512), b16(96, 512), b16(96, 512),
                b16(512, 128), b16(512, 128), b16(512, 128), b16(256, 256), b16(256, 256),
                f32(4, 128, 512), f32(4, 128, 512), f32(128, 512), b16(1152, 512),
                b16(512, 512), b16(512, 512), b16(512, 512), b16(512, 512),
                b16(512, 1152), f32(256, 512), b16(256, 512), b16(256, 512), f32(256, 512), b16(512, 512),
                f32(256, 1152),
                f32(2, 4, 32, 256), f32(2, 4, 40, 256), f32(2, 4, 32, 256), f32(2, 4, 40, 256), f32(4, 256, 512),
                f32(8, 128, 128), f32(8, 128, 128), f32(8, 128, 128), f32(8, 128, 128),
                dma((20,)), dma((6,)), dma((6,)), dma((4,)), dma((4,)), dma((8,)), dma((8,)), dma((8,)), dma((8,)),
            ],
            compiler_params=pltpu.CompilerParams(
                collective_id=0, has_side_effects=True, vmem_limit_bytes=60 * 1024 * 1024
            ),
        )(
            in_hbm(first_guess.reshape(4, 125, 1, 512)),
            in_hbm(first_guess.reshape(4, 5, 25, 2, 1, 256)),
            in_hbm(first_guess.reshape(4, 5, 5, 5, 2, 2, 1, 128)),
            in_hbm(first_guess.reshape(4, 25, 5, 1, 512)),
            in_hbm(right_side.reshape(4, 125, 1, 512)),
            in_hbm(coefficient.reshape(4, 128)),
            in_hbm(modal_basis),
            in_hbm(modal_values),
            in_hbm(patch_inverse),
            in_hbm(patch_elements.T),
            in_hbm(patch_mask.T),
            in_hbm(jnp.asarray(table)),
        )
        return out.reshape(4, 5, 5, 5, 2, 2, 128)

    grid = P(None, None, None, None, "px", "py", None)
    rows = P(("px", "py"), None)
    return jax.shard_map(
        per_device,
        mesh=mesh,
        in_specs=(grid, grid, P("px", "py", None), P(), P(), P(), rows, rows),
        out_specs=grid,
        check_vma=False,
    )
```

```python
import math

import jax
import jax.numpy as jnp
import numpy as np
from jax import lax
from jax.experimental import pallas as pl
from jax.experimental.pallas import tpu as pltpu
from jax.sharding import PartitionSpec as P

MESH = pl.DeviceIdType.MESH
F32 = jnp.float32
BF16 = jnp.bfloat16
DIRS = ((1, 1), (1, -1), (-1, 1), (-1, -1), (1, 0), (-1, 0), (0, 1), (0, -1))
LANES = 512


def linear_values():
    root = np.float32(math.sqrt(3.0 / 7.0))
    points = np.array([-1.0, -root, 0.0, root, 1.0], np.float32)
    half = np.float32(0.5)
    return (1 - points) * half, (1 + points) * half


def column_table():
    table = np.full((8, 640), 7, np.int32)
    table[3] = 9

    def put(column, i, j, k, f=9):
        table[0:4, column] = (i, j, k, f)

    for n in range(125):
        put(n, n // 25, n // 5 % 5, n % 5)
    for g in range(25):
        u, v = g // 5, g % 5
        put(128 + g, 4, u, v)
        put(160 + g, 0, u, v)
        put(192 + u * 8 + v, u, 4, v)
        put(232 + u * 8 + v, u, 0, v)
        put(272 + g, u, v, 4)
        put(304 + g, u, v, 0)
    for r in range(32):
        a, b, f, c = r // 16, r // 8 % 2, r // 2 % 4, r % 2
        for copy in range(3):
            put(384 + 32 * copy + r, 5 + a, 5 + b, 5 + c, f)
        put(512 + 64 + r, 5 + a, 5 + b, 4 if c == 0 else 0, f)
    for r in range(16):
        h, f, c = r // 8, r // 2 % 4, r % 2
        put(512 + r, 4, 5 + h, 5 + c, f)
        put(528 + r, 0, 5 + h, 5 + c, f)
        put(544 + r, 5 + h, 4, 5 + c, f)
        put(560 + r, 5 + h, 0, 5 + c, f)
    return table


def split(value):
    high = value.astype(BF16)
    return high, (value - high.astype(F32)).astype(BF16)


def dot(a, b):
    return lax.dot_general(a, b, (((1,), (0,)), ((), ())), preferred_element_type=F32)


def dot_nt(a, b):
    return lax.dot_general(a, b, (((1,), (1,)), ((), ())), preferred_element_type=F32)


def mm3(ah, al, x):
    xh, xl = split(x)
    return dot(ah, xh) + dot(ah, xl) + dot(al, xh)


def iota(shape, dim):
    return lax.broadcasted_iota(jnp.int32, shape, dim)


def a_half(v, a):
    return v[16 * a : 16 * a + 16]


def b_half(v, b):
    return jnp.concatenate([v[8 * b : 8 * b + 8], v[16 + 8 * b : 24 + 8 * b]], axis=0)


def add_a(v, a, h):
    parts = [v[0:16], v[16:32]]
    parts[a] = parts[a] + h
    return jnp.concatenate(parts, axis=0)


def add_b(v, b, h):
    parts = [v[0:8], v[8:16], v[16:24], v[24:32]]
    parts[b] = parts[b] + h[0:8]
    parts[2 + b] = parts[2 + b] + h[8:16]
    return jnp.concatenate(parts, axis=0)


def rows_to(v, rows):
    return jnp.concatenate([v, jnp.zeros((rows - v.shape[0], v.shape[1]), v.dtype)], axis=0)


def from_next(v):
    lane = iota(v.shape, 1)
    return jnp.where(lane == 127, 0.0, pltpu.roll(v, 127, 1))


def from_previous(v):
    lane = iota(v.shape, 1)
    return jnp.where(lane == 0, 0.0, pltpu.roll(v, 1, 1))


def by_column(fn, v):
    return jnp.concatenate([fn(v[:, 128 * c : 128 * c + 128]) for c in range(4)], axis=1)


def kernel(
    nx, ny,
    xa, xx, xy, xz, ba, coef_h, ub_h, mv_h, pinv_h, pe_h, pm_h, tab_h,
    outv,
    ub, mv, xin, bin_, nfx, nfy, nfz, coef, pinv, pe, pm, tab,
    bt_h, bt_l, bte_h, bte_l, bb_h, bb_l, fb_h, fb_l,
    qc, qf, tc, tf_h, tf_l, mi_h, mi_l,
    xhat, bhat, dinv, oh, xs_h, xs_l, ts_h, ts_l,
    cp, gath, wh, wl, ans, ap, vv,
    sx, sy, rx, ry, fz, s2, r2, s3, r3,
    lsem, ssem1, rsem1, ssemf, rsemf, ssem2, rsem2, ssem3, rsem3,
):
    px, py = lax.axis_index("px"), lax.axis_index("py")

    def peer(dx, dy):
        return (lax.rem(px + dx + nx, nx), lax.rem(py + dy + ny, ny))

    inside = {(1, 0): px < nx - 1, (-1, 0): px > 0, (0, 1): py < ny - 1, (0, -1): py > 0}

    def exists(dx, dy):
        if dx == 0 or dy == 0:
            return inside[(dx, dy)]
        return inside[(dx, 0)] & inside[(0, dy)]

    def unless(condition):
        return pl.when(jnp.logical_not(condition))

    local = []

    def load(src, dst):
        copy = pltpu.make_async_copy(src, dst, lsem.at[len(local)])
        copy.start()
        local.append(copy)

    load(tab_h, tab)
    load(coef_h, coef)
    load(ub_h, ub)
    load(mv_h, mv)
    load(xa.at[:, :, 0, :], xin)
    load(ba.at[:, :, 0, :], bin_)
    load(pe_h, pe)
    load(pm_h, pm)
    load(pinv_h, pinv)
    load(xx.at[:, 0, :, 1, 0, :], nfx.at[0, :, :, pl.ds(0, 256)])
    load(xx.at[:, 4, :, 0, 0, :], nfx.at[1, :, :, pl.ds(256, 256)])
    for x in range(2):
        load(xy.at[:, :, 0, :, x, 1, 0, :], nfy.at[0, :, :, :, pl.ds(256 * x, 128)])
        load(xy.at[:, :, 4, :, x, 0, 0, :], nfy.at[1, :, :, :, pl.ds(256 * x + 128, 128)])
    load(xz.at[:, :, 0, 0, :], nfz.at[0])
    load(xz.at[:, :, 4, 0, :], nfz.at[1])

    barrier = pltpu.get_barrier_semaphore()
    greeted = 0
    for dx, dy in DIRS[4:]:
        greeted = greeted + jnp.where(exists(dx, dy), 1, 0)

        @pl.when(exists(dx, dy))
        def _():
            pl.semaphore_signal(barrier, inc=1, device_id=peer(dx, dy), device_id_type=MESH)

    @unless(inside[(1, 0)])
    def _():
        nfx[0, :, :, 256:512] = jnp.zeros((4, 25, 256), F32)
        rx[1] = jnp.zeros((4, 32, 256), F32)

    @unless(inside[(-1, 0)])
    def _():
        nfx[1, :, :, 0:256] = jnp.zeros((4, 25, 256), F32)
        rx[0] = jnp.zeros((4, 32, 256), F32)

    @unless(inside[(0, 1)])
    def _():
        for x in range(2):
            nfy[0, :, :, :, 256 * x + 128 : 256 * x + 256] = jnp.zeros((4, 5, 5, 128), F32)
        ry[1] = jnp.zeros((4, 40, 256), F32)

    @unless(inside[(0, -1)])
    def _():
        for x in range(2):
            nfy[1, :, :, :, 256 * x : 256 * x + 128] = jnp.zeros((4, 5, 5, 128), F32)
        ry[0] = jnp.zeros((4, 40, 256), F32)

    for n, (dx, dy) in enumerate(DIRS):

        @unless(exists(-dx, -dy))
        def _():
            r2[n] = jnp.zeros((128, 128), F32)
            r3[n] = jnp.zeros((128, 128), F32)

    pl.semaphore_wait(barrier, greeted)

    sent = []

    def send(src, dst, ssem, rsem, dx, dy):
        copy = pltpu.make_async_remote_copy(
            src_ref=src, dst_ref=dst, send_sem=ssem, recv_sem=rsem, device_id=peer(dx, dy), device_id_type=MESH
        )

        @pl.when(exists(dx, dy))
        def _():
            copy.start()

        sent.append((copy, dx, dy))
        return sent[-1]

    def receive(copies):
        for copy, dx, dy in copies:

            @pl.when(exists(-dx, -dy))
            def _():
                copy.wait_recv()

    first = [
        send(xx.at[:, 4, :, 1, 0, :], nfx.at[1, :, :, pl.ds(0, 256)], ssem1.at[0], rsem1.at[0], 1, 0),
        send(xx.at[:, 0, :, 0, 0, :], nfx.at[0, :, :, pl.ds(256, 256)], ssem1.at[1], rsem1.at[1], -1, 0),
    ]
    for x in range(2):
        first.append(
            send(xy.at[:, :, 4, :, x, 1, 0, :], nfy.at[1, :, :, :, pl.ds(256 * x, 128)],
                 ssem1.at[2 + 2 * x], rsem1.at[2 + 2 * x], 0, 1)
        )
        first.append(
            send(xy.at[:, :, 0, :, x, 0, 0, :], nfy.at[0, :, :, :, pl.ds(256 * x + 128, 128)],
                 ssem1.at[3 + 2 * x], rsem1.at[3 + 2 * x], 0, -1)
        )

    for copy in local[0:4]:
        copy.wait()
    basis = [[ub[p, q] for q in range(5)] for p in range(5)]
    for weights in linear_values():
        basis.append([sum(float(weights[i]) * basis[i][q] for i in range(5)) for q in range(5)])
    spectrum = [mv[q] for q in range(5)]

    def mode_index(shape):
        row = iota(shape, 0)
        i = (row * 41) >> 10
        rest = row - 25 * i
        j = (rest * 13) >> 6
        return i, j, rest - 5 * j

    def block(start):
        modes = mode_index((128, 128))
        result = None
        for d in range(3):
            index = tab[d : d + 1, start : start + 128]
            hits = [index == p for p in range(7)]
            grown = jnp.zeros((128, 128), F32)
            for q in range(5):
                line = jnp.zeros((1, 128), F32)
                for p in range(7):
                    line = jnp.where(hits[p], basis[p][q], line)
                grown = jnp.where(modes[d] == q, line, grown)
            result = grown if result is None else result * grown
        return result

    nodes = block(0)
    bt_h[...], bt_l[...] = split(nodes)
    high, low = split(nodes.T)
    bb_h[...] = jnp.concatenate([high, high], axis=1)
    bb_l[...] = low
    for part in range(2):
        faces = block(128 + 128 * part)
        span = pl.ds(128 * part, 128)
        bte_h[:, span], bte_l[:, span] = split(faces)
        fb_h[span, :], fb_l[span, :] = split(faces.T)
    field = tab[3:4, 384:512]
    coarse_block = block(384)
    copy_of = iota((128, 128), 1)
    for f in range(4):
        part = jnp.where(field == f, coarse_block, 0.0)
        high, low = split(part)
        tc[pl.ds(128 * f, 128), :] = jnp.where(copy_of < 64, high.astype(F32), low.astype(F32)).astype(BF16)
        high, low = split(part.T[0:32])
        qc[0:32, pl.ds(128 * f, 128)] = high
        qc[32:64, pl.ds(128 * f, 128)] = low
    field = tab[3:4, 512:640]
    face_block = block(512)
    for f in range(4):
        part = jnp.where(field == f, face_block, 0.0)
        high, low = split(part)
        tf_h[pl.ds(128 * f, 128), :] = jnp.concatenate([high, high], axis=1)
        tf_l[pl.ds(128 * f, 128), :] = low
        high, low = split(part.T[0:96])
        qf[0:96, pl.ds(128 * f, 128)] = high
        qf[96:192, pl.ds(128 * f, 128)] = low

    modes = mode_index((128, 128))
    total = jnp.zeros((128, 128), F32)
    for d in range(3):
        for q in range(5):
            total = jnp.where(modes[d] == q, total + spectrum[q], total)

    def diagonal(c):
        return total * coef[c : c + 1, :] + 1.0

    for c in range(4):
        dinv[:, pl.ds(128 * c, 128)] = 1.0 / diagonal(c)

    local[4].wait()
    local[5].wait()
    for f in range(4):
        xhat[f] = mm3(bt_h[...], bt_l[...], rows_to(xin[f], 128))
        bhat[f] = mm3(bt_h[...], bt_l[...], rows_to(bin_[f], 128))

    local[6].wait()
    local[7].wait()
    elements = pe[...]
    alive = pm[...] != 0
    at_x = (elements >> 11) - 2 * px + 1
    at_y = ((elements >> 7) & 15) - 2 * py + 1
    at_z = elements & 127

    def least(v, most):
        return jnp.minimum(jnp.min(jnp.where(alive, v, most), axis=0, keepdims=True), most)

    low_x, low_y, low_z = least(at_x, 2), least(at_y, 2), least(at_z, 126)
    key = (low_x * 3 + low_y) * 128 + low_z
    place = (at_x - low_x) * 4 + (at_y - low_y) * 2 + (at_z - low_z)
    place = jnp.where(alive, place, 99)
    vertex = iota((128, LANES), 0)
    for v in range(9):
        oh[pl.ds(128 * v, 128), :] = jnp.where(vertex + 128 * v == key, 1.0, 0.0).astype(BF16)

    local[8].wait()
    r = iota((256, 256), 0)
    source = (((r >> 1) & 3) * 8 + ((r >> 4) & 1) * 4 + ((r >> 3) & 1) * 2 + (r & 1)) * 8 + (r >> 5)
    order = jnp.where(iota((256, 256), 1) == source, 1.0, 0.0).astype(BF16)
    for piece, target in zip(split(pinv[...]), (mi_h, mi_l)):
        target[...] = dot_nt(dot(order, piece).astype(BF16), order).astype(BF16)

    for copy in local[9:]:
        copy.wait()
    receive(first)

    for f in range(4):
        parts = [
            rows_to(nfx[0, f], 32),
            rows_to(nfx[1, f], 32),
        ]
        parts += [rows_to(nfy[0, f, i], 8) for i in range(5)]
        parts += [rows_to(nfy[1, f, i], 8) for i in range(5)]
        parts.append(by_column(from_next, rows_to(nfz[0, f], 32)))
        parts.append(by_column(from_previous, rows_to(nfz[1, f], 32)))
        parts.append(jnp.zeros((48, LANES), F32))
        around = mm3(bte_h[...], bte_l[...], jnp.concatenate(parts, axis=0))
        loaded = bhat[f] + 0.5 * around
        x0 = xhat[f]
        x1 = 0.2 * x0 + 0.8 * (dinv[...] * loaded)
        diag = jnp.concatenate([diagonal(c) for c in range(4)], axis=1)
        rest = bhat[f] - 0.2 * (diag * x0) - 0.8 * loaded
        xhat[f] = x1
        rows = pl.ds(128 * f, 128)
        xs_h[rows, :], xs_l[rows, :] = split(x1)
        ts_h[rows, :], ts_l[rows, :] = split(rest)

    both = dot(qc[...], ts_h[...])
    inner = both[0:32] + both[32:64] + dot(qc[0:32, :], ts_l[...])
    both = dot(qf[...], xs_h[...])
    rim = 0.5 * (both[0:96] + both[96:192] + dot(qf[0:96, :], xs_l[...]))
    up_row = ((iota((32, 128), 0) & 1) == 1)

    def rim_of(start, size, c):
        return rim[start : start + size, 128 * c : 128 * c + 128]

    own = {}
    for x in range(2):
        for y in range(2):
            c = 2 * x + y
            v = inner[:, 128 * c : 128 * c + 128]
            faces = rim_of(64, 32, c)
            v = v + jnp.where(up_row, from_next(faces), from_previous(faces))
            v = add_a(v, 0, rim_of(0, 16, y)) if x == 1 else add_a(v, 1, rim_of(16, 16, 2 + y))
            v = add_b(v, 0, rim_of(32, 16, 2 * x)) if y == 1 else add_b(v, 1, rim_of(48, 16, 2 * x + 1))
            own[(x, y)] = v
    hx = {(1, y): rim_of(0, 16, 2 + y) for y in range(2)} | {(-1, y): rim_of(16, 16, y) for y in range(2)}
    hy = {(1, x): rim_of(32, 16, 2 * x + 1) for x in range(2)} | {(-1, x): rim_of(48, 16, 2 * x) for x in range(2)}

    def edge(d):
        return 1 if d == 1 else 0

    def exchange(blocks, sbuf, rbuf, ssem, rsem):
        copies = []
        for n, (dx, dy) in enumerate(DIRS):
            at = 0
            for v in blocks(dx, dy):
                sbuf[n, pl.ds(at, v.shape[0]), :] = v
                at += v.shape[0]
            copies.append(
                send(sbuf.at[n, pl.ds(0, at)], rbuf.at[n, pl.ds(0, at)], ssem.at[n], rsem.at[n], dx, dy)
            )
        return copies

    def residual_blocks(dx, dy):
        x, y = edge(dx), edge(dy)
        if dy == 0:
            return [own[(x, 0)], own[(x, 1)], hx[(dx, 0)], hx[(dx, 1)], hy[(1, x)], hy[(-1, x)]]
        if dx == 0:
            return [own[(0, y)], own[(1, y)], hy[(dy, 0)], hy[(dy, 1)], hx[(1, y)], hx[(-1, y)]]
        return [own[(x, y)], hx[(dx, y)], hy[(dy, x)]]

    second = exchange(residual_blocks, s2, r2, ssem2, rsem2)

    for f in range(4):
        rows = pl.ds(128 * f, 128)
        for part in range(2):
            span = pl.ds(128 * part, 128)
            faces = (
                dot(fb_h[span, :], xs_h[rows, :])
                + dot(fb_h[span, :], xs_l[rows, :])
                + dot(fb_l[span, :], xs_h[rows, :])
            )
            fz[f, span, :] = faces
        sx[0, f] = fz[f, 0:32, 256:512]
        sx[1, f] = fz[f, 32:64, 0:256]
        for x in range(2):
            sy[0, f, :, pl.ds(128 * x, 128)] = fz[f, 64:104, 256 * x + 128 : 256 * x + 256]
            sy[1, f, :, pl.ds(128 * x, 128)] = fz[f, 104:144, 256 * x : 256 * x + 128]
    receive(second)
    whole = [
        send(sx.at[0], rx.at[0], ssemf.at[0], rsemf.at[0], 1, 0),
        send(sx.at[1], rx.at[1], ssemf.at[1], rsemf.at[1], -1, 0),
        send(sy.at[0], ry.at[0], ssemf.at[2], rsemf.at[2], 0, 1),
        send(sy.at[1], ry.at[1], ssemf.at[3], rsemf.at[3], 0, -1),
    ]
    field_of = {}

    def put(at, v):
        field_of[at] = field_of[at] + v if at in field_of else v

    for at, v in own.items():
        put(at, v)
    late = []
    for y in range(2):
        late += [("a", 0, (2, y), hx[(1, y)]), ("a", 1, (-1, y), hx[(-1, y)])]
        late += [("b", 0, (y, 2), hy[(1, y)]), ("b", 1, (y, -1), hy[(-1, y)])]
    for n, (dx, dy) in enumerate(DIRS):
        x, y = edge(dx), edge(dy)
        side_a, side_b = (0 if dx == 1 else 1), (0 if dy == 1 else 1)
        if dy == 0:
            for t in range(2):
                put((x - 2 * dx, t), r2[n, 32 * t : 32 * t + 32, :])
                late.append(("a", side_a, (x - dx, t), r2[n, 64 + 16 * t : 80 + 16 * t, :]))
            late.append(("b", 0, (x - 2 * dx, 2), r2[n, 96:112, :]))
            late.append(("b", 1, (x - 2 * dx, -1), r2[n, 112:128, :]))
        elif dx == 0:
            for t in range(2):
                put((t, y - 2 * dy), r2[n, 32 * t : 32 * t + 32, :])
                late.append(("b", side_b, (t, y - dy), r2[n, 64 + 16 * t : 80 + 16 * t, :]))
            late.append(("a", 0, (2, y - 2 * dy), r2[n, 96:112, :]))
            late.append(("a", 1, (-1, y - 2 * dy), r2[n, 112:128, :]))
        else:
            put((x - 2 * dx, y - 2 * dy), r2[n, 0:32, :])
            late.append(("a", side_a, (x - dx, y - 2 * dy), r2[n, 32:48, :]))
            late.append(("b", side_b, (x - 2 * dx, y - dy), r2[n, 48:64, :]))
    for kind, side, at, v in late:
        field_of[at] = add_a(field_of[at], side, v) if kind == "a" else add_b(field_of[at], side, v)

    for (x, y), v in field_of.items():
        moved = pltpu.roll(v, 127, 1)
        for z, value in enumerate((v, moved)):
            pieces = split(value)
            for sx_, sy_ in ((0, 0), (0, 1), (1, 0), (1, 1)):
                vx, vy = x + 1 - sx_, y + 1 - sy_
                if 0 <= vx <= 2 and 0 <= vy <= 2:
                    p = sx_ * 4 + sy_ * 2 + z
                    for t in range(2):
                        cp[pl.ds(256 * t + 32 * p, 32), pl.ds(128 * (3 * vx + vy), 128)] = pieces[t]
    halves = [pl.ds(256 * h, 256) for h in range(2)]

    def slots(h):
        return [jnp.broadcast_to(place[t : t + 1, 256 * h : 256 * h + 256], (32, 256)) for t in range(8)]

    for half in halves:
        gath[:, half] = dot(cp[pl.ds(0, 256), :], oh[:, half]) + dot(cp[pl.ds(256, 256), :], oh[:, half])
    for h, half in enumerate(halves):
        for t, slot in enumerate(slots(h)):
            value = jnp.zeros((32, 256), F32)
            for p in range(8):
                value = jnp.where(slot == p, gath[pl.ds(32 * p, 32), half], value)
            rows = pl.ds(32 * t, 32)
            wh[rows, half], wl[rows, half] = split(value)
        ans[:, half] = dot(mi_h[...], wh[:, half]) + dot(mi_h[...], wl[:, half]) + dot(mi_l[...], wh[:, half])
    for h, half in enumerate(halves):
        places = slots(h)
        for p in range(8):
            value = jnp.zeros((32, 256), F32)
            for t in range(8):
                value = jnp.where(places[t] == p, ans[pl.ds(32 * t, 32), half], value)
            ap[pl.ds(32 * p, 32), half], ap[pl.ds(256 + 32 * p, 32), half] = split(value)
    vv[...] = dot_nt(ap[pl.ds(0, 256), :], oh[...]) + dot_nt(ap[pl.ds(256, 256), :], oh[...])
    spread = {}
    for x in range(-1, 3):
        for y in range(-1, 3):
            sums = [None, None]
            for sx_, sy_ in ((0, 0), (0, 1), (1, 0), (1, 1)):
                vx, vy = x + 1 - sx_, y + 1 - sy_
                if 0 <= vx <= 2 and 0 <= vy <= 2:
                    for z in range(2):
                        p = sx_ * 4 + sy_ * 2 + z
                        v = vv[pl.ds(32 * p, 32), pl.ds(128 * (3 * vx + vy), 128)]
                        sums[z] = v if sums[z] is None else sums[z] + v
            spread[(x, y)] = sums[0] + pltpu.roll(sums[1], 1, 1)

    def correction_blocks(dx, dy):
        x, y = edge(dx), edge(dy)
        if dy == 0:
            return [
                spread[(x + dx, 0)], spread[(x + dx, 1)], a_half(spread[(x, 0)], x), a_half(spread[(x, 1)], x),
                b_half(spread[(x + dx, 2)], 0), b_half(spread[(x + dx, -1)], 1),
            ]
        if dx == 0:
            return [
                spread[(0, y + dy)], spread[(1, y + dy)], b_half(spread[(0, y)], y), b_half(spread[(1, y)], y),
                a_half(spread[(2, y + dy)], 0), a_half(spread[(-1, y + dy)], 1),
            ]
        return [spread[(x + dx, y + dy)], a_half(spread[(x, y + dy)], x), b_half(spread[(x + dx, y)], y)]

    third = exchange(correction_blocks, s3, r3, ssem3, rsem3)

    receive(whole)
    for f in range(4):
        x_up = jnp.concatenate([fz[f, 32:64, 256:512], rx[1, f]], axis=1)
        x_down = jnp.concatenate([rx[0, f], fz[f, 0:32, 0:256]], axis=1)
        y_up, y_down = [], []
        for x in range(2):
            y_up += [fz[f, 104:144, 256 * x + 128 : 256 * x + 256], ry[1, f, :, 128 * x : 128 * x + 128]]
            y_down += [ry[0, f, :, 128 * x : 128 * x + 128], fz[f, 64:104, 256 * x : 256 * x + 128]]
        parts = [
            x_up, x_down,
            jnp.concatenate(y_up, axis=1),
            jnp.concatenate(y_down, axis=1),
            by_column(from_next, fz[f, 176:208, :]),
            by_column(from_previous, fz[f, 144:176, :]),
            jnp.zeros((48, LANES), F32),
        ]
        around = mm3(bte_h[...], bte_l[...], jnp.concatenate(parts, axis=0))
        xhat[f] = 0.2 * xhat[f] + 0.8 * (dinv[...] * (bhat[f] + 0.5 * around))

    receive(third)
    fixed = {at: spread[at] for at in own}
    near_x = {(2, y): a_half(spread[(2, y)], 0) for y in range(2)} | {
        (-1, y): a_half(spread[(-1, y)], 1) for y in range(2)
    }
    near_y = {(x, 2): b_half(spread[(x, 2)], 0) for x in range(2)} | {
        (x, -1): b_half(spread[(x, -1)], 1) for x in range(2)
    }
    for n, (dx, dy) in enumerate(DIRS):
        x, y = edge(dx), edge(dy)
        if dy == 0:
            for t in range(2):
                fixed[(x - dx, t)] += r3[n, 32 * t : 32 * t + 32, :]
                near_x[(x - 2 * dx, t)] += r3[n, 64 + 16 * t : 80 + 16 * t, :]
            near_y[(x - dx, 2)] += r3[n, 96:112, :]
            near_y[(x - dx, -1)] += r3[n, 112:128, :]
        elif dx == 0:
            for t in range(2):
                fixed[(t, y - dy)] += r3[n, 32 * t : 32 * t + 32, :]
                near_y[(t, y - 2 * dy)] += r3[n, 64 + 16 * t : 80 + 16 * t, :]
            near_x[(2, y - dy)] += r3[n, 96:112, :]
            near_x[(-1, y - dy)] += r3[n, 112:128, :]
        else:
            fixed[(x - dx, y - dy)] += r3[n, 0:32, :]
            near_x[(x - 2 * dx, y - dy)] += r3[n, 32:48, :]
            near_y[(x - dx, y - 2 * dy)] += r3[n, 48:64, :]

    columns, rims = [], []
    for x in range(2):
        for y in range(2):
            v = fixed[(x, y)]
            columns.append(v)
            rims.append(
                jnp.concatenate(
                    [
                        a_half(fixed[(1, y)], 0) if x == 0 else near_x[(2, y)],
                        a_half(fixed[(0, y)], 1) if x == 1 else near_x[(-1, y)],
                        b_half(fixed[(x, 1)], 0) if y == 0 else near_y[(x, 2)],
                        b_half(fixed[(x, 0)], 1) if y == 1 else near_y[(x, -1)],
                        jnp.where(up_row, from_previous(v), from_next(v)),
                        jnp.zeros((32, 128), F32),
                    ],
                    axis=0,
                )
            )
    ch, cl = split(jnp.concatenate(columns, axis=1))
    stacked = jnp.concatenate([ch, cl, ch, jnp.zeros((32, LANES), BF16)], axis=0)
    rh, rl = split(jnp.concatenate(rims, axis=1))
    rims_both = jnp.concatenate([rh, rl], axis=0)
    for f in range(4):
        rows = pl.ds(128 * f, 128)
        direct = dot(tc[rows, :], stacked)
        coupled = dot(tf_h[rows, :], rims_both) + dot(tf_l[rows, :], rh)
        final = xhat[f] + 0.2 * direct + 0.4 * (dinv[...] * coupled)
        high, low = split(final)
        value = dot(bb_h[...], jnp.concatenate([high, low], axis=0)) + dot(bb_l[...], high)
        for c in range(4):
            outv[pl.ds(500 * f + c, 125, stride=4), :] = value[0:125, 128 * c : 128 * c + 128]
    for copy, dx, dy in sent:

        @pl.when(exists(dx, dy))
        def _():
            copy.wait_send()


def solution(mesh):
    nx, ny = mesh.shape["px"], mesh.shape["py"]
    table = column_table()

    def per_device(
        right_side, first_guess, coefficient, modal_basis, modal_values, patch_inverse, patch_elements, patch_mask
    ):
        hbm = pl.BlockSpec(memory_space=pltpu.HBM)

        def body(*refs):
            kernel(nx, ny, *refs)

        def f32(*shape):
            return pltpu.VMEM(shape, F32)

        def b16(*shape):
            return pltpu.VMEM(shape, BF16)

        def in_hbm(array):
            return pltpu.with_memory_space_constraint(array, pltpu.HBM)

        dma = pltpu.SemaphoreType.DMA
        out = pl.pallas_call(
            body,
            out_shape=pltpu.VMEM((2000, 128), F32),
            in_specs=[hbm] * 12,
            out_specs=pl.BlockSpec(memory_space=pltpu.VMEM),
            scratch_shapes=[
                pltpu.SMEM((5, 5), F32), pltpu.SMEM((5,), F32),
                f32(4, 125, 512), f32(4, 125, 512), f32(2, 4, 25, 512), f32(2, 4, 5, 5, 512), f32(2, 4, 25, 512),
                f32(4, 128), f32(256, 256), pltpu.VMEM((8, 512), jnp.int32), pltpu.VMEM((8, 512), jnp.int32),
                pltpu.VMEM((8, 640), jnp.int32),
                b16(128, 128), b16(128, 128), b16(128, 256), b16(128, 256), b16(128, 256), b16(128, 128),
                b16(256, 128), b16(256, 128),
                b16(64, 512), b16(192, 512),
                b16(512, 128), b16(512, 256), b16(512, 128), b16(256, 256), b16(256, 256),
                f32(4, 128, 512), f32(4, 128, 512), f32(128, 512), b16(1152, 512),
                b16(512, 512), b16(512, 512), b16(512, 512), b16(512, 512),
                b16(512, 1152), f32(256, 512), b16(256, 512), b16(256, 512), f32(256, 512), b16(512, 512),
                f32(256, 1152),
                f32(2, 4, 32, 256), f32(2, 4, 40, 256), f32(2, 4, 32, 256), f32(2, 4, 40, 256), f32(4, 256, 512),
                f32(8, 128, 128), f32(8, 128, 128), f32(8, 128, 128), f32(8, 128, 128),
                dma((20,)), dma((6,)), dma((6,)), dma((4,)), dma((4,)), dma((8,)), dma((8,)), dma((8,)), dma((8,)),
            ],
            compiler_params=pltpu.CompilerParams(
                collective_id=0, has_side_effects=True, vmem_limit_bytes=60 * 1024 * 1024
            ),
        )(
            in_hbm(first_guess.reshape(4, 125, 1, 512)),
            in_hbm(first_guess.reshape(4, 5, 25, 2, 1, 256)),
            in_hbm(first_guess.reshape(4, 5, 5, 5, 2, 2, 1, 128)),
            in_hbm(first_guess.reshape(4, 25, 5, 1, 512)),
            in_hbm(right_side.reshape(4, 125, 1, 512)),
            in_hbm(coefficient.reshape(4, 128)),
            in_hbm(modal_basis),
            in_hbm(modal_values),
            in_hbm(patch_inverse),
            in_hbm(patch_elements.T),
            in_hbm(patch_mask.T),
            in_hbm(jnp.asarray(table)),
        )
        return out.reshape(4, 5, 5, 5, 2, 2, 128)

    grid = P(None, None, None, None, "px", "py", None)
    rows = P(("px", "py"), None)
    return jax.shard_map(
        per_device,
        mesh=mesh,
        in_specs=(grid, grid, P("px", "py", None), P(), P(), P(), rows, rows),
        out_specs=grid,
        check_vma=False,
    )
```

```python
import math

import jax
import jax.numpy as jnp
import numpy as np
from jax import lax
from jax.experimental import pallas as pl
from jax.experimental.pallas import tpu as pltpu
from jax.sharding import PartitionSpec as P

MESH = pl.DeviceIdType.MESH
F32 = jnp.float32
BF16 = jnp.bfloat16
DIRS = ((1, 1), (1, -1), (-1, 1), (-1, -1), (1, 0), (-1, 0), (0, 1), (0, -1))
LANES = 512


def linear_values():
    root = np.float32(math.sqrt(3.0 / 7.0))
    points = np.array([-1.0, -root, 0.0, root, 1.0], np.float32)
    half = np.float32(0.5)
    return (1 - points) * half, (1 + points) * half


def column_table():
    table = np.full((8, 1152), 7, np.int32)
    table[3] = 9

    def put(column, i, j, k, f=9):
        table[0:4, column] = (i, j, k, f)

    for n in range(125):
        put(n, n // 25, n // 5 % 5, n % 5)
    for g in range(25):
        u, v = g // 5, g % 5
        put(128 + g, 4, u, v)
        put(160 + g, 0, u, v)
        put(192 + u * 8 + v, u, 4, v)
        put(232 + u * 8 + v, u, 0, v)
        put(272 + g, u, v, 4)
        put(304 + g, u, v, 0)
    for c in range(4):
        for g in range(25):
            u, v = g // 5, g % 5
            put(640 + 128 * c + g, 4 if c >= 2 else 0, u, v)
            put(672 + 128 * c + u * 8 + v, u, 4 if c % 2 else 0, v)
    for r in range(32):
        a, b, f, c = r // 16, r // 8 % 2, r // 2 % 4, r % 2
        for copy in range(3):
            put(384 + 32 * copy + r, 5 + a, 5 + b, 5 + c, f)
        put(512 + 64 + r, 5 + a, 5 + b, 4 if c == 0 else 0, f)
    for r in range(16):
        h, f, c = r // 8, r // 2 % 4, r % 2
        put(512 + r, 4, 5 + h, 5 + c, f)
        put(528 + r, 0, 5 + h, 5 + c, f)
        put(544 + r, 5 + h, 4, 5 + c, f)
        put(560 + r, 5 + h, 0, 5 + c, f)
    return table


def split(value):
    high = value.astype(BF16)
    return high, (value - high.astype(F32)).astype(BF16)


def dot(a, b):
    return lax.dot_general(a, b, (((1,), (0,)), ((), ())), preferred_element_type=F32)


def dot_nt(a, b):
    return lax.dot_general(a, b, (((1,), (1,)), ((), ())), preferred_element_type=F32)


def mm3(ah, al, x):
    xh, xl = split(x)
    return dot(ah, xh) + dot(ah, xl) + dot(al, xh)


def iota(shape, dim):
    return lax.broadcasted_iota(jnp.int32, shape, dim)


def a_half(v, a):
    return v[16 * a : 16 * a + 16]


def b_half(v, b):
    return jnp.concatenate([v[8 * b : 8 * b + 8], v[16 + 8 * b : 24 + 8 * b]], axis=0)


def add_a(v, a, h):
    parts = [v[0:16], v[16:32]]
    parts[a] = parts[a] + h
    return jnp.concatenate(parts, axis=0)


def add_b(v, b, h):
    parts = [v[0:8], v[8:16], v[16:24], v[24:32]]
    parts[b] = parts[b] + h[0:8]
    parts[2 + b] = parts[2 + b] + h[8:16]
    return jnp.concatenate(parts, axis=0)


def rows_to(v, rows):
    return jnp.concatenate([v, jnp.zeros((rows - v.shape[0], v.shape[1]), v.dtype)], axis=0)


def from_next(v):
    lane = iota(v.shape, 1)
    return jnp.where(lane == 127, 0.0, pltpu.roll(v, 127, 1))


def from_previous(v):
    lane = iota(v.shape, 1)
    return jnp.where(lane == 0, 0.0, pltpu.roll(v, 1, 1))


def by_column(fn, v):
    return jnp.concatenate([fn(v[:, 128 * c : 128 * c + 128]) for c in range(4)], axis=1)


def kernel(
    nx, ny,
    xa, xx, xy, xz, ba, coef_h, ub_h, mv_h, pinv_h, pe_h, pm_h, tab_h,
    outv,
    ub, mv, xin, bin_, nfx, nfy, nfz, coef, pinv, pe, pm, tab,
    bt_h, bt_l, bte_h, bte_l, bb_h, bb_l, fb_h, fb_l,
    sel_h, sel_l, zb, inn, qc, qf, tc, tf_h, tf_l, mi_h, mi_l,
    xhat, bhat, dinv, oh, xs_h, xs_l, ts_h, ts_l,
    cp, gath, wh, wl, ans, ap, vv,
    sx, sy, rx, ry, fz, s2, r2, s3, r3,
    lsem, ssem1, rsem1, ssemf, rsemf, ssem2, rsem2, ssem3, rsem3,
):
    px, py = lax.axis_index("px"), lax.axis_index("py")

    def peer(dx, dy):
        return (lax.rem(px + dx + nx, nx), lax.rem(py + dy + ny, ny))

    inside = {(1, 0): px < nx - 1, (-1, 0): px > 0, (0, 1): py < ny - 1, (0, -1): py > 0}

    def exists(dx, dy):
        if dx == 0 or dy == 0:
            return inside[(dx, dy)]
        return inside[(dx, 0)] & inside[(0, dy)]

    def unless(condition):
        return pl.when(jnp.logical_not(condition))

    local = []

    def load(src, dst):
        copy = pltpu.make_async_copy(src, dst, lsem.at[len(local)])
        copy.start()
        local.append(copy)

    load(tab_h, tab)
    load(coef_h, coef)
    load(ub_h, ub)
    load(mv_h, mv)
    load(xa.at[:, :, 0, :], xin)
    load(ba.at[:, :, 0, :], bin_)
    load(pe_h, pe)
    load(pm_h, pm)
    load(pinv_h, pinv)
    load(xx.at[:, 0, :, 1, 0, :], nfx.at[0, :, :, pl.ds(0, 256)])
    load(xx.at[:, 4, :, 0, 0, :], nfx.at[1, :, :, pl.ds(256, 256)])
    for x in range(2):
        load(xy.at[:, :, 0, :, x, 1, 0, :], nfy.at[0, :, :, :, pl.ds(256 * x, 128)])
        load(xy.at[:, :, 4, :, x, 0, 0, :], nfy.at[1, :, :, :, pl.ds(256 * x + 128, 128)])
    load(xz.at[:, :, 0, 0, :], nfz.at[0])
    load(xz.at[:, :, 4, 0, :], nfz.at[1])

    barrier = pltpu.get_barrier_semaphore()
    greeted = 0
    for dx, dy in DIRS[4:]:
        greeted = greeted + jnp.where(exists(dx, dy), 1, 0)

        @pl.when(exists(dx, dy))
        def _():
            pl.semaphore_signal(barrier, inc=1, device_id=peer(dx, dy), device_id_type=MESH)

    @unless(inside[(1, 0)])
    def _():
        nfx[0, :, :, 256:512] = jnp.zeros((4, 25, 256), F32)
        rx[1] = jnp.zeros((4, 25, 256), F32)

    @unless(inside[(-1, 0)])
    def _():
        nfx[1, :, :, 0:256] = jnp.zeros((4, 25, 256), F32)
        rx[0] = jnp.zeros((4, 25, 256), F32)

    @unless(inside[(0, 1)])
    def _():
        for x in range(2):
            nfy[0, :, :, :, 256 * x + 128 : 256 * x + 256] = jnp.zeros((4, 5, 5, 128), F32)
        ry[1] = jnp.zeros((4, 40, 256), F32)

    @unless(inside[(0, -1)])
    def _():
        for x in range(2):
            nfy[1, :, :, :, 256 * x : 256 * x + 128] = jnp.zeros((4, 5, 5, 128), F32)
        ry[0] = jnp.zeros((4, 40, 256), F32)

    for n, (dx, dy) in enumerate(DIRS):

        @unless(exists(-dx, -dy))
        def _():
            r2[n] = jnp.zeros((128, 128), F32)
            r3[n] = jnp.zeros((128, 128), F32)

    pl.semaphore_wait(barrier, greeted)

    sent = []

    def send(src, dst, ssem, rsem, dx, dy):
        copy = pltpu.make_async_remote_copy(
            src_ref=src, dst_ref=dst, send_sem=ssem, recv_sem=rsem, device_id=peer(dx, dy), device_id_type=MESH
        )

        @pl.when(exists(dx, dy))
        def _():
            copy.start()

        sent.append((copy, dx, dy))
        return sent[-1]

    def receive(copies):
        for copy, dx, dy in copies:

            @pl.when(exists(-dx, -dy))
            def _():
                copy.wait_recv()

    first = [
        send(xx.at[:, 4, :, 1, 0, :], nfx.at[1, :, :, pl.ds(0, 256)], ssem1.at[0], rsem1.at[0], 1, 0),
        send(xx.at[:, 0, :, 0, 0, :], nfx.at[0, :, :, pl.ds(256, 256)], ssem1.at[1], rsem1.at[1], -1, 0),
    ]
    for x in range(2):
        first.append(
            send(xy.at[:, :, 4, :, x, 1, 0, :], nfy.at[1, :, :, :, pl.ds(256 * x, 128)],
                 ssem1.at[2 + 2 * x], rsem1.at[2 + 2 * x], 0, 1)
        )
        first.append(
            send(xy.at[:, :, 0, :, x, 0, 0, :], nfy.at[0, :, :, :, pl.ds(256 * x + 128, 128)],
                 ssem1.at[3 + 2 * x], rsem1.at[3 + 2 * x], 0, -1)
        )

    for copy in local[0:4]:
        copy.wait()
    basis = [[ub[p, q] for q in range(5)] for p in range(5)]
    for weights in linear_values():
        basis.append([sum(float(weights[i]) * basis[i][q] for i in range(5)) for q in range(5)])
    spectrum = [mv[q] for q in range(5)]

    def mode_index(shape):
        row = iota(shape, 0)
        i = (row * 41) >> 10
        rest = row - 25 * i
        j = (rest * 13) >> 6
        return i, j, rest - 5 * j

    def block(start):
        modes = mode_index((128, 128))
        result = None
        for d in range(3):
            index = tab[d : d + 1, start : start + 128]
            hits = [index == p for p in range(7)]
            grown = jnp.zeros((128, 128), F32)
            for q in range(5):
                line = jnp.zeros((1, 128), F32)
                for p in range(7):
                    line = jnp.where(hits[p], basis[p][q], line)
                grown = jnp.where(modes[d] == q, line, grown)
            result = grown if result is None else result * grown
        return result

    nodes = block(0)
    bt_h[...], bt_l[...] = split(nodes)
    high, low = split(nodes.T)
    bb_h[...] = jnp.concatenate([high, high], axis=1)
    bb_l[...] = low
    for part in range(2):
        faces = block(128 + 128 * part)
        span = pl.ds(128 * part, 128)
        bte_h[:, span], bte_l[:, span] = split(faces)
        fb_h[span, :], fb_l[span, :] = split(faces.T)
    for c in range(4):
        high, low = split(block(640 + 128 * c))
        sel_h[c] = jnp.concatenate([high, high], axis=1)
        sel_l[c] = low
    field = tab[3:4, 384:512]
    coarse_block = block(384)
    copy_of = iota((128, 128), 1)
    for f in range(4):
        part = jnp.where(field == f, coarse_block, 0.0)
        high, low = split(part)
        tc[pl.ds(128 * f, 128), :] = jnp.where(copy_of < 64, high.astype(F32), low.astype(F32)).astype(BF16)
        high, low = split(part.T[0:32])
        qc[0:32, pl.ds(128 * f, 128)] = high
        qc[32:64, pl.ds(128 * f, 128)] = low
    field = tab[3:4, 512:640]
    face_block = block(512)
    for f in range(4):
        part = jnp.where(field == f, face_block, 0.0)
        high, low = split(part)
        tf_h[pl.ds(128 * f, 128), :] = jnp.concatenate([high, high], axis=1)
        tf_l[pl.ds(128 * f, 128), :] = low
        high, low = split(part.T[0:96])
        qf[0:96, pl.ds(128 * f, 128)] = high
        qf[96:192, pl.ds(128 * f, 128)] = low

    modes = mode_index((128, 128))
    total = jnp.zeros((128, 128), F32)
    for d in range(3):
        for q in range(5):
            total = jnp.where(modes[d] == q, total + spectrum[q], total)

    def diagonal(c):
        return total * coef[c : c + 1, :] + 1.0

    for c in range(4):
        dinv[:, pl.ds(128 * c, 128)] = 1.0 / diagonal(c)

    local[4].wait()
    local[5].wait()
    for f in range(4):
        xhat[f] = mm3(bt_h[...], bt_l[...], rows_to(xin[f], 128))
        bhat[f] = mm3(bt_h[...], bt_l[...], rows_to(bin_[f], 128))

    local[6].wait()
    local[7].wait()
    elements = pe[...]
    alive = pm[...] != 0
    at_x = (elements >> 11) - 2 * px + 1
    at_y = ((elements >> 7) & 15) - 2 * py + 1
    at_z = elements & 127

    def least(v, most):
        return jnp.minimum(jnp.min(jnp.where(alive, v, most), axis=0, keepdims=True), most)

    low_x, low_y, low_z = least(at_x, 2), least(at_y, 2), least(at_z, 126)
    key = (low_x * 3 + low_y) * 128 + low_z
    place = (at_x - low_x) * 4 + (at_y - low_y) * 2 + (at_z - low_z)
    place = jnp.where(alive, place, 99)
    vertex = iota((128, LANES), 0)
    for v in range(9):
        oh[pl.ds(128 * v, 128), :] = jnp.where(vertex + 128 * v == key, 1.0, 0.0).astype(BF16)

    local[8].wait()
    r = iota((256, 256), 0)
    source = (((r >> 1) & 3) * 8 + ((r >> 4) & 1) * 4 + ((r >> 3) & 1) * 2 + (r & 1)) * 8 + (r >> 5)
    order = jnp.where(iota((256, 256), 1) == source, 1.0, 0.0).astype(BF16)
    for piece, target in zip(split(pinv[...]), (mi_h, mi_l)):
        target[...] = dot_nt(dot(order, piece).astype(BF16), order).astype(BF16)

    for copy in local[9:]:
        copy.wait()

    none = jnp.zeros((32, 256), F32)
    gap = jnp.zeros((8, 128), F32)
    for f in range(4):
        parts = [
            jnp.concatenate([rows_to(nfx[0, f, :, 0:256], 32), none], axis=1),
            jnp.concatenate([none, rows_to(nfx[1, f, :, 256:512], 32)], axis=1),
        ]
        for i in range(5):
            near = [rows_to(nfy[0, f, i, :, 256 * x : 256 * x + 128], 8) for x in range(2)]
            parts.append(jnp.concatenate([near[0], gap, near[1], gap], axis=1))
        for i in range(5):
            near = [rows_to(nfy[1, f, i, :, 256 * x + 128 : 256 * x + 256], 8) for x in range(2)]
            parts.append(jnp.concatenate([gap, near[0], gap, near[1]], axis=1))
        parts.append(by_column(from_next, rows_to(nfz[0, f], 32)))
        parts.append(by_column(from_previous, rows_to(nfz[1, f], 32)))
        parts.append(jnp.zeros((48, LANES), F32))
        around = mm3(bte_h[...], bte_l[...], jnp.concatenate(parts, axis=0))
        x0 = xhat[f]
        zb[f] = 0.4 * (dinv[...] * (bhat[f] + 0.5 * around)) - 0.3 * x0
        diag = jnp.concatenate([diagonal(c) for c in range(4)], axis=1)
        rows = pl.ds(128 * f, 128)
        ts_h[rows, :], ts_l[rows, :] = split(bhat[f] - diag * x0)
    both = dot(qc[...], ts_h[...])
    inn[...] = 0.2 * (both[0:32] + both[32:64] + dot(qc[0:32, :], ts_l[...]))

    receive(first)

    for c in range(4):
        x, y = c // 2, c % 2
        lanes = slice(128 * c, 128 * c + 128)
        columns = []
        for f in range(4):
            parts = [rows_to(nfx[1 - x, f, :, lanes], 32)]
            parts += [rows_to(nfy[1 - y, f, i, :, lanes], 8) for i in range(5)]
            parts.append(jnp.zeros((56, 128), F32))
            columns.append(jnp.concatenate(parts, axis=0))
        high, low = split(jnp.concatenate(columns, axis=1))
        around = dot(sel_h[c], jnp.concatenate([high, low], axis=0)) + dot(sel_l[c], high)
        for f in range(4):
            z = zb[f, :, lanes] + 0.2 * (dinv[:, lanes] * around[:, 128 * f : 128 * f + 128])
            zb[f, :, lanes] = z
            rows = pl.ds(128 * f, 128)
            xs_h[rows, lanes], xs_l[rows, lanes] = split(z)

    inner = inn[...]
    both = dot(qf[...], xs_h[...])
    rim = both[0:96] + both[96:192] + dot(qf[0:96, :], xs_l[...])
    up_row = ((iota((32, 128), 0) & 1) == 1)

    def rim_of(start, size, c):
        return rim[start : start + size, 128 * c : 128 * c + 128]

    own = {}
    for x in range(2):
        for y in range(2):
            c = 2 * x + y
            v = inner[:, 128 * c : 128 * c + 128]
            faces = rim_of(64, 32, c)
            v = v + jnp.where(up_row, from_next(faces), from_previous(faces))
            v = add_a(v, 0, rim_of(0, 16, y)) if x == 1 else add_a(v, 1, rim_of(16, 16, 2 + y))
            v = add_b(v, 0, rim_of(32, 16, 2 * x)) if y == 1 else add_b(v, 1, rim_of(48, 16, 2 * x + 1))
            own[(x, y)] = v
    hx = {(1, y): rim_of(0, 16, 2 + y) for y in range(2)} | {(-1, y): rim_of(16, 16, y) for y in range(2)}
    hy = {(1, x): rim_of(32, 16, 2 * x + 1) for x in range(2)} | {(-1, x): rim_of(48, 16, 2 * x) for x in range(2)}

    def edge(d):
        return 1 if d == 1 else 0

    def exchange(blocks, sbuf, rbuf, ssem, rsem):
        copies = []
        for n, (dx, dy) in enumerate(DIRS):
            at = 0
            for v in blocks(dx, dy):
                sbuf[n, pl.ds(at, v.shape[0]), :] = v
                at += v.shape[0]
            copies.append(
                send(sbuf.at[n, pl.ds(0, at)], rbuf.at[n, pl.ds(0, at)], ssem.at[n], rsem.at[n], dx, dy)
            )
        return copies

    def residual_blocks(dx, dy):
        x, y = edge(dx), edge(dy)
        if dy == 0:
            return [own[(x, 0)], own[(x, 1)], hx[(dx, 0)], hx[(dx, 1)], hy[(1, x)], hy[(-1, x)]]
        if dx == 0:
            return [own[(0, y)], own[(1, y)], hy[(dy, 0)], hy[(dy, 1)], hx[(1, y)], hx[(-1, y)]]
        return [own[(x, y)], hx[(dx, y)], hy[(dy, x)]]

    second = exchange(residual_blocks, s2, r2, ssem2, rsem2)

    for f in range(4):
        rows = pl.ds(128 * f, 128)
        x1 = 2.0 * zb[f] + 0.8 * xhat[f]
        xhat[f] = x1
        xs_h[rows, :], xs_l[rows, :] = split(x1)
        for part in range(2):
            span = pl.ds(128 * part, 128)
            faces = (
                dot(fb_h[span, :], xs_h[rows, :])
                + dot(fb_h[span, :], xs_l[rows, :])
                + dot(fb_l[span, :], xs_h[rows, :])
            )
            fz[f, span, :] = faces
        sx[0, f] = fz[f, 0:25, 256:512]
        sx[1, f] = fz[f, 32:57, 0:256]
        for x in range(2):
            sy[0, f, :, pl.ds(128 * x, 128)] = fz[f, 64:104, 256 * x + 128 : 256 * x + 256]
            sy[1, f, :, pl.ds(128 * x, 128)] = fz[f, 104:144, 256 * x : 256 * x + 128]
    receive(second[6:])
    whole = [
        send(sx.at[0], rx.at[0], ssemf.at[0], rsemf.at[0], 1, 0),
        send(sx.at[1], rx.at[1], ssemf.at[1], rsemf.at[1], -1, 0),
        send(sy.at[0], ry.at[0], ssemf.at[2], rsemf.at[2], 0, 1),
        send(sy.at[1], ry.at[1], ssemf.at[3], rsemf.at[3], 0, -1),
    ]
    receive(second[:6])
    field_of = {}

    def put(at, v):
        field_of[at] = field_of[at] + v if at in field_of else v

    for at, v in own.items():
        put(at, v)
    late = []
    for y in range(2):
        late += [("a", 0, (2, y), hx[(1, y)]), ("a", 1, (-1, y), hx[(-1, y)])]
        late += [("b", 0, (y, 2), hy[(1, y)]), ("b", 1, (y, -1), hy[(-1, y)])]
    for n, (dx, dy) in enumerate(DIRS):
        x, y = edge(dx), edge(dy)
        side_a, side_b = (0 if dx == 1 else 1), (0 if dy == 1 else 1)
        if dy == 0:
            for t in range(2):
                put((x - 2 * dx, t), r2[n, 32 * t : 32 * t + 32, :])
                late.append(("a", side_a, (x - dx, t), r2[n, 64 + 16 * t : 80 + 16 * t, :]))
            late.append(("b", 0, (x - 2 * dx, 2), r2[n, 96:112, :]))
            late.append(("b", 1, (x - 2 * dx, -1), r2[n, 112:128, :]))
        elif dx == 0:
            for t in range(2):
                put((t, y - 2 * dy), r2[n, 32 * t : 32 * t + 32, :])
                late.append(("b", side_b, (t, y - dy), r2[n, 64 + 16 * t : 80 + 16 * t, :]))
            late.append(("a", 0, (2, y - 2 * dy), r2[n, 96:112, :]))
            late.append(("a", 1, (-1, y - 2 * dy), r2[n, 112:128, :]))
        else:
            put((x - 2 * dx, y - 2 * dy), r2[n, 0:32, :])
            late.append(("a", side_a, (x - dx, y - 2 * dy), r2[n, 32:48, :]))
            late.append(("b", side_b, (x - 2 * dx, y - dy), r2[n, 48:64, :]))
    for kind, side, at, v in late:
        field_of[at] = add_a(field_of[at], side, v) if kind == "a" else add_b(field_of[at], side, v)

    for (x, y), v in field_of.items():
        moved = pltpu.roll(v, 127, 1)
        for z, value in enumerate((v, moved)):
            pieces = split(value)
            for sx_, sy_ in ((0, 0), (0, 1), (1, 0), (1, 1)):
                vx, vy = x + 1 - sx_, y + 1 - sy_
                if 0 <= vx <= 2 and 0 <= vy <= 2:
                    p = sx_ * 4 + sy_ * 2 + z
                    for t in range(2):
                        cp[pl.ds(256 * t + 32 * p, 32), pl.ds(128 * (3 * vx + vy), 128)] = pieces[t]
    halves = [pl.ds(256 * h, 256) for h in range(2)]

    def slots(h):
        return [jnp.broadcast_to(place[t : t + 1, 256 * h : 256 * h + 256], (32, 256)) for t in range(8)]

    for half in halves:
        gath[:, half] = dot(cp[pl.ds(0, 256), :], oh[:, half]) + dot(cp[pl.ds(256, 256), :], oh[:, half])
    for h, half in enumerate(halves):
        for t, slot in enumerate(slots(h)):
            value = jnp.zeros((32, 256), F32)
            for p in range(8):
                value = jnp.where(slot == p, gath[pl.ds(32 * p, 32), half], value)
            rows = pl.ds(32 * t, 32)
            wh[rows, half], wl[rows, half] = split(value)
        ans[:, half] = dot(mi_h[...], wh[:, half]) + dot(mi_h[...], wl[:, half]) + dot(mi_l[...], wh[:, half])
    for h, half in enumerate(halves):
        places = slots(h)
        for p in range(8):
            value = jnp.zeros((32, 256), F32)
            for t in range(8):
                value = jnp.where(places[t] == p, ans[pl.ds(32 * t, 32), half], value)
            ap[pl.ds(32 * p, 32), half], ap[pl.ds(256 + 32 * p, 32), half] = split(value)
    vv[...] = dot_nt(ap[pl.ds(0, 256), :], oh[...]) + dot_nt(ap[pl.ds(256, 256), :], oh[...])
    spread = {}
    for x in range(-1, 3):
        for y in range(-1, 3):
            sums = [None, None]
            for sx_, sy_ in ((0, 0), (0, 1), (1, 0), (1, 1)):
                vx, vy = x + 1 - sx_, y + 1 - sy_
                if 0 <= vx <= 2 and 0 <= vy <= 2:
                    for z in range(2):
                        p = sx_ * 4 + sy_ * 2 + z
                        v = vv[pl.ds(32 * p, 32), pl.ds(128 * (3 * vx + vy), 128)]
                        sums[z] = v if sums[z] is None else sums[z] + v
            spread[(x, y)] = sums[0] + pltpu.roll(sums[1], 1, 1)

    def correction_blocks(dx, dy):
        x, y = edge(dx), edge(dy)
        if dy == 0:
            return [
                spread[(x + dx, 0)], spread[(x + dx, 1)], a_half(spread[(x, 0)], x), a_half(spread[(x, 1)], x),
                b_half(spread[(x + dx, 2)], 0), b_half(spread[(x + dx, -1)], 1),
            ]
        if dx == 0:
            return [
                spread[(0, y + dy)], spread[(1, y + dy)], b_half(spread[(0, y)], y), b_half(spread[(1, y)], y),
                a_half(spread[(2, y + dy)], 0), a_half(spread[(-1, y + dy)], 1),
            ]
        return [spread[(x + dx, y + dy)], a_half(spread[(x, y + dy)], x), b_half(spread[(x + dx, y)], y)]

    third = exchange(correction_blocks, s3, r3, ssem3, rsem3)

    receive(whole)
    for f in range(4):
        x_up = jnp.concatenate([fz[f, 32:64, 256:512], rows_to(rx[1, f], 32)], axis=1)
        x_down = jnp.concatenate([rows_to(rx[0, f], 32), fz[f, 0:32, 0:256]], axis=1)
        y_up, y_down = [], []
        for x in range(2):
            y_up += [fz[f, 104:144, 256 * x + 128 : 256 * x + 256], ry[1, f, :, 128 * x : 128 * x + 128]]
            y_down += [ry[0, f, :, 128 * x : 128 * x + 128], fz[f, 64:104, 256 * x : 256 * x + 128]]
        parts = [
            x_up, x_down,
            jnp.concatenate(y_up, axis=1),
            jnp.concatenate(y_down, axis=1),
            by_column(from_next, fz[f, 176:208, :]),
            by_column(from_previous, fz[f, 144:176, :]),
            jnp.zeros((48, LANES), F32),
        ]
        around = mm3(bte_h[...], bte_l[...], jnp.concatenate(parts, axis=0))
        xhat[f] = 0.2 * xhat[f] + 0.8 * (dinv[...] * (bhat[f] + 0.5 * around))

    receive(third)
    fixed = {at: spread[at] for at in own}
    near_x = {(2, y): a_half(spread[(2, y)], 0) for y in range(2)} | {
        (-1, y): a_half(spread[(-1, y)], 1) for y in range(2)
    }
    near_y = {(x, 2): b_half(spread[(x, 2)], 0) for x in range(2)} | {
        (x, -1): b_half(spread[(x, -1)], 1) for x in range(2)
    }
    for n, (dx, dy) in enumerate(DIRS):
        x, y = edge(dx), edge(dy)
        if dy == 0:
            for t in range(2):
                fixed[(x - dx, t)] += r3[n, 32 * t : 32 * t + 32, :]
                near_x[(x - 2 * dx, t)] += r3[n, 64 + 16 * t : 80 + 16 * t, :]
            near_y[(x - dx, 2)] += r3[n, 96:112, :]
            near_y[(x - dx, -1)] += r3[n, 112:128, :]
        elif dx == 0:
            for t in range(2):
                fixed[(t, y - dy)] += r3[n, 32 * t : 32 * t + 32, :]
                near_y[(t, y - 2 * dy)] += r3[n, 64 + 16 * t : 80 + 16 * t, :]
            near_x[(2, y - dy)] += r3[n, 96:112, :]
            near_x[(-1, y - dy)] += r3[n, 112:128, :]
        else:
            fixed[(x - dx, y - dy)] += r3[n, 0:32, :]
            near_x[(x - 2 * dx, y - dy)] += r3[n, 32:48, :]
            near_y[(x - dx, y - 2 * dy)] += r3[n, 48:64, :]

    columns, rims = [], []
    for x in range(2):
        for y in range(2):
            v = fixed[(x, y)]
            columns.append(v)
            rims.append(
                jnp.concatenate(
                    [
                        a_half(fixed[(1, y)], 0) if x == 0 else near_x[(2, y)],
                        a_half(fixed[(0, y)], 1) if x == 1 else near_x[(-1, y)],
                        b_half(fixed[(x, 1)], 0) if y == 0 else near_y[(x, 2)],
                        b_half(fixed[(x, 0)], 1) if y == 1 else near_y[(x, -1)],
                        jnp.where(up_row, from_previous(v), from_next(v)),
                        jnp.zeros((32, 128), F32),
                    ],
                    axis=0,
                )
            )
    ch, cl = split(jnp.concatenate(columns, axis=1))
    stacked = jnp.concatenate([ch, cl, ch, jnp.zeros((32, LANES), BF16)], axis=0)
    rh, rl = split(jnp.concatenate(rims, axis=1))
    rims_both = jnp.concatenate([rh, rl], axis=0)
    for f in range(4):
        rows = pl.ds(128 * f, 128)
        direct = dot(tc[rows, :], stacked)
        coupled = dot(tf_h[rows, :], rims_both) + dot(tf_l[rows, :], rh)
        final = xhat[f] + 0.2 * direct + 0.4 * (dinv[...] * coupled)
        high, low = split(final)
        value = dot(bb_h[...], jnp.concatenate([high, low], axis=0)) + dot(bb_l[...], high)
        for c in range(4):
            outv[pl.ds(500 * f + c, 125, stride=4), :] = value[0:125, 128 * c : 128 * c + 128]
    for copy, dx, dy in sent:

        @pl.when(exists(dx, dy))
        def _():
            copy.wait_send()


def solution(mesh):
    nx, ny = mesh.shape["px"], mesh.shape["py"]
    table = column_table()

    def per_device(
        right_side, first_guess, coefficient, modal_basis, modal_values, patch_inverse, patch_elements, patch_mask
    ):
        hbm = pl.BlockSpec(memory_space=pltpu.HBM)

        def body(*refs):
            kernel(nx, ny, *refs)

        def f32(*shape):
            return pltpu.VMEM(shape, F32)

        def b16(*shape):
            return pltpu.VMEM(shape, BF16)

        def in_hbm(array):
            return pltpu.with_memory_space_constraint(array, pltpu.HBM)

        dma = pltpu.SemaphoreType.DMA
        out = pl.pallas_call(
            body,
            out_shape=pltpu.VMEM((2000, 128), F32),
            in_specs=[hbm] * 12,
            out_specs=pl.BlockSpec(memory_space=pltpu.VMEM),
            scratch_shapes=[
                pltpu.SMEM((5, 5), F32), pltpu.SMEM((5,), F32),
                f32(4, 125, 512), f32(4, 125, 512), f32(2, 4, 25, 512), f32(2, 4, 5, 5, 512), f32(2, 4, 25, 512),
                f32(4, 128), f32(256, 256), pltpu.VMEM((8, 512), jnp.int32), pltpu.VMEM((8, 512), jnp.int32),
                pltpu.VMEM((8, 1152), jnp.int32),
                b16(128, 128), b16(128, 128), b16(128, 256), b16(128, 256), b16(128, 256), b16(128, 128),
                b16(256, 128), b16(256, 128),
                b16(4, 128, 256), b16(4, 128, 128), f32(4, 128, 512), f32(32, 512), b16(64, 512), b16(192, 512),
                b16(512, 128), b16(512, 256), b16(512, 128), b16(256, 256), b16(256, 256),
                f32(4, 128, 512), f32(4, 128, 512), f32(128, 512), b16(1152, 512),
                b16(512, 512), b16(512, 512), b16(512, 512), b16(512, 512),
                b16(512, 1152), f32(256, 512), b16(256, 512), b16(256, 512), f32(256, 512), b16(512, 512),
                f32(256, 1152),
                f32(2, 4, 25, 256), f32(2, 4, 40, 256), f32(2, 4, 25, 256), f32(2, 4, 40, 256), f32(4, 256, 512),
                f32(8, 128, 128), f32(8, 128, 128), f32(8, 128, 128), f32(8, 128, 128),
                dma((20,)), dma((6,)), dma((6,)), dma((4,)), dma((4,)), dma((8,)), dma((8,)), dma((8,)), dma((8,)),
            ],
            compiler_params=pltpu.CompilerParams(
                collective_id=0, has_side_effects=True, vmem_limit_bytes=60 * 1024 * 1024
            ),
        )(
            in_hbm(first_guess.reshape(4, 125, 1, 512)),
            in_hbm(first_guess.reshape(4, 5, 25, 2, 1, 256)),
            in_hbm(first_guess.reshape(4, 5, 5, 5, 2, 2, 1, 128)),
            in_hbm(first_guess.reshape(4, 25, 5, 1, 512)),
            in_hbm(right_side.reshape(4, 125, 1, 512)),
            in_hbm(coefficient.reshape(4, 128)),
            in_hbm(modal_basis),
            in_hbm(modal_values),
            in_hbm(patch_inverse),
            in_hbm(patch_elements.T),
            in_hbm(patch_mask.T),
            in_hbm(jnp.asarray(table)),
        )
        return out.reshape(4, 5, 5, 5, 2, 2, 128)

    grid = P(None, None, None, None, "px", "py", None)
    rows = P(("px", "py"), None)
    return jax.shard_map(
        per_device,
        mesh=mesh,
        in_specs=(grid, grid, P("px", "py", None), P(), P(), P(), rows, rows),
        out_specs=grid,
        check_vma=False,
    )
```

```python
import math

import jax
import jax.numpy as jnp
import numpy as np
from jax import lax
from jax.experimental import pallas as pl
from jax.experimental.pallas import tpu as pltpu
from jax.sharding import PartitionSpec as P

MESH = pl.DeviceIdType.MESH
F32 = jnp.float32
BF16 = jnp.bfloat16
DIRS = ((1, 1), (1, -1), (-1, 1), (-1, -1), (1, 0), (-1, 0), (0, 1), (0, -1))
LANES = 512


def linear_values():
    root = np.float32(math.sqrt(3.0 / 7.0))
    points = np.array([-1.0, -root, 0.0, root, 1.0], np.float32)
    half = np.float32(0.5)
    return (1 - points) * half, (1 + points) * half


def column_table():
    table = np.full((8, 1152), 7, np.int32)
    table[3] = 9

    def put(column, i, j, k, f=9):
        table[0:4, column] = (i, j, k, f)

    for n in range(125):
        put(n, n // 25, n // 5 % 5, n % 5)
    for g in range(25):
        u, v = g // 5, g % 5
        put(128 + g, 4, u, v)
        put(160 + g, 0, u, v)
        put(192 + u * 8 + v, u, 4, v)
        put(232 + u * 8 + v, u, 0, v)
        put(272 + g, u, v, 4)
        put(304 + g, u, v, 0)
    for c in range(4):
        for g in range(25):
            u, v = g // 5, g % 5
            put(640 + 128 * c + g, 4 if c >= 2 else 0, u, v)
            put(672 + 128 * c + u * 8 + v, u, 4 if c % 2 else 0, v)
    for r in range(32):
        a, b, f, c = r // 16, r // 8 % 2, r // 2 % 4, r % 2
        for copy in range(3):
            put(384 + 32 * copy + r, 5 + a, 5 + b, 5 + c, f)
        put(512 + 64 + r, 5 + a, 5 + b, 4 if c == 0 else 0, f)
    for r in range(16):
        h, f, c = r // 8, r // 2 % 4, r % 2
        put(512 + r, 4, 5 + h, 5 + c, f)
        put(528 + r, 0, 5 + h, 5 + c, f)
        put(544 + r, 5 + h, 4, 5 + c, f)
        put(560 + r, 5 + h, 0, 5 + c, f)
    return table


def split(value):
    high = value.astype(BF16)
    return high, (value - high.astype(F32)).astype(BF16)


def dot(a, b):
    return lax.dot_general(a, b, (((1,), (0,)), ((), ())), preferred_element_type=F32)


def dot_nt(a, b):
    return lax.dot_general(a, b, (((1,), (1,)), ((), ())), preferred_element_type=F32)


def mm3(ah, al, x):
    xh, xl = split(x)
    return dot(ah, xh) + dot(ah, xl) + dot(al, xh)


def iota(shape, dim):
    return lax.broadcasted_iota(jnp.int32, shape, dim)


def a_half(v, a):
    return v[16 * a : 16 * a + 16]


def b_half(v, b):
    return jnp.concatenate([v[8 * b : 8 * b + 8], v[16 + 8 * b : 24 + 8 * b]], axis=0)


def add_a(v, a, h):
    parts = [v[0:16], v[16:32]]
    parts[a] = parts[a] + h
    return jnp.concatenate(parts, axis=0)


def add_b(v, b, h):
    parts = [v[0:8], v[8:16], v[16:24], v[24:32]]
    parts[b] = parts[b] + h[0:8]
    parts[2 + b] = parts[2 + b] + h[8:16]
    return jnp.concatenate(parts, axis=0)


def rows_to(v, rows):
    return jnp.concatenate([v, jnp.zeros((rows - v.shape[0], v.shape[1]), v.dtype)], axis=0)


def from_next(v):
    lane = iota(v.shape, 1)
    return jnp.where(lane == 127, 0.0, pltpu.roll(v, 127, 1))


def from_previous(v):
    lane = iota(v.shape, 1)
    return jnp.where(lane == 0, 0.0, pltpu.roll(v, 1, 1))


def by_column(fn, v):
    return jnp.concatenate([fn(v[:, 128 * c : 128 * c + 128]) for c in range(4)], axis=1)


def kernel(
    nx, ny,
    xa, xx, xy, xz, ba, coef_h, ub_h, mv_h, pinv_h, pe_h, pm_h, tab_h,
    outv,
    ub, mv, xin, bin_, nfx, nfy, nfz, coef, pinv, pe, pm, tab,
    bt_h, bt_l, bte_h, bte_l, bb_h, bb_l, fb_h, fb_l,
    sel_h, sel_l, zb, inn, qc, qf, tc, tf_h, tf_l, mi_h, mi_l,
    xhat, bhat, dinv, oh, xs_h, xs_l, ts_h, ts_l,
    cz, zz, gz, wf, ans, ap, vv,
    sx, sy, rx, ry, fz, s2, r2, s3, r3,
    lsem, ssem1, rsem1, ssemf, rsemf, ssem2, rsem2, ssem3, rsem3,
):
    px, py = lax.axis_index("px"), lax.axis_index("py")

    def peer(dx, dy):
        return (lax.rem(px + dx + nx, nx), lax.rem(py + dy + ny, ny))

    inside = {(1, 0): px < nx - 1, (-1, 0): px > 0, (0, 1): py < ny - 1, (0, -1): py > 0}

    def exists(dx, dy):
        if dx == 0 or dy == 0:
            return inside[(dx, dy)]
        return inside[(dx, 0)] & inside[(0, dy)]

    def unless(condition):
        return pl.when(jnp.logical_not(condition))

    barrier = pltpu.get_barrier_semaphore()
    greeted = 0
    for dx, dy in DIRS[4:]:
        greeted = greeted + jnp.where(exists(dx, dy), 1, 0)

        @pl.when(exists(dx, dy))
        def _():
            pl.semaphore_signal(barrier, inc=1, device_id=peer(dx, dy), device_id_type=MESH)

    local = []

    def load(src, dst):
        copy = pltpu.make_async_copy(src, dst, lsem.at[len(local)])
        copy.start()
        local.append(copy)

    load(tab_h, tab)
    load(coef_h, coef)
    load(ub_h, ub)
    load(mv_h, mv)
    load(xa.at[:, :, 0, :], xin)
    load(ba.at[:, :, 0, :], bin_)
    load(pe_h, pe)
    load(pm_h, pm)
    load(pinv_h, pinv)
    load(xx.at[:, 0, :, 1, 0, :], nfx.at[0, :, :, pl.ds(0, 256)])
    load(xx.at[:, 4, :, 0, 0, :], nfx.at[1, :, :, pl.ds(256, 256)])
    for x in range(2):
        load(xy.at[:, :, 0, :, x, 1, 0, :], nfy.at[0, :, :, :, pl.ds(256 * x, 128)])
        load(xy.at[:, :, 4, :, x, 0, 0, :], nfy.at[1, :, :, :, pl.ds(256 * x + 128, 128)])
    load(xz.at[:, :, 0, 0, :], nfz.at[0])
    load(xz.at[:, :, 4, 0, :], nfz.at[1])

    @unless(inside[(1, 0)])
    def _():
        nfx[0, :, :, 256:512] = jnp.zeros((4, 25, 256), F32)
        rx[1] = jnp.zeros((4, 25, 256), F32)

    @unless(inside[(-1, 0)])
    def _():
        nfx[1, :, :, 0:256] = jnp.zeros((4, 25, 256), F32)
        rx[0] = jnp.zeros((4, 25, 256), F32)

    @unless(inside[(0, 1)])
    def _():
        for x in range(2):
            nfy[0, :, :, :, 256 * x + 128 : 256 * x + 256] = jnp.zeros((4, 5, 5, 128), F32)
        ry[1] = jnp.zeros((4, 40, 256), F32)

    @unless(inside[(0, -1)])
    def _():
        for x in range(2):
            nfy[1, :, :, :, 256 * x : 256 * x + 128] = jnp.zeros((4, 5, 5, 128), F32)
        ry[0] = jnp.zeros((4, 40, 256), F32)

    for n, (dx, dy) in enumerate(DIRS):

        @unless(exists(-dx, -dy))
        def _():
            r2[n] = jnp.zeros((128, 128), F32)
            r3[n] = jnp.zeros((128, 128), F32)

    pl.semaphore_wait(barrier, greeted)

    sent = []

    def send(src, dst, ssem, rsem, dx, dy):
        copy = pltpu.make_async_remote_copy(
            src_ref=src, dst_ref=dst, send_sem=ssem, recv_sem=rsem, device_id=peer(dx, dy), device_id_type=MESH
        )

        @pl.when(exists(dx, dy))
        def _():
            copy.start()

        sent.append((copy, dx, dy))
        return sent[-1]

    def receive(copies):
        for copy, dx, dy in copies:

            @pl.when(exists(-dx, -dy))
            def _():
                copy.wait_recv()

    first = [
        send(xx.at[:, 4, :, 1, 0, :], nfx.at[1, :, :, pl.ds(0, 256)], ssem1.at[0], rsem1.at[0], 1, 0),
        send(xx.at[:, 0, :, 0, 0, :], nfx.at[0, :, :, pl.ds(256, 256)], ssem1.at[1], rsem1.at[1], -1, 0),
    ]
    for x in range(2):
        first.append(
            send(xy.at[:, :, 4, :, x, 1, 0, :], nfy.at[1, :, :, :, pl.ds(256 * x, 128)],
                 ssem1.at[2 + 2 * x], rsem1.at[2 + 2 * x], 0, 1)
        )
        first.append(
            send(xy.at[:, :, 0, :, x, 0, 0, :], nfy.at[0, :, :, :, pl.ds(256 * x + 128, 128)],
                 ssem1.at[3 + 2 * x], rsem1.at[3 + 2 * x], 0, -1)
        )

    for copy in local[0:4]:
        copy.wait()
    basis = [[ub[p, q] for q in range(5)] for p in range(5)]
    for weights in linear_values():
        basis.append([sum(float(weights[i]) * basis[i][q] for i in range(5)) for q in range(5)])
    spectrum = [mv[q] for q in range(5)]

    def mode_index(shape):
        row = iota(shape, 0)
        i = (row * 41) >> 10
        rest = row - 25 * i
        j = (rest * 13) >> 6
        return i, j, rest - 5 * j

    def block(start):
        modes = mode_index((128, 128))
        result = None
        for d in range(3):
            index = tab[d : d + 1, start : start + 128]
            hits = [index == p for p in range(7)]
            grown = jnp.zeros((128, 128), F32)
            for q in range(5):
                line = jnp.zeros((1, 128), F32)
                for p in range(7):
                    line = jnp.where(hits[p], basis[p][q], line)
                grown = jnp.where(modes[d] == q, line, grown)
            result = grown if result is None else result * grown
        return result

    nodes = block(0)
    bt_h[...], bt_l[...] = split(nodes)
    high, low = split(nodes.T)
    bb_h[...] = jnp.concatenate([high, high], axis=1)
    bb_l[...] = low
    for part in range(2):
        faces = block(128 + 128 * part)
        span = pl.ds(128 * part, 128)
        bte_h[:, span], bte_l[:, span] = split(faces)
        fb_h[span, :], fb_l[span, :] = split(faces.T)
    for c in range(4):
        high, low = split(block(640 + 128 * c))
        sel_h[c] = jnp.concatenate([high, high], axis=1)
        sel_l[c] = low
    field = tab[3:4, 384:512]
    coarse_block = block(384)
    copy_of = iota((128, 128), 1)
    for f in range(4):
        part = jnp.where(field == f, coarse_block, 0.0)
        high, low = split(part)
        tc[pl.ds(128 * f, 128), :] = jnp.where(copy_of < 64, high.astype(F32), low.astype(F32)).astype(BF16)
        high, low = split(part.T[0:32])
        qc[0:32, pl.ds(128 * f, 128)] = high
        qc[32:64, pl.ds(128 * f, 128)] = low
    field = tab[3:4, 512:640]
    face_block = block(512)
    for f in range(4):
        part = jnp.where(field == f, face_block, 0.0)
        high, low = split(part)
        tf_h[pl.ds(128 * f, 128), :] = jnp.concatenate([high, high], axis=1)
        tf_l[pl.ds(128 * f, 128), :] = low
        high, low = split(part.T[0:96])
        qf[0:96, pl.ds(128 * f, 128)] = high
        qf[96:192, pl.ds(128 * f, 128)] = low

    modes = mode_index((128, 128))
    total = jnp.zeros((128, 128), F32)
    for d in range(3):
        for q in range(5):
            total = jnp.where(modes[d] == q, total + spectrum[q], total)

    def diagonal(c):
        return total * coef[c : c + 1, :] + 1.0

    for c in range(4):
        dinv[:, pl.ds(128 * c, 128)] = 1.0 / diagonal(c)

    local[4].wait()
    local[5].wait()
    for f in range(4):
        xhat[f] = mm3(bt_h[...], bt_l[...], rows_to(xin[f], 128))
        bhat[f] = mm3(bt_h[...], bt_l[...], rows_to(bin_[f], 128))

    local[6].wait()
    local[7].wait()
    elements = pe[...]
    alive = pm[...] != 0
    at_x = (elements >> 11) - 2 * px + 1
    at_y = ((elements >> 7) & 15) - 2 * py + 1
    at_z = elements & 127

    def least(v, most):
        return jnp.minimum(jnp.min(jnp.where(alive, v, most), axis=0, keepdims=True), most)

    low_x, low_y, low_z = least(at_x, 2), least(at_y, 2), least(at_z, 126)
    key = (low_x * 3 + low_y) * 128 + low_z
    place = (at_x - low_x) * 4 + (at_y - low_y) * 2 + (at_z - low_z)
    place = jnp.where(alive, place, 99)
    vertex = iota((128, LANES), 0)
    lowest = jnp.where(vertex == low_z, 1.0, 0.0).astype(BF16)
    zz[0:128, :] = lowest
    zz[128:256, :] = lowest
    for v in range(9):
        oh[pl.ds(128 * v, 128), :] = jnp.where(vertex + 128 * v == key, 1.0, 0.0).astype(BF16)

    local[8].wait()
    r = iota((256, 256), 0)
    source = (((r >> 1) & 3) * 8 + ((r >> 4) & 1) * 4 + ((r >> 3) & 1) * 2 + (r & 1)) * 8 + (r >> 5)
    order = jnp.where(iota((256, 256), 1) == source, 1.0, 0.0).astype(BF16)
    for piece, target in zip(split(pinv[...]), (mi_h, mi_l)):
        target[...] = dot_nt(dot(order, piece).astype(BF16), order).astype(BF16)

    for copy in local[9:]:
        copy.wait()

    none = jnp.zeros((32, 256), F32)
    gap = jnp.zeros((8, 128), F32)
    for f in range(4):
        parts = [
            jnp.concatenate([rows_to(nfx[0, f, :, 0:256], 32), none], axis=1),
            jnp.concatenate([none, rows_to(nfx[1, f, :, 256:512], 32)], axis=1),
        ]
        for i in range(5):
            near = [rows_to(nfy[0, f, i, :, 256 * x : 256 * x + 128], 8) for x in range(2)]
            parts.append(jnp.concatenate([near[0], gap, near[1], gap], axis=1))
        for i in range(5):
            near = [rows_to(nfy[1, f, i, :, 256 * x + 128 : 256 * x + 256], 8) for x in range(2)]
            parts.append(jnp.concatenate([gap, near[0], gap, near[1]], axis=1))
        parts.append(by_column(from_next, rows_to(nfz[0, f], 32)))
        parts.append(by_column(from_previous, rows_to(nfz[1, f], 32)))
        parts.append(jnp.zeros((48, LANES), F32))
        around = mm3(bte_h[...], bte_l[...], jnp.concatenate(parts, axis=0))
        x0 = xhat[f]
        zb[f] = 0.4 * (dinv[...] * (bhat[f] + 0.5 * around)) - 0.3 * x0
        diag = jnp.concatenate([diagonal(c) for c in range(4)], axis=1)
        rows = pl.ds(128 * f, 128)
        ts_h[rows, :], ts_l[rows, :] = split(bhat[f] - diag * x0)
    both = dot(qc[...], ts_h[...])
    inn[...] = 0.2 * (both[0:32] + both[32:64] + dot(qc[0:32, :], ts_l[...]))

    receive(first)

    for c in range(4):
        x, y = c // 2, c % 2
        lanes = slice(128 * c, 128 * c + 128)
        columns = []
        for f in range(4):
            parts = [rows_to(nfx[1 - x, f, :, lanes], 32)]
            parts += [rows_to(nfy[1 - y, f, i, :, lanes], 8) for i in range(5)]
            parts.append(jnp.zeros((56, 128), F32))
            columns.append(jnp.concatenate(parts, axis=0))
        high, low = split(jnp.concatenate(columns, axis=1))
        around = dot(sel_h[c], jnp.concatenate([high, low], axis=0)) + dot(sel_l[c], high)
        for f in range(4):
            z = zb[f, :, lanes] + 0.2 * (dinv[:, lanes] * around[:, 128 * f : 128 * f + 128])
            zb[f, :, lanes] = z
            rows = pl.ds(128 * f, 128)
            xs_h[rows, lanes], xs_l[rows, lanes] = split(z)

    inner = inn[...]
    both = dot(qf[...], xs_h[...])
    rim = both[0:96] + both[96:192] + dot(qf[0:96, :], xs_l[...])
    up_row = ((iota((32, 128), 0) & 1) == 1)

    def rim_of(start, size, c):
        return rim[start : start + size, 128 * c : 128 * c + 128]

    own = {}
    for x in range(2):
        for y in range(2):
            c = 2 * x + y
            v = inner[:, 128 * c : 128 * c + 128]
            faces = rim_of(64, 32, c)
            v = v + jnp.where(up_row, from_next(faces), from_previous(faces))
            v = add_a(v, 0, rim_of(0, 16, y)) if x == 1 else add_a(v, 1, rim_of(16, 16, 2 + y))
            v = add_b(v, 0, rim_of(32, 16, 2 * x)) if y == 1 else add_b(v, 1, rim_of(48, 16, 2 * x + 1))
            own[(x, y)] = v
    hx = {(1, y): rim_of(0, 16, 2 + y) for y in range(2)} | {(-1, y): rim_of(16, 16, y) for y in range(2)}
    hy = {(1, x): rim_of(32, 16, 2 * x + 1) for x in range(2)} | {(-1, x): rim_of(48, 16, 2 * x) for x in range(2)}

    def edge(d):
        return 1 if d == 1 else 0

    def exchange(blocks, sbuf, rbuf, ssem, rsem):
        copies = []
        for n, (dx, dy) in enumerate(DIRS):
            at = 0
            for v in blocks(dx, dy):
                sbuf[n, pl.ds(at, v.shape[0]), :] = v
                at += v.shape[0]
            copies.append(
                send(sbuf.at[n, pl.ds(0, at)], rbuf.at[n, pl.ds(0, at)], ssem.at[n], rsem.at[n], dx, dy)
            )
        return copies

    def residual_blocks(dx, dy):
        x, y = edge(dx), edge(dy)
        if dy == 0:
            return [own[(x, 0)], own[(x, 1)], hx[(dx, 0)], hx[(dx, 1)], hy[(1, x)], hy[(-1, x)]]
        if dx == 0:
            return [own[(0, y)], own[(1, y)], hy[(dy, 0)], hy[(dy, 1)], hx[(1, y)], hx[(-1, y)]]
        return [own[(x, y)], hx[(dx, y)], hy[(dy, x)]]

    second = exchange(residual_blocks, s2, r2, ssem2, rsem2)

    for f in range(4):
        rows = pl.ds(128 * f, 128)
        x1 = 2.0 * zb[f] + 0.8 * xhat[f]
        xhat[f] = x1
        xs_h[rows, :], xs_l[rows, :] = split(x1)
        for part in range(2):
            span = pl.ds(128 * part, 128)
            faces = (
                dot(fb_h[span, :], xs_h[rows, :])
                + dot(fb_h[span, :], xs_l[rows, :])
                + dot(fb_l[span, :], xs_h[rows, :])
            )
            fz[f, span, :] = faces
        sx[0, f] = fz[f, 0:25, 256:512]
        sx[1, f] = fz[f, 32:57, 0:256]
        for x in range(2):
            sy[0, f, :, pl.ds(128 * x, 128)] = fz[f, 64:104, 256 * x + 128 : 256 * x + 256]
            sy[1, f, :, pl.ds(128 * x, 128)] = fz[f, 104:144, 256 * x : 256 * x + 128]
    receive(second[6:])
    whole = [
        send(sx.at[0], rx.at[0], ssemf.at[0], rsemf.at[0], 1, 0),
        send(sx.at[1], rx.at[1], ssemf.at[1], rsemf.at[1], -1, 0),
        send(sy.at[0], ry.at[0], ssemf.at[2], rsemf.at[2], 0, 1),
        send(sy.at[1], ry.at[1], ssemf.at[3], rsemf.at[3], 0, -1),
    ]
    receive(second[:6])
    field_of = {}

    def put(at, v):
        field_of[at] = field_of[at] + v if at in field_of else v

    for at, v in own.items():
        put(at, v)
    late = []
    for y in range(2):
        late += [("a", 0, (2, y), hx[(1, y)]), ("a", 1, (-1, y), hx[(-1, y)])]
        late += [("b", 0, (y, 2), hy[(1, y)]), ("b", 1, (y, -1), hy[(-1, y)])]
    for n, (dx, dy) in enumerate(DIRS):
        x, y = edge(dx), edge(dy)
        side_a, side_b = (0 if dx == 1 else 1), (0 if dy == 1 else 1)
        if dy == 0:
            for t in range(2):
                put((x - 2 * dx, t), r2[n, 32 * t : 32 * t + 32, :])
                late.append(("a", side_a, (x - dx, t), r2[n, 64 + 16 * t : 80 + 16 * t, :]))
            late.append(("b", 0, (x - 2 * dx, 2), r2[n, 96:112, :]))
            late.append(("b", 1, (x - 2 * dx, -1), r2[n, 112:128, :]))
        elif dx == 0:
            for t in range(2):
                put((t, y - 2 * dy), r2[n, 32 * t : 32 * t + 32, :])
                late.append(("b", side_b, (t, y - dy), r2[n, 64 + 16 * t : 80 + 16 * t, :]))
            late.append(("a", 0, (2, y - 2 * dy), r2[n, 96:112, :]))
            late.append(("a", 1, (-1, y - 2 * dy), r2[n, 112:128, :]))
        else:
            put((x - 2 * dx, y - 2 * dy), r2[n, 0:32, :])
            late.append(("a", side_a, (x - dx, y - 2 * dy), r2[n, 32:48, :]))
            late.append(("b", side_b, (x - 2 * dx, y - dy), r2[n, 48:64, :]))
    for kind, side, at, v in late:
        field_of[at] = add_a(field_of[at], side, v) if kind == "a" else add_b(field_of[at], side, v)

    for (x, y), v in field_of.items():
        for z, value in enumerate((v, pltpu.roll(v, 127, 1))):
            rows = pl.ds(32 * (8 * (x + 1) + 2 * (y + 1) + z), 32)
            cz[rows, 0:128], cz[rows, 128:256] = split(value)
    halves = [pl.ds(256 * h, 256) for h in range(2)]

    def row_of(v, h):
        return jnp.broadcast_to(v[:, 256 * h : 256 * h + 256], (8, 256))

    def slots(h):
        return [row_of(place[t : t + 1], h) for t in range(8)]

    for half in halves:
        gz[:, half] = dot(cz[...], zz[:, half])
    for h, half in enumerate(halves):
        places = slots(h)
        in_x, in_y = row_of(low_x, h), row_of(low_y, h)
        x_one, x_two, y_one, y_two = in_x == 1, in_x == 2, in_y == 1, in_y == 2
        for t in range(4):

            def at(x, y, z):
                return gz[pl.ds(32 * (8 * x + 2 * y + z) + 8 * t, 8), half]

            cube = []
            for x in range(2):
                by_y = []
                for y in range(4):
                    by_y.append([
                        jnp.where(x_two, at(x + 2, y, z), jnp.where(x_one, at(x + 1, y, z), at(x, y, z)))
                        for z in range(2)
                    ])
                for y in range(2):
                    for z in range(2):
                        cube.append(jnp.where(y_two, by_y[y + 2][z], jnp.where(y_one, by_y[y + 1][z], by_y[y][z])))
            for slot in range(8):
                value = jnp.zeros((8, 256), F32)
                for p in range(8):
                    value = jnp.where(places[slot] == p, cube[p], value)
                wf[pl.ds(32 * slot + 8 * t, 8), half] = value
        wh, wl = split(wf[:, half])
        ans[:, half] = dot(mi_h[...], wh) + dot(mi_h[...], wl) + dot(mi_l[...], wh)
    for h, half in enumerate(halves):
        places = slots(h)
        for t in range(4):
            solved = [ans[pl.ds(32 * slot + 8 * t, 8), half] for slot in range(8)]
            for p in range(8):
                value = jnp.zeros((8, 256), F32)
                for slot in range(8):
                    value = jnp.where(places[slot] == p, solved[slot], value)
                wf[pl.ds(32 * p + 8 * t, 8), half] = value
        ap[0:256, half], ap[256:512, half] = split(wf[:, half])
    vv[...] = dot_nt(ap[pl.ds(0, 256), :], oh[...]) + dot_nt(ap[pl.ds(256, 256), :], oh[...])
    spread = {}
    for x in range(-1, 3):
        for y in range(-1, 3):
            sums = [None, None]
            for sx_, sy_ in ((0, 0), (0, 1), (1, 0), (1, 1)):
                vx, vy = x + 1 - sx_, y + 1 - sy_
                if 0 <= vx <= 2 and 0 <= vy <= 2:
                    for z in range(2):
                        p = sx_ * 4 + sy_ * 2 + z
                        v = vv[pl.ds(32 * p, 32), pl.ds(128 * (3 * vx + vy), 128)]
                        sums[z] = v if sums[z] is None else sums[z] + v
            spread[(x, y)] = sums[0] + pltpu.roll(sums[1], 1, 1)

    def correction_blocks(dx, dy):
        x, y = edge(dx), edge(dy)
        if dy == 0:
            return [
                spread[(x + dx, 0)], spread[(x + dx, 1)], a_half(spread[(x, 0)], x), a_half(spread[(x, 1)], x),
                b_half(spread[(x + dx, 2)], 0), b_half(spread[(x + dx, -1)], 1),
            ]
        if dx == 0:
            return [
                spread[(0, y + dy)], spread[(1, y + dy)], b_half(spread[(0, y)], y), b_half(spread[(1, y)], y),
                a_half(spread[(2, y + dy)], 0), a_half(spread[(-1, y + dy)], 1),
            ]
        return [spread[(x + dx, y + dy)], a_half(spread[(x, y + dy)], x), b_half(spread[(x + dx, y)], y)]

    third = exchange(correction_blocks, s3, r3, ssem3, rsem3)

    receive(whole)
    for f in range(4):
        x_up = jnp.concatenate([fz[f, 32:64, 256:512], rows_to(rx[1, f], 32)], axis=1)
        x_down = jnp.concatenate([rows_to(rx[0, f], 32), fz[f, 0:32, 0:256]], axis=1)
        y_up, y_down = [], []
        for x in range(2):
            y_up += [fz[f, 104:144, 256 * x + 128 : 256 * x + 256], ry[1, f, :, 128 * x : 128 * x + 128]]
            y_down += [ry[0, f, :, 128 * x : 128 * x + 128], fz[f, 64:104, 256 * x : 256 * x + 128]]
        parts = [
            x_up, x_down,
            jnp.concatenate(y_up, axis=1),
            jnp.concatenate(y_down, axis=1),
            by_column(from_next, fz[f, 176:208, :]),
            by_column(from_previous, fz[f, 144:176, :]),
            jnp.zeros((48, LANES), F32),
        ]
        around = mm3(bte_h[...], bte_l[...], jnp.concatenate(parts, axis=0))
        xhat[f] = 0.2 * xhat[f] + 0.8 * (dinv[...] * (bhat[f] + 0.5 * around))

    receive(third)
    fixed = {at: spread[at] for at in own}
    near_x = {(2, y): a_half(spread[(2, y)], 0) for y in range(2)} | {
        (-1, y): a_half(spread[(-1, y)], 1) for y in range(2)
    }
    near_y = {(x, 2): b_half(spread[(x, 2)], 0) for x in range(2)} | {
        (x, -1): b_half(spread[(x, -1)], 1) for x in range(2)
    }
    for n, (dx, dy) in enumerate(DIRS):
        x, y = edge(dx), edge(dy)
        if dy == 0:
            for t in range(2):
                fixed[(x - dx, t)] += r3[n, 32 * t : 32 * t + 32, :]
                near_x[(x - 2 * dx, t)] += r3[n, 64 + 16 * t : 80 + 16 * t, :]
            near_y[(x - dx, 2)] += r3[n, 96:112, :]
            near_y[(x - dx, -1)] += r3[n, 112:128, :]
        elif dx == 0:
            for t in range(2):
                fixed[(t, y - dy)] += r3[n, 32 * t : 32 * t + 32, :]
                near_y[(t, y - 2 * dy)] += r3[n, 64 + 16 * t : 80 + 16 * t, :]
            near_x[(2, y - dy)] += r3[n, 96:112, :]
            near_x[(-1, y - dy)] += r3[n, 112:128, :]
        else:
            fixed[(x - dx, y - dy)] += r3[n, 0:32, :]
            near_x[(x - 2 * dx, y - dy)] += r3[n, 32:48, :]
            near_y[(x - dx, y - 2 * dy)] += r3[n, 48:64, :]

    columns, rims = [], []
    for x in range(2):
        for y in range(2):
            v = fixed[(x, y)]
            columns.append(v)
            rims.append(
                jnp.concatenate(
                    [
                        a_half(fixed[(1, y)], 0) if x == 0 else near_x[(2, y)],
                        a_half(fixed[(0, y)], 1) if x == 1 else near_x[(-1, y)],
                        b_half(fixed[(x, 1)], 0) if y == 0 else near_y[(x, 2)],
                        b_half(fixed[(x, 0)], 1) if y == 1 else near_y[(x, -1)],
                        jnp.where(up_row, from_previous(v), from_next(v)),
                        jnp.zeros((32, 128), F32),
                    ],
                    axis=0,
                )
            )
    ch, cl = split(jnp.concatenate(columns, axis=1))
    stacked = jnp.concatenate([ch, cl, ch, jnp.zeros((32, LANES), BF16)], axis=0)
    rh, rl = split(jnp.concatenate(rims, axis=1))
    rims_both = jnp.concatenate([rh, rl], axis=0)
    for f in range(4):
        rows = pl.ds(128 * f, 128)
        direct = dot(tc[rows, :], stacked)
        coupled = dot(tf_h[rows, :], rims_both) + dot(tf_l[rows, :], rh)
        final = xhat[f] + 0.2 * direct + 0.4 * (dinv[...] * coupled)
        high, low = split(final)
        value = dot(bb_h[...], jnp.concatenate([high, low], axis=0)) + dot(bb_l[...], high)
        for c in range(4):
            outv[pl.ds(500 * f + c, 125, stride=4), :] = value[0:125, 128 * c : 128 * c + 128]
    for copy, dx, dy in sent:

        @pl.when(exists(dx, dy))
        def _():
            copy.wait_send()


def solution(mesh):
    nx, ny = mesh.shape["px"], mesh.shape["py"]
    table = column_table()

    def per_device(
        right_side, first_guess, coefficient, modal_basis, modal_values, patch_inverse, patch_elements, patch_mask
    ):
        hbm = pl.BlockSpec(memory_space=pltpu.HBM)

        def body(*refs):
            kernel(nx, ny, *refs)

        def f32(*shape):
            return pltpu.VMEM(shape, F32)

        def b16(*shape):
            return pltpu.VMEM(shape, BF16)

        def in_hbm(array):
            return pltpu.with_memory_space_constraint(array, pltpu.HBM)

        dma = pltpu.SemaphoreType.DMA
        out = pl.pallas_call(
            body,
            out_shape=pltpu.VMEM((2000, 128), F32),
            in_specs=[hbm] * 12,
            out_specs=pl.BlockSpec(memory_space=pltpu.VMEM),
            scratch_shapes=[
                pltpu.SMEM((5, 5), F32), pltpu.SMEM((5,), F32),
                f32(4, 125, 512), f32(4, 125, 512), f32(2, 4, 25, 512), f32(2, 4, 5, 5, 512), f32(2, 4, 25, 512),
                f32(4, 128), f32(256, 256), pltpu.VMEM((8, 512), jnp.int32), pltpu.VMEM((8, 512), jnp.int32),
                pltpu.VMEM((8, 1152), jnp.int32),
                b16(128, 128), b16(128, 128), b16(128, 256), b16(128, 256), b16(128, 256), b16(128, 128),
                b16(256, 128), b16(256, 128),
                b16(4, 128, 256), b16(4, 128, 128), f32(4, 128, 512), f32(32, 512), b16(64, 512), b16(192, 512),
                b16(512, 128), b16(512, 256), b16(512, 128), b16(256, 256), b16(256, 256),
                f32(4, 128, 512), f32(4, 128, 512), f32(128, 512), b16(1152, 512),
                b16(512, 512), b16(512, 512), b16(512, 512), b16(512, 512),
                b16(1024, 256), b16(256, 512), f32(1024, 512), f32(256, 512), f32(256, 512), b16(512, 512),
                f32(256, 1152),
                f32(2, 4, 25, 256), f32(2, 4, 40, 256), f32(2, 4, 25, 256), f32(2, 4, 40, 256), f32(4, 256, 512),
                f32(8, 128, 128), f32(8, 128, 128), f32(8, 128, 128), f32(8, 128, 128),
                dma((20,)), dma((6,)), dma((6,)), dma((4,)), dma((4,)), dma((8,)), dma((8,)), dma((8,)), dma((8,)),
            ],
            compiler_params=pltpu.CompilerParams(
                collective_id=0, has_side_effects=True, vmem_limit_bytes=60 * 1024 * 1024
            ),
        )(
            in_hbm(first_guess.reshape(4, 125, 1, 512)),
            in_hbm(first_guess.reshape(4, 5, 25, 2, 1, 256)),
            in_hbm(first_guess.reshape(4, 5, 5, 5, 2, 2, 1, 128)),
            in_hbm(first_guess.reshape(4, 25, 5, 1, 512)),
            in_hbm(right_side.reshape(4, 125, 1, 512)),
            in_hbm(coefficient.reshape(4, 128)),
            in_hbm(modal_basis),
            in_hbm(modal_values),
            in_hbm(patch_inverse),
            in_hbm(patch_elements.T),
            in_hbm(patch_mask.T),
            in_hbm(jnp.asarray(table)),
        )
        return out.reshape(4, 5, 5, 5, 2, 2, 128)

    grid = P(None, None, None, None, "px", "py", None)
    rows = P(("px", "py"), None)
    return jax.shard_map(
        per_device,
        mesh=mesh,
        in_specs=(grid, grid, P("px", "py", None), P(), P(), P(), rows, rows),
        out_specs=grid,
        check_vma=False,
    )
```

```python
import math

import jax
import jax.numpy as jnp
import numpy as np
from jax import lax
from jax.experimental import pallas as pl
from jax.experimental.pallas import tpu as pltpu
from jax.sharding import PartitionSpec as P

MESH = pl.DeviceIdType.MESH
F32 = jnp.float32
BF16 = jnp.bfloat16
DIRS = ((1, 1), (1, -1), (-1, 1), (-1, -1), (1, 0), (-1, 0), (0, 1), (0, -1))
LANES = 512


def linear_values():
    root = np.float32(math.sqrt(3.0 / 7.0))
    points = np.array([-1.0, -root, 0.0, root, 1.0], np.float32)
    half = np.float32(0.5)
    return (1 - points) * half, (1 + points) * half


def column_table():
    table = np.full((8, 1152), 7, np.int32)
    table[3] = 9

    def put(column, i, j, k, f=9):
        table[0:4, column] = (i, j, k, f)

    for n in range(125):
        put(n, n // 25, n // 5 % 5, n % 5)
    for g in range(25):
        u, v = g // 5, g % 5
        put(128 + g, 4, u, v)
        put(160 + g, 0, u, v)
        put(192 + u * 8 + v, u, 4, v)
        put(232 + u * 8 + v, u, 0, v)
        put(272 + g, u, v, 4)
        put(304 + g, u, v, 0)
    for c in range(4):
        for g in range(25):
            u, v = g // 5, g % 5
            put(640 + 128 * c + g, 4 if c >= 2 else 0, u, v)
            put(672 + 128 * c + u * 8 + v, u, 4 if c % 2 else 0, v)
    for r in range(32):
        a, b, f, c = r // 16, r // 8 % 2, r // 2 % 4, r % 2
        for copy in range(3):
            put(384 + 32 * copy + r, 5 + a, 5 + b, 5 + c, f)
        put(512 + 64 + r, 5 + a, 5 + b, 4 if c == 0 else 0, f)
    for r in range(16):
        h, f, c = r // 8, r // 2 % 4, r % 2
        put(512 + r, 4, 5 + h, 5 + c, f)
        put(528 + r, 0, 5 + h, 5 + c, f)
        put(544 + r, 5 + h, 4, 5 + c, f)
        put(560 + r, 5 + h, 0, 5 + c, f)
    return table


def split(value):
    high = value.astype(BF16)
    return high, (value - high.astype(F32)).astype(BF16)


def dot(a, b):
    return lax.dot_general(a, b, (((1,), (0,)), ((), ())), preferred_element_type=F32)


def dot_nt(a, b):
    return lax.dot_general(a, b, (((1,), (1,)), ((), ())), preferred_element_type=F32)


def mm3(ah, al, x):
    xh, xl = split(x)
    return dot(ah, xh) + dot(ah, xl) + dot(al, xh)


def iota(shape, dim):
    return lax.broadcasted_iota(jnp.int32, shape, dim)


def a_half(v, a):
    return v[16 * a : 16 * a + 16]


def b_half(v, b):
    return jnp.concatenate([v[8 * b : 8 * b + 8], v[16 + 8 * b : 24 + 8 * b]], axis=0)


def add_a(v, a, h):
    parts = [v[0:16], v[16:32]]
    parts[a] = parts[a] + h
    return jnp.concatenate(parts, axis=0)


def add_b(v, b, h):
    parts = [v[0:8], v[8:16], v[16:24], v[24:32]]
    parts[b] = parts[b] + h[0:8]
    parts[2 + b] = parts[2 + b] + h[8:16]
    return jnp.concatenate(parts, axis=0)


def rows_to(v, rows):
    return jnp.concatenate([v, jnp.zeros((rows - v.shape[0], v.shape[1]), v.dtype)], axis=0)


def from_next(v):
    lane = iota(v.shape, 1)
    return jnp.where(lane == 127, 0.0, pltpu.roll(v, 127, 1))


def from_previous(v):
    lane = iota(v.shape, 1)
    return jnp.where(lane == 0, 0.0, pltpu.roll(v, 1, 1))


def by_column(fn, v):
    return jnp.concatenate([fn(v[:, 128 * c : 128 * c + 128]) for c in range(4)], axis=1)


def kernel(
    nx, ny,
    xa, xx, xy, xz, ba, coef_h, ub_h, mv_h, pinv_h, pe_h, pm_h, tab_h,
    fin, turn,
    ub, mv, xin, bin_, nfx, nfy, nfz, coef, pinv, pe, pm, tab,
    bt_h, bt_l, bte_h, bte_l, fb_h, fb_l,
    sel_h, sel_l, zb, inn, qc, qf, tc, tf_h, tf_l, mi_h, mi_l,
    xhat, bhat, dinv, oh, xs_h, xs_l, ts_h, ts_l,
    cz, zz, gz, wf, ans, ap, vv,
    sx, sy, rx, ry, fz, s2, r2, s3, r3,
    lsem, ssem1, rsem1, ssemf, rsemf, ssem2, rsem2, ssem3, rsem3,
):
    px, py = lax.axis_index("px"), lax.axis_index("py")

    def peer(dx, dy):
        return (lax.rem(px + dx + nx, nx), lax.rem(py + dy + ny, ny))

    inside = {(1, 0): px < nx - 1, (-1, 0): px > 0, (0, 1): py < ny - 1, (0, -1): py > 0}

    def exists(dx, dy):
        if dx == 0 or dy == 0:
            return inside[(dx, dy)]
        return inside[(dx, 0)] & inside[(0, dy)]

    def unless(condition):
        return pl.when(jnp.logical_not(condition))

    barrier = pltpu.get_barrier_semaphore()
    greeted = 0
    for dx, dy in DIRS[4:]:
        greeted = greeted + jnp.where(exists(dx, dy), 1, 0)

        @pl.when(exists(dx, dy))
        def _():
            pl.semaphore_signal(barrier, inc=1, device_id=peer(dx, dy), device_id_type=MESH)

    local = []

    def load(src, dst):
        copy = pltpu.make_async_copy(src, dst, lsem.at[len(local)])
        copy.start()
        local.append(copy)

    load(tab_h, tab)
    load(coef_h, coef)
    load(ub_h, ub)
    load(mv_h, mv)
    load(xa.at[:, :, 0, :], xin)
    load(ba.at[:, :, 0, :], bin_)
    load(pe_h, pe)
    load(pm_h, pm)
    load(pinv_h, pinv)
    load(xx.at[:, 0, :, 1, 0, :], nfx.at[0, :, :, pl.ds(0, 256)])
    load(xx.at[:, 4, :, 0, 0, :], nfx.at[1, :, :, pl.ds(256, 256)])
    for x in range(2):
        load(xy.at[:, :, 0, :, x, 1, 0, :], nfy.at[0, :, :, :, pl.ds(256 * x, 128)])
        load(xy.at[:, :, 4, :, x, 0, 0, :], nfy.at[1, :, :, :, pl.ds(256 * x + 128, 128)])
    load(xz.at[:, :, 0, 0, :], nfz.at[0])
    load(xz.at[:, :, 4, 0, :], nfz.at[1])

    @unless(inside[(1, 0)])
    def _():
        nfx[0, :, :, 256:512] = jnp.zeros((4, 25, 256), F32)
        rx[1] = jnp.zeros((4, 25, 256), F32)

    @unless(inside[(-1, 0)])
    def _():
        nfx[1, :, :, 0:256] = jnp.zeros((4, 25, 256), F32)
        rx[0] = jnp.zeros((4, 25, 256), F32)

    @unless(inside[(0, 1)])
    def _():
        for x in range(2):
            nfy[0, :, :, :, 256 * x + 128 : 256 * x + 256] = jnp.zeros((4, 5, 5, 128), F32)
        ry[1] = jnp.zeros((4, 40, 256), F32)

    @unless(inside[(0, -1)])
    def _():
        for x in range(2):
            nfy[1, :, :, :, 256 * x : 256 * x + 128] = jnp.zeros((4, 5, 5, 128), F32)
        ry[0] = jnp.zeros((4, 40, 256), F32)

    for n, (dx, dy) in enumerate(DIRS):

        @unless(exists(-dx, -dy))
        def _():
            r2[n] = jnp.zeros((128, 128), F32)
            r3[n] = jnp.zeros((128, 128), F32)

    pl.semaphore_wait(barrier, greeted)

    sent = []

    def send(src, dst, ssem, rsem, dx, dy):
        copy = pltpu.make_async_remote_copy(
            src_ref=src, dst_ref=dst, send_sem=ssem, recv_sem=rsem, device_id=peer(dx, dy), device_id_type=MESH
        )

        @pl.when(exists(dx, dy))
        def _():
            copy.start()

        sent.append((copy, dx, dy))
        return sent[-1]

    def receive(copies):
        for copy, dx, dy in copies:

            @pl.when(exists(-dx, -dy))
            def _():
                copy.wait_recv()

    first = [
        send(xx.at[:, 4, :, 1, 0, :], nfx.at[1, :, :, pl.ds(0, 256)], ssem1.at[0], rsem1.at[0], 1, 0),
        send(xx.at[:, 0, :, 0, 0, :], nfx.at[0, :, :, pl.ds(256, 256)], ssem1.at[1], rsem1.at[1], -1, 0),
    ]
    for x in range(2):
        first.append(
            send(xy.at[:, :, 4, :, x, 1, 0, :], nfy.at[1, :, :, :, pl.ds(256 * x, 128)],
                 ssem1.at[2 + 2 * x], rsem1.at[2 + 2 * x], 0, 1)
        )
        first.append(
            send(xy.at[:, :, 0, :, x, 0, 0, :], nfy.at[0, :, :, :, pl.ds(256 * x + 128, 128)],
                 ssem1.at[3 + 2 * x], rsem1.at[3 + 2 * x], 0, -1)
        )

    for copy in local[0:4]:
        copy.wait()
    basis = [[ub[p, q] for q in range(5)] for p in range(5)]
    for weights in linear_values():
        basis.append([sum(float(weights[i]) * basis[i][q] for i in range(5)) for q in range(5)])
    spectrum = [mv[q] for q in range(5)]

    def mode_index(shape):
        row = iota(shape, 0)
        i = (row * 41) >> 10
        rest = row - 25 * i
        j = (rest * 13) >> 6
        return i, j, rest - 5 * j

    def block(start):
        modes = mode_index((128, 128))
        result = None
        for d in range(3):
            index = tab[d : d + 1, start : start + 128]
            hits = [index == p for p in range(7)]
            grown = jnp.zeros((128, 128), F32)
            for q in range(5):
                line = jnp.zeros((1, 128), F32)
                for p in range(7):
                    line = jnp.where(hits[p], basis[p][q], line)
                grown = jnp.where(modes[d] == q, line, grown)
            result = grown if result is None else result * grown
        return result

    nodes = block(0)
    bt_h[...], bt_l[...] = split(nodes)
    high, low = split(nodes.T)
    turn[...] = jnp.concatenate([high, high, low], axis=1)
    for part in range(2):
        faces = block(128 + 128 * part)
        span = pl.ds(128 * part, 128)
        bte_h[:, span], bte_l[:, span] = split(faces)
        fb_h[span, :], fb_l[span, :] = split(faces.T)
    for c in range(4):
        high, low = split(block(640 + 128 * c))
        sel_h[c] = jnp.concatenate([high, high], axis=1)
        sel_l[c] = low
    field = tab[3:4, 384:512]
    coarse_block = block(384)
    copy_of = iota((128, 128), 1)
    for f in range(4):
        part = jnp.where(field == f, coarse_block, 0.0)
        high, low = split(part)
        tc[pl.ds(128 * f, 128), :] = jnp.where(copy_of < 64, high.astype(F32), low.astype(F32)).astype(BF16)
        high, low = split(part.T[0:32])
        qc[0:32, pl.ds(128 * f, 128)] = high
        qc[32:64, pl.ds(128 * f, 128)] = low
    field = tab[3:4, 512:640]
    face_block = block(512)
    for f in range(4):
        part = jnp.where(field == f, face_block, 0.0)
        high, low = split(part)
        tf_h[pl.ds(128 * f, 128), :] = jnp.concatenate([high, high], axis=1)
        tf_l[pl.ds(128 * f, 128), :] = low
        high, low = split(part.T[0:96])
        qf[0:96, pl.ds(128 * f, 128)] = high
        qf[96:192, pl.ds(128 * f, 128)] = low

    modes = mode_index((128, 128))
    total = jnp.zeros((128, 128), F32)
    for d in range(3):
        for q in range(5):
            total = jnp.where(modes[d] == q, total + spectrum[q], total)

    def diagonal(c):
        return total * coef[c : c + 1, :] + 1.0

    for c in range(4):
        dinv[:, pl.ds(128 * c, 128)] = 1.0 / diagonal(c)

    local[4].wait()
    local[5].wait()
    for f in range(4):
        xhat[f] = mm3(bt_h[...], bt_l[...], rows_to(xin[f], 128))
        bhat[f] = mm3(bt_h[...], bt_l[...], rows_to(bin_[f], 128))

    local[6].wait()
    local[7].wait()
    elements = pe[...]
    alive = pm[...] != 0
    at_x = (elements >> 11) - 2 * px + 1
    at_y = ((elements >> 7) & 15) - 2 * py + 1
    at_z = elements & 127

    def least(v, most):
        return jnp.minimum(jnp.min(jnp.where(alive, v, most), axis=0, keepdims=True), most)

    low_x, low_y, low_z = least(at_x, 2), least(at_y, 2), least(at_z, 126)
    key = (low_x * 3 + low_y) * 128 + low_z
    place = (at_x - low_x) * 4 + (at_y - low_y) * 2 + (at_z - low_z)
    place = jnp.where(alive, place, 99)
    vertex = iota((128, LANES), 0)
    lowest = jnp.where(vertex == low_z, 1.0, 0.0).astype(BF16)
    zz[0:128, :] = lowest
    zz[128:256, :] = lowest
    for v in range(9):
        oh[pl.ds(128 * v, 128), :] = jnp.where(vertex + 128 * v == key, 1.0, 0.0).astype(BF16)

    local[8].wait()
    r = iota((256, 256), 0)
    source = (((r >> 1) & 3) * 8 + ((r >> 4) & 1) * 4 + ((r >> 3) & 1) * 2 + (r & 1)) * 8 + (r >> 5)
    order = jnp.where(iota((256, 256), 1) == source, 1.0, 0.0).astype(BF16)
    for piece, target in zip(split(pinv[...]), (mi_h, mi_l)):
        target[...] = dot_nt(dot(order, piece).astype(BF16), order).astype(BF16)

    for copy in local[9:]:
        copy.wait()

    none = jnp.zeros((32, 256), F32)
    gap = jnp.zeros((8, 128), F32)
    for f in range(4):
        parts = [
            jnp.concatenate([rows_to(nfx[0, f, :, 0:256], 32), none], axis=1),
            jnp.concatenate([none, rows_to(nfx[1, f, :, 256:512], 32)], axis=1),
        ]
        for i in range(5):
            near = [rows_to(nfy[0, f, i, :, 256 * x : 256 * x + 128], 8) for x in range(2)]
            parts.append(jnp.concatenate([near[0], gap, near[1], gap], axis=1))
        for i in range(5):
            near = [rows_to(nfy[1, f, i, :, 256 * x + 128 : 256 * x + 256], 8) for x in range(2)]
            parts.append(jnp.concatenate([gap, near[0], gap, near[1]], axis=1))
        parts.append(by_column(from_next, rows_to(nfz[0, f], 32)))
        parts.append(by_column(from_previous, rows_to(nfz[1, f], 32)))
        parts.append(jnp.zeros((48, LANES), F32))
        around = mm3(bte_h[...], bte_l[...], jnp.concatenate(parts, axis=0))
        x0 = xhat[f]
        zb[f] = 0.4 * (dinv[...] * (bhat[f] + 0.5 * around)) - 0.3 * x0
        diag = jnp.concatenate([diagonal(c) for c in range(4)], axis=1)
        rows = pl.ds(128 * f, 128)
        ts_h[rows, :], ts_l[rows, :] = split(bhat[f] - diag * x0)
    both = dot(qc[...], ts_h[...])
    inn[...] = 0.2 * (both[0:32] + both[32:64] + dot(qc[0:32, :], ts_l[...]))

    receive(first)

    for c in range(4):
        x, y = c // 2, c % 2
        lanes = slice(128 * c, 128 * c + 128)
        columns = []
        for f in range(4):
            parts = [rows_to(nfx[1 - x, f, :, lanes], 32)]
            parts += [rows_to(nfy[1 - y, f, i, :, lanes], 8) for i in range(5)]
            parts.append(jnp.zeros((56, 128), F32))
            columns.append(jnp.concatenate(parts, axis=0))
        high, low = split(jnp.concatenate(columns, axis=1))
        around = dot(sel_h[c], jnp.concatenate([high, low], axis=0)) + dot(sel_l[c], high)
        for f in range(4):
            z = zb[f, :, lanes] + 0.2 * (dinv[:, lanes] * around[:, 128 * f : 128 * f + 128])
            zb[f, :, lanes] = z
            rows = pl.ds(128 * f, 128)
            xs_h[rows, lanes], xs_l[rows, lanes] = split(z)

    inner = inn[...]
    both = dot(qf[...], xs_h[...])
    rim = both[0:96] + both[96:192] + dot(qf[0:96, :], xs_l[...])
    up_row = ((iota((32, 128), 0) & 1) == 1)

    def rim_of(start, size, c):
        return rim[start : start + size, 128 * c : 128 * c + 128]

    own = {}
    for x in range(2):
        for y in range(2):
            c = 2 * x + y
            v = inner[:, 128 * c : 128 * c + 128]
            faces = rim_of(64, 32, c)
            v = v + jnp.where(up_row, from_next(faces), from_previous(faces))
            v = add_a(v, 0, rim_of(0, 16, y)) if x == 1 else add_a(v, 1, rim_of(16, 16, 2 + y))
            v = add_b(v, 0, rim_of(32, 16, 2 * x)) if y == 1 else add_b(v, 1, rim_of(48, 16, 2 * x + 1))
            own[(x, y)] = v
    hx = {(1, y): rim_of(0, 16, 2 + y) for y in range(2)} | {(-1, y): rim_of(16, 16, y) for y in range(2)}
    hy = {(1, x): rim_of(32, 16, 2 * x + 1) for x in range(2)} | {(-1, x): rim_of(48, 16, 2 * x) for x in range(2)}

    def edge(d):
        return 1 if d == 1 else 0

    def exchange(blocks, sbuf, rbuf, ssem, rsem):
        copies = []
        for n, (dx, dy) in enumerate(DIRS):
            at = 0
            for v in blocks(dx, dy):
                sbuf[n, pl.ds(at, v.shape[0]), :] = v
                at += v.shape[0]
            copies.append(
                send(sbuf.at[n, pl.ds(0, at)], rbuf.at[n, pl.ds(0, at)], ssem.at[n], rsem.at[n], dx, dy)
            )
        return copies

    def residual_blocks(dx, dy):
        x, y = edge(dx), edge(dy)
        if dy == 0:
            return [own[(x, 0)], own[(x, 1)], hx[(dx, 0)], hx[(dx, 1)], hy[(1, x)], hy[(-1, x)]]
        if dx == 0:
            return [own[(0, y)], own[(1, y)], hy[(dy, 0)], hy[(dy, 1)], hx[(1, y)], hx[(-1, y)]]
        return [own[(x, y)], hx[(dx, y)], hy[(dy, x)]]

    second = exchange(residual_blocks, s2, r2, ssem2, rsem2)

    for f in range(4):
        rows = pl.ds(128 * f, 128)
        x1 = 2.0 * zb[f] + 0.8 * xhat[f]
        xhat[f] = x1
        xs_h[rows, :], xs_l[rows, :] = split(x1)
        for part in range(2):
            span = pl.ds(128 * part, 128)
            faces = (
                dot(fb_h[span, :], xs_h[rows, :])
                + dot(fb_h[span, :], xs_l[rows, :])
                + dot(fb_l[span, :], xs_h[rows, :])
            )
            fz[f, span, :] = faces
        sx[0, f] = fz[f, 0:25, 256:512]
        sx[1, f] = fz[f, 32:57, 0:256]
        for x in range(2):
            sy[0, f, :, pl.ds(128 * x, 128)] = fz[f, 64:104, 256 * x + 128 : 256 * x + 256]
            sy[1, f, :, pl.ds(128 * x, 128)] = fz[f, 104:144, 256 * x : 256 * x + 128]
    receive(second[6:])
    whole = [
        send(sx.at[0], rx.at[0], ssemf.at[0], rsemf.at[0], 1, 0),
        send(sx.at[1], rx.at[1], ssemf.at[1], rsemf.at[1], -1, 0),
        send(sy.at[0], ry.at[0], ssemf.at[2], rsemf.at[2], 0, 1),
        send(sy.at[1], ry.at[1], ssemf.at[3], rsemf.at[3], 0, -1),
    ]
    receive(second[:6])
    field_of = {}

    def put(at, v):
        field_of[at] = field_of[at] + v if at in field_of else v

    for at, v in own.items():
        put(at, v)
    late = []
    for y in range(2):
        late += [("a", 0, (2, y), hx[(1, y)]), ("a", 1, (-1, y), hx[(-1, y)])]
        late += [("b", 0, (y, 2), hy[(1, y)]), ("b", 1, (y, -1), hy[(-1, y)])]
    for n, (dx, dy) in enumerate(DIRS):
        x, y = edge(dx), edge(dy)
        side_a, side_b = (0 if dx == 1 else 1), (0 if dy == 1 else 1)
        if dy == 0:
            for t in range(2):
                put((x - 2 * dx, t), r2[n, 32 * t : 32 * t + 32, :])
                late.append(("a", side_a, (x - dx, t), r2[n, 64 + 16 * t : 80 + 16 * t, :]))
            late.append(("b", 0, (x - 2 * dx, 2), r2[n, 96:112, :]))
            late.append(("b", 1, (x - 2 * dx, -1), r2[n, 112:128, :]))
        elif dx == 0:
            for t in range(2):
                put((t, y - 2 * dy), r2[n, 32 * t : 32 * t + 32, :])
                late.append(("b", side_b, (t, y - dy), r2[n, 64 + 16 * t : 80 + 16 * t, :]))
            late.append(("a", 0, (2, y - 2 * dy), r2[n, 96:112, :]))
            late.append(("a", 1, (-1, y - 2 * dy), r2[n, 112:128, :]))
        else:
            put((x - 2 * dx, y - 2 * dy), r2[n, 0:32, :])
            late.append(("a", side_a, (x - dx, y - 2 * dy), r2[n, 32:48, :]))
            late.append(("b", side_b, (x - 2 * dx, y - dy), r2[n, 48:64, :]))
    for kind, side, at, v in late:
        field_of[at] = add_a(field_of[at], side, v) if kind == "a" else add_b(field_of[at], side, v)

    for (x, y), v in field_of.items():
        for z, value in enumerate((v, pltpu.roll(v, 127, 1))):
            rows = pl.ds(32 * (8 * (x + 1) + 2 * (y + 1) + z), 32)
            cz[rows, 0:128], cz[rows, 128:256] = split(value)
    halves = [pl.ds(256 * h, 256) for h in range(2)]

    def row_of(v, h):
        return jnp.broadcast_to(v[:, 256 * h : 256 * h + 256], (8, 256))

    def slots(h):
        return [row_of(place[t : t + 1], h) for t in range(8)]

    for half in halves:
        gz[:, half] = dot(cz[...], zz[:, half])
    for h, half in enumerate(halves):
        places = slots(h)
        in_x, in_y = row_of(low_x, h), row_of(low_y, h)
        x_one, x_two, y_one, y_two = in_x == 1, in_x == 2, in_y == 1, in_y == 2
        for t in range(4):

            def at(x, y, z):
                return gz[pl.ds(32 * (8 * x + 2 * y + z) + 8 * t, 8), half]

            cube = []
            for x in range(2):
                by_y = []
                for y in range(4):
                    by_y.append([
                        jnp.where(x_two, at(x + 2, y, z), jnp.where(x_one, at(x + 1, y, z), at(x, y, z)))
                        for z in range(2)
                    ])
                for y in range(2):
                    for z in range(2):
                        cube.append(jnp.where(y_two, by_y[y + 2][z], jnp.where(y_one, by_y[y + 1][z], by_y[y][z])))
            for slot in range(8):
                value = jnp.zeros((8, 256), F32)
                for p in range(8):
                    value = jnp.where(places[slot] == p, cube[p], value)
                wf[pl.ds(32 * slot + 8 * t, 8), half] = value
        wh, wl = split(wf[:, half])
        ans[:, half] = dot(mi_h[...], wh) + dot(mi_h[...], wl) + dot(mi_l[...], wh)
    for h, half in enumerate(halves):
        places = slots(h)
        for t in range(4):
            solved = [ans[pl.ds(32 * slot + 8 * t, 8), half] for slot in range(8)]
            for p in range(8):
                value = jnp.zeros((8, 256), F32)
                for slot in range(8):
                    value = jnp.where(places[slot] == p, solved[slot], value)
                wf[pl.ds(32 * p + 8 * t, 8), half] = value
        ap[0:256, half], ap[256:512, half] = split(wf[:, half])
    vv[...] = dot_nt(ap[pl.ds(0, 256), :], oh[...]) + dot_nt(ap[pl.ds(256, 256), :], oh[...])
    spread = {}
    for x in range(-1, 3):
        for y in range(-1, 3):
            sums = [None, None]
            for sx_, sy_ in ((0, 0), (0, 1), (1, 0), (1, 1)):
                vx, vy = x + 1 - sx_, y + 1 - sy_
                if 0 <= vx <= 2 and 0 <= vy <= 2:
                    for z in range(2):
                        p = sx_ * 4 + sy_ * 2 + z
                        v = vv[pl.ds(32 * p, 32), pl.ds(128 * (3 * vx + vy), 128)]
                        sums[z] = v if sums[z] is None else sums[z] + v
            spread[(x, y)] = sums[0] + pltpu.roll(sums[1], 1, 1)

    def correction_blocks(dx, dy):
        x, y = edge(dx), edge(dy)
        if dy == 0:
            return [
                spread[(x + dx, 0)], spread[(x + dx, 1)], a_half(spread[(x, 0)], x), a_half(spread[(x, 1)], x),
                b_half(spread[(x + dx, 2)], 0), b_half(spread[(x + dx, -1)], 1),
            ]
        if dx == 0:
            return [
                spread[(0, y + dy)], spread[(1, y + dy)], b_half(spread[(0, y)], y), b_half(spread[(1, y)], y),
                a_half(spread[(2, y + dy)], 0), a_half(spread[(-1, y + dy)], 1),
            ]
        return [spread[(x + dx, y + dy)], a_half(spread[(x, y + dy)], x), b_half(spread[(x + dx, y)], y)]

    third = exchange(correction_blocks, s3, r3, ssem3, rsem3)

    receive(whole)
    for f in range(4):
        x_up = jnp.concatenate([fz[f, 32:64, 256:512], rows_to(rx[1, f], 32)], axis=1)
        x_down = jnp.concatenate([rows_to(rx[0, f], 32), fz[f, 0:32, 0:256]], axis=1)
        y_up, y_down = [], []
        for x in range(2):
            y_up += [fz[f, 104:144, 256 * x + 128 : 256 * x + 256], ry[1, f, :, 128 * x : 128 * x + 128]]
            y_down += [ry[0, f, :, 128 * x : 128 * x + 128], fz[f, 64:104, 256 * x : 256 * x + 128]]
        parts = [
            x_up, x_down,
            jnp.concatenate(y_up, axis=1),
            jnp.concatenate(y_down, axis=1),
            by_column(from_next, fz[f, 176:208, :]),
            by_column(from_previous, fz[f, 144:176, :]),
            jnp.zeros((48, LANES), F32),
        ]
        around = mm3(bte_h[...], bte_l[...], jnp.concatenate(parts, axis=0))
        xhat[f] = 0.2 * xhat[f] + 0.8 * (dinv[...] * (bhat[f] + 0.5 * around))

    receive(third)
    fixed = {at: spread[at] for at in own}
    near_x = {(2, y): a_half(spread[(2, y)], 0) for y in range(2)} | {
        (-1, y): a_half(spread[(-1, y)], 1) for y in range(2)
    }
    near_y = {(x, 2): b_half(spread[(x, 2)], 0) for x in range(2)} | {
        (x, -1): b_half(spread[(x, -1)], 1) for x in range(2)
    }
    for n, (dx, dy) in enumerate(DIRS):
        x, y = edge(dx), edge(dy)
        if dy == 0:
            for t in range(2):
                fixed[(x - dx, t)] += r3[n, 32 * t : 32 * t + 32, :]
                near_x[(x - 2 * dx, t)] += r3[n, 64 + 16 * t : 80 + 16 * t, :]
            near_y[(x - dx, 2)] += r3[n, 96:112, :]
            near_y[(x - dx, -1)] += r3[n, 112:128, :]
        elif dx == 0:
            for t in range(2):
                fixed[(t, y - dy)] += r3[n, 32 * t : 32 * t + 32, :]
                near_y[(t, y - 2 * dy)] += r3[n, 64 + 16 * t : 80 + 16 * t, :]
            near_x[(2, y - dy)] += r3[n, 96:112, :]
            near_x[(-1, y - dy)] += r3[n, 112:128, :]
        else:
            fixed[(x - dx, y - dy)] += r3[n, 0:32, :]
            near_x[(x - 2 * dx, y - dy)] += r3[n, 32:48, :]
            near_y[(x - dx, y - 2 * dy)] += r3[n, 48:64, :]

    columns, rims = [], []
    for x in range(2):
        for y in range(2):
            v = fixed[(x, y)]
            columns.append(v)
            rims.append(
                jnp.concatenate(
                    [
                        a_half(fixed[(1, y)], 0) if x == 0 else near_x[(2, y)],
                        a_half(fixed[(0, y)], 1) if x == 1 else near_x[(-1, y)],
                        b_half(fixed[(x, 1)], 0) if y == 0 else near_y[(x, 2)],
                        b_half(fixed[(x, 0)], 1) if y == 1 else near_y[(x, -1)],
                        jnp.where(up_row, from_previous(v), from_next(v)),
                        jnp.zeros((32, 128), F32),
                    ],
                    axis=0,
                )
            )
    ch, cl = split(jnp.concatenate(columns, axis=1))
    stacked = jnp.concatenate([ch, cl, ch, jnp.zeros((32, LANES), BF16)], axis=0)
    rh, rl = split(jnp.concatenate(rims, axis=1))
    rims_both = jnp.concatenate([rh, rl], axis=0)
    for f in range(4):
        rows = pl.ds(128 * f, 128)
        direct = dot(tc[rows, :], stacked)
        coupled = dot(tf_h[rows, :], rims_both) + dot(tf_l[rows, :], rh)
        final = xhat[f] + 0.2 * direct + 0.4 * (dinv[...] * coupled)
        fin[f, 0:128, :], fin[f, 128:256, :] = split(final)
    for copy, dx, dy in sent:

        @pl.when(exists(dx, dy))
        def _():
            copy.wait_send()


def to_nodes(fin, turn, out, value, sem):
    copies = []
    for f in range(4):
        pieces = fin[f]
        nodes = dot(turn[:, 0:256], pieces) + dot(turn[:, 256:384], pieces[0:128])
        for c in range(4):
            value[pl.ds(500 * f + c, 125, stride=4), :] = nodes[0:125, 128 * c : 128 * c + 128]
        start, end = 500 * f // 8 * 8, 500 * (f + 1) // 8 * 8
        span = pl.ds(start, end - start)
        copies.append(pltpu.make_async_copy(value.at[span], out.at[span], sem.at[f]))
        copies[-1].start()
    for copy in copies:
        copy.wait()


def solution(mesh):
    nx, ny = mesh.shape["px"], mesh.shape["py"]
    table = column_table()

    def per_device(
        right_side, first_guess, coefficient, modal_basis, modal_values, patch_inverse, patch_elements, patch_mask
    ):
        hbm = pl.BlockSpec(memory_space=pltpu.HBM)

        def body(*refs):
            kernel(nx, ny, *refs)

        def f32(*shape):
            return pltpu.VMEM(shape, F32)

        def b16(*shape):
            return pltpu.VMEM(shape, BF16)

        def in_hbm(array):
            return pltpu.with_memory_space_constraint(array, pltpu.HBM)

        dma = pltpu.SemaphoreType.DMA
        fin, turn = pl.pallas_call(
            body,
            out_shape=(pltpu.VMEM((4, 256, 512), BF16), pltpu.VMEM((128, 384), BF16)),
            in_specs=[hbm] * 12,
            out_specs=(pl.BlockSpec(memory_space=pltpu.VMEM),) * 2,
            scratch_shapes=[
                pltpu.SMEM((5, 5), F32), pltpu.SMEM((5,), F32),
                f32(4, 125, 512), f32(4, 125, 512), f32(2, 4, 25, 512), f32(2, 4, 5, 5, 512), f32(2, 4, 25, 512),
                f32(4, 128), f32(256, 256), pltpu.VMEM((8, 512), jnp.int32), pltpu.VMEM((8, 512), jnp.int32),
                pltpu.VMEM((8, 1152), jnp.int32),
                b16(128, 128), b16(128, 128), b16(128, 256), b16(128, 256),
                b16(256, 128), b16(256, 128),
                b16(4, 128, 256), b16(4, 128, 128), f32(4, 128, 512), f32(32, 512), b16(64, 512), b16(192, 512),
                b16(512, 128), b16(512, 256), b16(512, 128), b16(256, 256), b16(256, 256),
                f32(4, 128, 512), f32(4, 128, 512), f32(128, 512), b16(1152, 512),
                b16(512, 512), b16(512, 512), b16(512, 512), b16(512, 512),
                b16(1024, 256), b16(256, 512), f32(1024, 512), f32(256, 512), f32(256, 512), b16(512, 512),
                f32(256, 1152),
                f32(2, 4, 25, 256), f32(2, 4, 40, 256), f32(2, 4, 25, 256), f32(2, 4, 40, 256), f32(4, 256, 512),
                f32(8, 128, 128), f32(8, 128, 128), f32(8, 128, 128), f32(8, 128, 128),
                dma((20,)), dma((6,)), dma((6,)), dma((4,)), dma((4,)), dma((8,)), dma((8,)), dma((8,)), dma((8,)),
            ],
            compiler_params=pltpu.CompilerParams(
                collective_id=0, has_side_effects=True, vmem_limit_bytes=60 * 1024 * 1024
            ),
        )(
            in_hbm(first_guess.reshape(4, 125, 1, 512)),
            in_hbm(first_guess.reshape(4, 5, 25, 2, 1, 256)),
            in_hbm(first_guess.reshape(4, 5, 5, 5, 2, 2, 1, 128)),
            in_hbm(first_guess.reshape(4, 25, 5, 1, 512)),
            in_hbm(right_side.reshape(4, 125, 1, 512)),
            in_hbm(coefficient.reshape(4, 128)),
            in_hbm(modal_basis),
            in_hbm(modal_values),
            in_hbm(patch_inverse),
            in_hbm(patch_elements.T),
            in_hbm(patch_mask.T),
            in_hbm(jnp.asarray(table)),
        )
        out = pl.pallas_call(
            to_nodes,
            out_shape=jax.ShapeDtypeStruct((2000, 128), F32),
            in_specs=[pl.BlockSpec(memory_space=pltpu.VMEM)] * 2,
            out_specs=pl.BlockSpec(memory_space=pl.ANY),
            scratch_shapes=[f32(2000, 128), dma((4,))],
            compiler_params=pltpu.CompilerParams(vmem_limit_bytes=16 * 1024 * 1024),
        )(fin, turn)
        return out.reshape(4, 5, 5, 5, 2, 2, 128)

    grid = P(None, None, None, None, "px", "py", None)
    rows = P(("px", "py"), None)
    return jax.shard_map(
        per_device,
        mesh=mesh,
        in_specs=(grid, grid, P("px", "py", None), P(), P(), P(), rows, rows),
        out_specs=grid,
        check_vma=False,
    )
```

```python
import math

import jax
import jax.numpy as jnp
import numpy as np
from jax import lax
from jax.experimental import pallas as pl
from jax.experimental.pallas import tpu as pltpu
from jax.sharding import PartitionSpec as P

MESH = pl.DeviceIdType.MESH
F32 = jnp.float32
BF16 = jnp.bfloat16
DIRS = ((1, 1), (1, -1), (-1, 1), (-1, -1), (1, 0), (-1, 0), (0, 1), (0, -1))
LANES = 512


def linear_values():
    root = np.float32(math.sqrt(3.0 / 7.0))
    points = np.array([-1.0, -root, 0.0, root, 1.0], np.float32)
    half = np.float32(0.5)
    return (1 - points) * half, (1 + points) * half


def column_table():
    table = np.full((8, 1152), 7, np.int32)
    table[3] = 9

    def put(column, i, j, k, f=9):
        table[0:4, column] = (i, j, k, f)

    for n in range(125):
        put(n, n // 25, n // 5 % 5, n % 5)
    for g in range(25):
        u, v = g // 5, g % 5
        put(128 + g, 4, u, v)
        put(160 + g, 0, u, v)
        put(192 + u * 8 + v, u, 4, v)
        put(232 + u * 8 + v, u, 0, v)
        put(272 + g, u, v, 4)
        put(304 + g, u, v, 0)
    for c in range(4):
        for g in range(25):
            u, v = g // 5, g % 5
            put(640 + 128 * c + g, 4 if c >= 2 else 0, u, v)
            put(672 + 128 * c + u * 8 + v, u, 4 if c % 2 else 0, v)
    for r in range(32):
        a, b, f, c = r // 16, r // 8 % 2, r // 2 % 4, r % 2
        for copy in range(3):
            put(384 + 32 * copy + r, 5 + a, 5 + b, 5 + c, f)
        put(512 + 64 + r, 5 + a, 5 + b, 4 if c == 0 else 0, f)
    for r in range(16):
        h, f, c = r // 8, r // 2 % 4, r % 2
        put(512 + r, 4, 5 + h, 5 + c, f)
        put(528 + r, 0, 5 + h, 5 + c, f)
        put(544 + r, 5 + h, 4, 5 + c, f)
        put(560 + r, 5 + h, 0, 5 + c, f)
    return table


def split(value):
    high = value.astype(BF16)
    return high, (value - high.astype(F32)).astype(BF16)


def dot(a, b):
    return lax.dot_general(a, b, (((1,), (0,)), ((), ())), preferred_element_type=F32)


def dot_nt(a, b):
    return lax.dot_general(a, b, (((1,), (1,)), ((), ())), preferred_element_type=F32)


def mm3(ah, al, x):
    xh, xl = split(x)
    return dot(ah, xh) + dot(ah, xl) + dot(al, xh)


def iota(shape, dim):
    return lax.broadcasted_iota(jnp.int32, shape, dim)


def a_half(v, a):
    return v[16 * a : 16 * a + 16]


def b_half(v, b):
    return jnp.concatenate([v[8 * b : 8 * b + 8], v[16 + 8 * b : 24 + 8 * b]], axis=0)


def add_a(v, a, h):
    parts = [v[0:16], v[16:32]]
    parts[a] = parts[a] + h
    return jnp.concatenate(parts, axis=0)


def add_b(v, b, h):
    parts = [v[0:8], v[8:16], v[16:24], v[24:32]]
    parts[b] = parts[b] + h[0:8]
    parts[2 + b] = parts[2 + b] + h[8:16]
    return jnp.concatenate(parts, axis=0)


def rows_to(v, rows):
    return jnp.concatenate([v, jnp.zeros((rows - v.shape[0], v.shape[1]), v.dtype)], axis=0)


def from_next(v):
    lane = iota(v.shape, 1)
    return jnp.where(lane == 127, 0.0, pltpu.roll(v, 127, 1))


def from_previous(v):
    lane = iota(v.shape, 1)
    return jnp.where(lane == 0, 0.0, pltpu.roll(v, 1, 1))


def by_column(fn, v):
    return jnp.concatenate([fn(v[:, 128 * c : 128 * c + 128]) for c in range(4)], axis=1)


def kernel(
    nx, ny,
    xa, xx, xy, xz, ba, coef_h, ub_h, mv_h, pinv_h, pe_h, pm_h, tab_h,
    fin, turn,
    ub, mv, xin, bin_, nfx, nfy, nfz, coef, pinv, pe, pm, tab,
    bt_h, bt_l, bte_h, bte_l, fb_h, fb_l,
    sel_h, sel_l, zb, inn, qc, qf, tc, tf_h, tf_l, mi_h, mi_l,
    xhat, bhat, dinv, oh, xs_h, xs_l, ts_h, ts_l,
    cz, zz, gz, wf, ans, ap, vv,
    sx, sy, rx, ry, fz, s2, r2, s3, r3,
    lsem, ssem1, rsem1, ssemf, rsemf, ssem2, rsem2, ssem3, rsem3,
):
    px, py = lax.axis_index("px"), lax.axis_index("py")

    def peer(dx, dy):
        return (lax.rem(px + dx + nx, nx), lax.rem(py + dy + ny, ny))

    inside = {(1, 0): px < nx - 1, (-1, 0): px > 0, (0, 1): py < ny - 1, (0, -1): py > 0}

    def exists(dx, dy):
        if dx == 0 or dy == 0:
            return inside[(dx, dy)]
        return inside[(dx, 0)] & inside[(0, dy)]

    def unless(condition):
        return pl.when(jnp.logical_not(condition))

    barrier = pltpu.get_barrier_semaphore()
    greeted = 0
    for dx, dy in DIRS[4:]:
        greeted = greeted + jnp.where(exists(dx, dy), 1, 0)

        @pl.when(exists(dx, dy))
        def _():
            pl.semaphore_signal(barrier, inc=1, device_id=peer(dx, dy), device_id_type=MESH)

    local = []

    def load(src, dst):
        copy = pltpu.make_async_copy(src, dst, lsem.at[len(local)])
        copy.start()
        local.append(copy)

    load(tab_h, tab)
    load(coef_h, coef)
    load(ub_h, ub)
    load(mv_h, mv)
    load(xa.at[:, :, 0, :], xin)
    load(ba.at[:, :, 0, :], bin_)
    load(pe_h, pe)
    load(pm_h, pm)
    load(pinv_h, pinv)
    load(xx.at[:, 0, :, 1, 0, :], nfx.at[0, :, :, pl.ds(0, 256)])
    load(xx.at[:, 4, :, 0, 0, :], nfx.at[1, :, :, pl.ds(256, 256)])
    for x in range(2):
        load(xy.at[:, :, 0, :, x, 1, 0, :], nfy.at[0, :, :, :, pl.ds(256 * x, 128)])
        load(xy.at[:, :, 4, :, x, 0, 0, :], nfy.at[1, :, :, :, pl.ds(256 * x + 128, 128)])
    load(xz.at[:, :, 0, 0, :], nfz.at[0])
    load(xz.at[:, :, 4, 0, :], nfz.at[1])

    @unless(inside[(1, 0)])
    def _():
        nfx[0, :, :, 256:512] = jnp.zeros((4, 25, 256), F32)
        rx[1] = jnp.zeros((4, 25, 256), F32)

    @unless(inside[(-1, 0)])
    def _():
        nfx[1, :, :, 0:256] = jnp.zeros((4, 25, 256), F32)
        rx[0] = jnp.zeros((4, 25, 256), F32)

    @unless(inside[(0, 1)])
    def _():
        for x in range(2):
            nfy[0, :, :, :, 256 * x + 128 : 256 * x + 256] = jnp.zeros((4, 5, 5, 128), F32)
        ry[1] = jnp.zeros((4, 40, 256), F32)

    @unless(inside[(0, -1)])
    def _():
        for x in range(2):
            nfy[1, :, :, :, 256 * x : 256 * x + 128] = jnp.zeros((4, 5, 5, 128), F32)
        ry[0] = jnp.zeros((4, 40, 256), F32)

    for n, (dx, dy) in enumerate(DIRS):

        @unless(exists(-dx, -dy))
        def _():
            r2[n] = jnp.zeros((128, 128), F32)
            r3[n] = jnp.zeros((128, 128), F32)

    pl.semaphore_wait(barrier, greeted)

    sent = []

    def send(src, dst, ssem, rsem, dx, dy):
        copy = pltpu.make_async_remote_copy(
            src_ref=src, dst_ref=dst, send_sem=ssem, recv_sem=rsem, device_id=peer(dx, dy), device_id_type=MESH
        )

        @pl.when(exists(dx, dy))
        def _():
            copy.start()

        sent.append((copy, dx, dy))
        return sent[-1]

    def receive(copies):
        for copy, dx, dy in copies:

            @pl.when(exists(-dx, -dy))
            def _():
                copy.wait_recv()

    first = [
        send(xx.at[:, 4, :, 1, 0, :], nfx.at[1, :, :, pl.ds(0, 256)], ssem1.at[0], rsem1.at[0], 1, 0),
        send(xx.at[:, 0, :, 0, 0, :], nfx.at[0, :, :, pl.ds(256, 256)], ssem1.at[1], rsem1.at[1], -1, 0),
    ]
    for x in range(2):
        first.append(
            send(xy.at[:, :, 4, :, x, 1, 0, :], nfy.at[1, :, :, :, pl.ds(256 * x, 128)],
                 ssem1.at[2 + 2 * x], rsem1.at[2 + 2 * x], 0, 1)
        )
        first.append(
            send(xy.at[:, :, 0, :, x, 0, 0, :], nfy.at[0, :, :, :, pl.ds(256 * x + 128, 128)],
                 ssem1.at[3 + 2 * x], rsem1.at[3 + 2 * x], 0, -1)
        )

    for copy in local[0:4]:
        copy.wait()
    basis = [[ub[p, q] for q in range(5)] for p in range(5)]
    for weights in linear_values():
        basis.append([sum(float(weights[i]) * basis[i][q] for i in range(5)) for q in range(5)])
    spectrum = [mv[q] for q in range(5)]

    def mode_index(shape):
        row = iota(shape, 0)
        i = (row * 41) >> 10
        rest = row - 25 * i
        j = (rest * 13) >> 6
        return i, j, rest - 5 * j

    def block(start):
        modes = mode_index((128, 128))
        result = None
        for d in range(3):
            index = tab[d : d + 1, start : start + 128]
            hits = [index == p for p in range(7)]
            grown = jnp.zeros((128, 128), F32)
            for q in range(5):
                line = jnp.zeros((1, 128), F32)
                for p in range(7):
                    line = jnp.where(hits[p], basis[p][q], line)
                grown = jnp.where(modes[d] == q, line, grown)
            result = grown if result is None else result * grown
        return result

    nodes = block(0)
    bt_h[...], bt_l[...] = split(nodes)
    high, low = split(nodes.T)
    turn[...] = jnp.concatenate([high, high, low], axis=1)
    for part in range(2):
        faces = block(128 + 128 * part)
        span = pl.ds(128 * part, 128)
        bte_h[:, span], bte_l[:, span] = split(faces)
        fb_h[span, :], fb_l[span, :] = split(faces.T)
    for c in range(4):
        high, low = split(block(640 + 128 * c))
        sel_h[c] = jnp.concatenate([high, high], axis=1)
        sel_l[c] = low
    field = tab[3:4, 384:512]
    coarse_block = block(384)
    copy_of = iota((128, 128), 1)
    for f in range(4):
        part = jnp.where(field == f, coarse_block, 0.0)
        high, low = split(part)
        tc[pl.ds(128 * f, 128), :] = jnp.where(copy_of < 64, high.astype(F32), low.astype(F32)).astype(BF16)
        high, low = split(part.T[0:32])
        qc[0:32, pl.ds(128 * f, 128)] = high
        qc[32:64, pl.ds(128 * f, 128)] = low
    field = tab[3:4, 512:640]
    face_block = block(512)
    for f in range(4):
        part = jnp.where(field == f, face_block, 0.0)
        high, low = split(part)
        tf_h[pl.ds(128 * f, 128), :] = jnp.concatenate([high, high], axis=1)
        tf_l[pl.ds(128 * f, 128), :] = low
        high, low = split(part.T[0:96])
        qf[0:96, pl.ds(128 * f, 128)] = high
        qf[96:192, pl.ds(128 * f, 128)] = low

    modes = mode_index((128, 128))
    total = jnp.zeros((128, 128), F32)
    for d in range(3):
        for q in range(5):
            total = jnp.where(modes[d] == q, total + spectrum[q], total)

    def diagonal(c):
        return total * coef[c : c + 1, :] + 1.0

    for c in range(4):
        dinv[:, pl.ds(128 * c, 128)] = 1.0 / diagonal(c)

    local[4].wait()
    local[5].wait()
    for f in range(4):
        xhat[f] = mm3(bt_h[...], bt_l[...], rows_to(xin[f], 128))
        bhat[f] = mm3(bt_h[...], bt_l[...], rows_to(bin_[f], 128))

    local[6].wait()
    local[7].wait()
    elements = pe[...]
    alive = pm[...] != 0
    at_x = (elements >> 11) - 2 * px + 1
    at_y = ((elements >> 7) & 15) - 2 * py + 1
    at_z = elements & 127

    def least(v, most):
        return jnp.minimum(jnp.min(jnp.where(alive, v, most), axis=0, keepdims=True), most)

    low_x, low_y, low_z = least(at_x, 2), least(at_y, 2), least(at_z, 126)
    key = (low_x * 3 + low_y) * 128 + low_z
    place = (at_x - low_x) * 4 + (at_y - low_y) * 2 + (at_z - low_z)
    place = jnp.where(alive, place, 99)
    vertex = iota((128, LANES), 0)
    lowest = jnp.where(vertex == low_z, 1.0, 0.0).astype(BF16)
    zz[0:128, :] = lowest
    zz[128:256, :] = lowest
    for v in range(9):
        oh[pl.ds(128 * v, 128), :] = jnp.where(vertex + 128 * v == key, 1.0, 0.0).astype(BF16)

    local[8].wait()
    r = iota((256, 256), 0)
    source = (((r >> 1) & 3) * 8 + ((r >> 4) & 1) * 4 + ((r >> 3) & 1) * 2 + (r & 1)) * 8 + (r >> 5)
    order = jnp.where(iota((256, 256), 1) == source, 1.0, 0.0).astype(BF16)
    for piece, target in zip(split(pinv[...]), (mi_h, mi_l)):
        target[...] = dot_nt(dot(order, piece).astype(BF16), order).astype(BF16)

    for copy in local[9:]:
        copy.wait()

    none = jnp.zeros((32, 256), F32)
    gap = jnp.zeros((8, 128), F32)
    for f in range(4):
        parts = [
            jnp.concatenate([rows_to(nfx[0, f, :, 0:256], 32), none], axis=1),
            jnp.concatenate([none, rows_to(nfx[1, f, :, 256:512], 32)], axis=1),
        ]
        for i in range(5):
            near = [rows_to(nfy[0, f, i, :, 256 * x : 256 * x + 128], 8) for x in range(2)]
            parts.append(jnp.concatenate([near[0], gap, near[1], gap], axis=1))
        for i in range(5):
            near = [rows_to(nfy[1, f, i, :, 256 * x + 128 : 256 * x + 256], 8) for x in range(2)]
            parts.append(jnp.concatenate([gap, near[0], gap, near[1]], axis=1))
        parts.append(by_column(from_next, rows_to(nfz[0, f], 32)))
        parts.append(by_column(from_previous, rows_to(nfz[1, f], 32)))
        parts.append(jnp.zeros((48, LANES), F32))
        around = mm3(bte_h[...], bte_l[...], jnp.concatenate(parts, axis=0))
        x0 = xhat[f]
        zb[f] = 0.4 * (dinv[...] * (bhat[f] + 0.5 * around)) - 0.3 * x0
        diag = jnp.concatenate([diagonal(c) for c in range(4)], axis=1)
        rows = pl.ds(128 * f, 128)
        ts_h[rows, :], ts_l[rows, :] = split(bhat[f] - diag * x0)
    both = dot(qc[...], ts_h[...])
    inn[...] = 0.2 * (both[0:32] + both[32:64] + dot(qc[0:32, :], ts_l[...]))

    receive(first)

    for c in range(4):
        x, y = c // 2, c % 2
        lanes = slice(128 * c, 128 * c + 128)
        columns = []
        for f in range(4):
            parts = [rows_to(nfx[1 - x, f, :, lanes], 32)]
            parts += [rows_to(nfy[1 - y, f, i, :, lanes], 8) for i in range(5)]
            parts.append(jnp.zeros((56, 128), F32))
            columns.append(jnp.concatenate(parts, axis=0))
        high, low = split(jnp.concatenate(columns, axis=1))
        around = dot(sel_h[c], jnp.concatenate([high, low], axis=0)) + dot(sel_l[c], high)
        for f in range(4):
            z = zb[f, :, lanes] + 0.2 * (dinv[:, lanes] * around[:, 128 * f : 128 * f + 128])
            zb[f, :, lanes] = z
            rows = pl.ds(128 * f, 128)
            xs_h[rows, lanes], xs_l[rows, lanes] = split(z)

    inner = inn[...]
    both = dot(qf[...], xs_h[...])
    rim = both[0:96] + both[96:192] + dot(qf[0:96, :], xs_l[...])
    up_row = ((iota((32, 128), 0) & 1) == 1)

    def rim_of(start, size, c):
        return rim[start : start + size, 128 * c : 128 * c + 128]

    own = {}
    for x in range(2):
        for y in range(2):
            c = 2 * x + y
            v = inner[:, 128 * c : 128 * c + 128]
            faces = rim_of(64, 32, c)
            v = v + jnp.where(up_row, from_next(faces), from_previous(faces))
            v = add_a(v, 0, rim_of(0, 16, y)) if x == 1 else add_a(v, 1, rim_of(16, 16, 2 + y))
            v = add_b(v, 0, rim_of(32, 16, 2 * x)) if y == 1 else add_b(v, 1, rim_of(48, 16, 2 * x + 1))
            own[(x, y)] = v
    hx = {(1, y): rim_of(0, 16, 2 + y) for y in range(2)} | {(-1, y): rim_of(16, 16, y) for y in range(2)}
    hy = {(1, x): rim_of(32, 16, 2 * x + 1) for x in range(2)} | {(-1, x): rim_of(48, 16, 2 * x) for x in range(2)}

    def edge(d):
        return 1 if d == 1 else 0

    def exchange(blocks, sbuf, rbuf, ssem, rsem):
        copies = []
        for n, (dx, dy) in enumerate(DIRS):
            at = 0
            for v in blocks(dx, dy):
                sbuf[n, pl.ds(at, v.shape[0]), :] = v
                at += v.shape[0]
            copies.append(
                send(sbuf.at[n, pl.ds(0, at)], rbuf.at[n, pl.ds(0, at)], ssem.at[n], rsem.at[n], dx, dy)
            )
        return copies

    def residual_blocks(dx, dy):
        x, y = edge(dx), edge(dy)
        if dy == 0:
            return [own[(x, 0)], own[(x, 1)], hx[(dx, 0)], hx[(dx, 1)], hy[(1, x)], hy[(-1, x)]]
        if dx == 0:
            return [own[(0, y)], own[(1, y)], hy[(dy, 0)], hy[(dy, 1)], hx[(1, y)], hx[(-1, y)]]
        return [own[(x, y)], hx[(dx, y)], hy[(dy, x)]]

    second = exchange(residual_blocks, s2, r2, ssem2, rsem2)

    for f in range(4):
        rows = pl.ds(128 * f, 128)
        x1 = 2.0 * zb[f] + 0.8 * xhat[f]
        xhat[f] = x1
        xs_h[rows, :], xs_l[rows, :] = split(x1)
        for part in range(2):
            span = pl.ds(128 * part, 128)
            faces = (
                dot(fb_h[span, :], xs_h[rows, :])
                + dot(fb_h[span, :], xs_l[rows, :])
                + dot(fb_l[span, :], xs_h[rows, :])
            )
            fz[f, span, :] = faces
        sx[0, f] = fz[f, 0:25, 256:512]
        sx[1, f] = fz[f, 32:57, 0:256]
        for x in range(2):
            sy[0, f, :, pl.ds(128 * x, 128)] = fz[f, 64:104, 256 * x + 128 : 256 * x + 256]
            sy[1, f, :, pl.ds(128 * x, 128)] = fz[f, 104:144, 256 * x : 256 * x + 128]
    receive(second[6:])
    whole = [
        send(sx.at[0], rx.at[0], ssemf.at[0], rsemf.at[0], 1, 0),
        send(sx.at[1], rx.at[1], ssemf.at[1], rsemf.at[1], -1, 0),
        send(sy.at[0], ry.at[0], ssemf.at[2], rsemf.at[2], 0, 1),
        send(sy.at[1], ry.at[1], ssemf.at[3], rsemf.at[3], 0, -1),
    ]
    receive(second[:6])
    field_of = {}

    def put(at, v):
        field_of[at] = field_of[at] + v if at in field_of else v

    for at, v in own.items():
        put(at, v)
    late = []
    for y in range(2):
        late += [("a", 0, (2, y), hx[(1, y)]), ("a", 1, (-1, y), hx[(-1, y)])]
        late += [("b", 0, (y, 2), hy[(1, y)]), ("b", 1, (y, -1), hy[(-1, y)])]
    for n, (dx, dy) in enumerate(DIRS):
        x, y = edge(dx), edge(dy)
        side_a, side_b = (0 if dx == 1 else 1), (0 if dy == 1 else 1)
        if dy == 0:
            for t in range(2):
                put((x - 2 * dx, t), r2[n, 32 * t : 32 * t + 32, :])
                late.append(("a", side_a, (x - dx, t), r2[n, 64 + 16 * t : 80 + 16 * t, :]))
            late.append(("b", 0, (x - 2 * dx, 2), r2[n, 96:112, :]))
            late.append(("b", 1, (x - 2 * dx, -1), r2[n, 112:128, :]))
        elif dx == 0:
            for t in range(2):
                put((t, y - 2 * dy), r2[n, 32 * t : 32 * t + 32, :])
                late.append(("b", side_b, (t, y - dy), r2[n, 64 + 16 * t : 80 + 16 * t, :]))
            late.append(("a", 0, (2, y - 2 * dy), r2[n, 96:112, :]))
            late.append(("a", 1, (-1, y - 2 * dy), r2[n, 112:128, :]))
        else:
            put((x - 2 * dx, y - 2 * dy), r2[n, 0:32, :])
            late.append(("a", side_a, (x - dx, y - 2 * dy), r2[n, 32:48, :]))
            late.append(("b", side_b, (x - 2 * dx, y - dy), r2[n, 48:64, :]))
    for kind, side, at, v in late:
        field_of[at] = add_a(field_of[at], side, v) if kind == "a" else add_b(field_of[at], side, v)

    for (x, y), v in field_of.items():
        for z, value in enumerate((v, pltpu.roll(v, 127, 1))):
            rows = pl.ds(32 * (8 * (x + 1) + 2 * (y + 1) + z), 32)
            cz[rows, 0:128], cz[rows, 128:256] = split(value)
    halves = [pl.ds(256 * h, 256) for h in range(2)]

    def row_of(v, h):
        return jnp.broadcast_to(v[:, 256 * h : 256 * h + 256], (8, 256))

    def slots(h):
        return [row_of(place[t : t + 1], h) for t in range(8)]

    for half in halves:
        gz[:, half] = dot(cz[...], zz[:, half])
    for h, half in enumerate(halves):
        places = slots(h)
        in_x, in_y = row_of(low_x, h), row_of(low_y, h)
        x_one, x_two, y_one, y_two = in_x == 1, in_x == 2, in_y == 1, in_y == 2
        for t in range(4):

            def at(x, y, z):
                return gz[pl.ds(32 * (8 * x + 2 * y + z) + 8 * t, 8), half]

            cube = []
            for x in range(2):
                by_y = []
                for y in range(4):
                    by_y.append([
                        jnp.where(x_two, at(x + 2, y, z), jnp.where(x_one, at(x + 1, y, z), at(x, y, z)))
                        for z in range(2)
                    ])
                for y in range(2):
                    for z in range(2):
                        cube.append(jnp.where(y_two, by_y[y + 2][z], jnp.where(y_one, by_y[y + 1][z], by_y[y][z])))
            for slot in range(8):
                value = jnp.zeros((8, 256), F32)
                for p in range(8):
                    value = jnp.where(places[slot] == p, cube[p], value)
                wf[pl.ds(32 * slot + 8 * t, 8), half] = value
        wh, wl = split(wf[:, half])
        ans[:, half] = dot(mi_h[...], wh) + dot(mi_h[...], wl) + dot(mi_l[...], wh)
    for h, half in enumerate(halves):
        places = slots(h)
        for t in range(4):
            solved = [ans[pl.ds(32 * slot + 8 * t, 8), half] for slot in range(8)]
            for p in range(8):
                value = jnp.zeros((8, 256), F32)
                for slot in range(8):
                    value = jnp.where(places[slot] == p, solved[slot], value)
                wf[pl.ds(32 * p + 8 * t, 8), half] = value
        ap[0:256, half], ap[256:512, half] = split(wf[:, half])
    vv[...] = dot_nt(ap[pl.ds(0, 256), :], oh[...]) + dot_nt(ap[pl.ds(256, 256), :], oh[...])
    spread = {}
    for x in range(-1, 3):
        for y in range(-1, 3):
            sums = [None, None]
            for sx_, sy_ in ((0, 0), (0, 1), (1, 0), (1, 1)):
                vx, vy = x + 1 - sx_, y + 1 - sy_
                if 0 <= vx <= 2 and 0 <= vy <= 2:
                    for z in range(2):
                        p = sx_ * 4 + sy_ * 2 + z
                        v = vv[pl.ds(32 * p, 32), pl.ds(128 * (3 * vx + vy), 128)]
                        sums[z] = v if sums[z] is None else sums[z] + v
            spread[(x, y)] = sums[0] + pltpu.roll(sums[1], 1, 1)

    def correction_blocks(dx, dy):
        x, y = edge(dx), edge(dy)
        if dy == 0:
            return [
                spread[(x + dx, 0)], spread[(x + dx, 1)], a_half(spread[(x, 0)], x), a_half(spread[(x, 1)], x),
                b_half(spread[(x + dx, 2)], 0), b_half(spread[(x + dx, -1)], 1),
            ]
        if dx == 0:
            return [
                spread[(0, y + dy)], spread[(1, y + dy)], b_half(spread[(0, y)], y), b_half(spread[(1, y)], y),
                a_half(spread[(2, y + dy)], 0), a_half(spread[(-1, y + dy)], 1),
            ]
        return [spread[(x + dx, y + dy)], a_half(spread[(x, y + dy)], x), b_half(spread[(x + dx, y)], y)]

    third = exchange(correction_blocks, s3, r3, ssem3, rsem3)

    receive(whole)
    for f in range(4):
        x_up = jnp.concatenate([fz[f, 32:64, 256:512], rows_to(rx[1, f], 32)], axis=1)
        x_down = jnp.concatenate([rows_to(rx[0, f], 32), fz[f, 0:32, 0:256]], axis=1)
        y_up, y_down = [], []
        for x in range(2):
            y_up += [fz[f, 104:144, 256 * x + 128 : 256 * x + 256], ry[1, f, :, 128 * x : 128 * x + 128]]
            y_down += [ry[0, f, :, 128 * x : 128 * x + 128], fz[f, 64:104, 256 * x : 256 * x + 128]]
        parts = [
            x_up, x_down,
            jnp.concatenate(y_up, axis=1),
            jnp.concatenate(y_down, axis=1),
            by_column(from_next, fz[f, 176:208, :]),
            by_column(from_previous, fz[f, 144:176, :]),
            jnp.zeros((48, LANES), F32),
        ]
        around = mm3(bte_h[...], bte_l[...], jnp.concatenate(parts, axis=0))
        xhat[f] = 0.2 * xhat[f] + 0.8 * (dinv[...] * (bhat[f] + 0.5 * around))

    receive(third)
    fixed = {at: spread[at] for at in own}
    near_x = {(2, y): a_half(spread[(2, y)], 0) for y in range(2)} | {
        (-1, y): a_half(spread[(-1, y)], 1) for y in range(2)
    }
    near_y = {(x, 2): b_half(spread[(x, 2)], 0) for x in range(2)} | {
        (x, -1): b_half(spread[(x, -1)], 1) for x in range(2)
    }
    for n, (dx, dy) in enumerate(DIRS):
        x, y = edge(dx), edge(dy)
        if dy == 0:
            for t in range(2):
                fixed[(x - dx, t)] += r3[n, 32 * t : 32 * t + 32, :]
                near_x[(x - 2 * dx, t)] += r3[n, 64 + 16 * t : 80 + 16 * t, :]
            near_y[(x - dx, 2)] += r3[n, 96:112, :]
            near_y[(x - dx, -1)] += r3[n, 112:128, :]
        elif dx == 0:
            for t in range(2):
                fixed[(t, y - dy)] += r3[n, 32 * t : 32 * t + 32, :]
                near_y[(t, y - 2 * dy)] += r3[n, 64 + 16 * t : 80 + 16 * t, :]
            near_x[(2, y - dy)] += r3[n, 96:112, :]
            near_x[(-1, y - dy)] += r3[n, 112:128, :]
        else:
            fixed[(x - dx, y - dy)] += r3[n, 0:32, :]
            near_x[(x - 2 * dx, y - dy)] += r3[n, 32:48, :]
            near_y[(x - dx, y - 2 * dy)] += r3[n, 48:64, :]

    columns, rims = [], []
    for x in range(2):
        for y in range(2):
            v = fixed[(x, y)]
            columns.append(v)
            rims.append(
                jnp.concatenate(
                    [
                        a_half(fixed[(1, y)], 0) if x == 0 else near_x[(2, y)],
                        a_half(fixed[(0, y)], 1) if x == 1 else near_x[(-1, y)],
                        b_half(fixed[(x, 1)], 0) if y == 0 else near_y[(x, 2)],
                        b_half(fixed[(x, 0)], 1) if y == 1 else near_y[(x, -1)],
                        jnp.where(up_row, from_previous(v), from_next(v)),
                        jnp.zeros((32, 128), F32),
                    ],
                    axis=0,
                )
            )
    ch, cl = split(jnp.concatenate(columns, axis=1))
    stacked = jnp.concatenate([ch, cl, ch, jnp.zeros((32, LANES), BF16)], axis=0)
    rh, rl = split(jnp.concatenate(rims, axis=1))
    rims_both = jnp.concatenate([rh, rl], axis=0)
    for f in range(4):
        rows = pl.ds(128 * f, 128)
        direct = dot(tc[rows, :], stacked)
        coupled = dot(tf_h[rows, :], rims_both) + dot(tf_l[rows, :], rh)
        final = xhat[f] + 0.2 * direct + 0.4 * (dinv[...] * coupled)
        fin[f, 0:128, :], fin[f, 128:256, :] = split(final)
    for copy, dx, dy in sent:

        @pl.when(exists(dx, dy))
        def _():
            copy.wait_send()


def to_nodes(fin, turn, out, value, sem):
    copies = []
    for f in range(4):
        pieces = fin[f]
        nodes = dot(turn[:, 0:256], pieces) + dot(turn[:, 256:384], pieces[0:128])
        for c in range(4):
            value[pl.ds(500 * f + c, 125, stride=4), :] = nodes[0:125, 128 * c : 128 * c + 128]
        start, end = 500 * f // 8 * 8, 500 * (f + 1) // 8 * 8
        span = pl.ds(start, end - start)
        copies.append(pltpu.make_async_copy(value.at[span], out.at[span], sem.at[f]))
        copies[-1].start()
    for copy in copies:
        copy.wait()


def solution(mesh):
    nx, ny = mesh.shape["px"], mesh.shape["py"]
    table = column_table()

    def per_device(
        right_side, first_guess, coefficient, modal_basis, modal_values, patch_inverse, patch_elements, patch_mask
    ):
        hbm = pl.BlockSpec(memory_space=pltpu.HBM)

        def body(*refs):
            kernel(nx, ny, *refs)

        def f32(*shape):
            return pltpu.VMEM(shape, F32)

        def b16(*shape):
            return pltpu.VMEM(shape, BF16)

        def in_hbm(array):
            return pltpu.with_memory_space_constraint(array, pltpu.HBM)

        dma = pltpu.SemaphoreType.DMA
        fin, turn = pl.pallas_call(
            body,
            out_shape=(pltpu.VMEM((4, 256, 512), BF16), pltpu.VMEM((128, 384), BF16)),
            in_specs=[hbm] * 12,
            out_specs=(pl.BlockSpec(memory_space=pltpu.VMEM),) * 2,
            scratch_shapes=[
                pltpu.SMEM((5, 5), F32), pltpu.SMEM((5,), F32),
                f32(4, 125, 512), f32(4, 125, 512), f32(2, 4, 25, 512), f32(2, 4, 5, 5, 512), f32(2, 4, 25, 512),
                f32(4, 128), f32(256, 256), pltpu.VMEM((8, 512), jnp.int32), pltpu.VMEM((8, 512), jnp.int32),
                pltpu.VMEM((8, 1152), jnp.int32),
                b16(128, 128), b16(128, 128), b16(128, 256), b16(128, 256),
                b16(256, 128), b16(256, 128),
                b16(4, 128, 256), b16(4, 128, 128), f32(4, 128, 512), f32(32, 512), b16(64, 512), b16(192, 512),
                b16(512, 128), b16(512, 256), b16(512, 128), b16(256, 256), b16(256, 256),
                f32(4, 128, 512), f32(4, 128, 512), f32(128, 512), b16(1152, 512),
                b16(512, 512), b16(512, 512), b16(512, 512), b16(512, 512),
                b16(1024, 256), b16(256, 512), f32(1024, 512), f32(256, 512), f32(256, 512), b16(512, 512),
                f32(256, 1152),
                f32(2, 4, 25, 256), f32(2, 4, 40, 256), f32(2, 4, 25, 256), f32(2, 4, 40, 256), f32(4, 256, 512),
                f32(8, 128, 128), f32(8, 128, 128), f32(8, 128, 128), f32(8, 128, 128),
                dma((20,)), dma((6,)), dma((6,)), dma((4,)), dma((4,)), dma((8,)), dma((8,)), dma((8,)), dma((8,)),
            ],
            compiler_params=pltpu.CompilerParams(
                collective_id=0, has_side_effects=True, vmem_limit_bytes=60 * 1024 * 1024
            ),
        )(
            in_hbm(first_guess.reshape(4, 125, 1, 512)),
            in_hbm(first_guess.reshape(4, 5, 25, 2, 1, 256)),
            in_hbm(first_guess.reshape(4, 5, 5, 5, 2, 2, 1, 128)),
            in_hbm(first_guess.reshape(4, 25, 5, 1, 512)),
            in_hbm(right_side.reshape(4, 125, 1, 512)),
            in_hbm(coefficient.reshape(4, 128)),
            in_hbm(modal_basis),
            in_hbm(modal_values),
            in_hbm(patch_inverse),
            in_hbm(patch_elements.T),
            in_hbm(patch_mask.T),
            in_hbm(jnp.asarray(table)),
        )
        out = pl.pallas_call(
            to_nodes,
            out_shape=jax.ShapeDtypeStruct((2000, 128), F32),
            in_specs=[pl.BlockSpec(memory_space=pltpu.VMEM)] * 2,
            out_specs=pl.BlockSpec(memory_space=pl.ANY),
            scratch_shapes=[f32(2016, 128), dma((4,))],
            compiler_params=pltpu.CompilerParams(vmem_limit_bytes=16 * 1024 * 1024),
        )(fin, turn)
        return out.reshape(4, 5, 5, 5, 2, 2, 128)

    grid = P(None, None, None, None, "px", "py", None)
    rows = P(("px", "py"), None)
    return jax.shard_map(
        per_device,
        mesh=mesh,
        in_specs=(grid, grid, P("px", "py", None), P(), P(), P(), rows, rows),
        out_specs=grid,
        check_vma=False,
    )
```

```python
import math

import jax
import jax.numpy as jnp
import numpy as np
from jax import lax
from jax.experimental import pallas as pl
from jax.experimental.pallas import tpu as pltpu
from jax.sharding import PartitionSpec as P

MESH = pl.DeviceIdType.MESH
F32 = jnp.float32
BF16 = jnp.bfloat16
DIRS = ((1, 1), (1, -1), (-1, 1), (-1, -1), (1, 0), (-1, 0), (0, 1), (0, -1))
LANES = 512


def linear_values():
    root = np.float32(math.sqrt(3.0 / 7.0))
    points = np.array([-1.0, -root, 0.0, root, 1.0], np.float32)
    half = np.float32(0.5)
    return (1 - points) * half, (1 + points) * half


def column_table():
    table = np.full((8, 1152), 7, np.int32)
    table[3] = 9

    def put(column, i, j, k, f=9):
        table[0:4, column] = (i, j, k, f)

    for n in range(125):
        put(n, n // 25, n // 5 % 5, n % 5)
    for g in range(25):
        u, v = g // 5, g % 5
        put(128 + g, 4, u, v)
        put(160 + g, 0, u, v)
        put(192 + u * 8 + v, u, 4, v)
        put(232 + u * 8 + v, u, 0, v)
        put(272 + g, u, v, 4)
        put(304 + g, u, v, 0)
    for c in range(4):
        for g in range(25):
            u, v = g // 5, g % 5
            put(640 + 128 * c + g, 4 if c >= 2 else 0, u, v)
            put(672 + 128 * c + u * 8 + v, u, 4 if c % 2 else 0, v)
    for r in range(32):
        a, b, f, c = r // 16, r // 8 % 2, r // 2 % 4, r % 2
        for copy in range(3):
            put(384 + 32 * copy + r, 5 + a, 5 + b, 5 + c, f)
        put(512 + 64 + r, 5 + a, 5 + b, 4 if c == 0 else 0, f)
    for r in range(16):
        h, f, c = r // 8, r // 2 % 4, r % 2
        put(512 + r, 4, 5 + h, 5 + c, f)
        put(528 + r, 0, 5 + h, 5 + c, f)
        put(544 + r, 5 + h, 4, 5 + c, f)
        put(560 + r, 5 + h, 0, 5 + c, f)
    return table


def split(value):
    high = value.astype(BF16)
    return high, (value - high.astype(F32)).astype(BF16)


def dot(a, b):
    return lax.dot_general(a, b, (((1,), (0,)), ((), ())), preferred_element_type=F32)


def dot_nt(a, b):
    return lax.dot_general(a, b, (((1,), (1,)), ((), ())), preferred_element_type=F32)


def mm3(ah, al, x):
    xh, xl = split(x)
    return dot(ah, xh) + dot(ah, xl) + dot(al, xh)


def iota(shape, dim):
    return lax.broadcasted_iota(jnp.int32, shape, dim)


def a_half(v, a):
    return v[16 * a : 16 * a + 16]


def b_half(v, b):
    return jnp.concatenate([v[8 * b : 8 * b + 8], v[16 + 8 * b : 24 + 8 * b]], axis=0)


def add_a(v, a, h):
    parts = [v[0:16], v[16:32]]
    parts[a] = parts[a] + h
    return jnp.concatenate(parts, axis=0)


def add_b(v, b, h):
    parts = [v[0:8], v[8:16], v[16:24], v[24:32]]
    parts[b] = parts[b] + h[0:8]
    parts[2 + b] = parts[2 + b] + h[8:16]
    return jnp.concatenate(parts, axis=0)


def rows_to(v, rows):
    return jnp.concatenate([v, jnp.zeros((rows - v.shape[0], v.shape[1]), v.dtype)], axis=0)


def from_next(v):
    lane = iota(v.shape, 1)
    return jnp.where(lane == 127, 0.0, pltpu.roll(v, 127, 1))


def from_previous(v):
    lane = iota(v.shape, 1)
    return jnp.where(lane == 0, 0.0, pltpu.roll(v, 1, 1))


def by_column(fn, v):
    return jnp.concatenate([fn(v[:, 128 * c : 128 * c + 128]) for c in range(4)], axis=1)


def kernel(
    nx, ny,
    xa, xx, xy, xz, ba, coef_h, ub_h, mv_h, pinv_h, pe_h, pm_h, tab_h,
    fin, turn,
    ub, mv, xin, bin_, nfx, nfy, nfz, coef, pinv, pe, pm, tab,
    bt_h, bt_l, bte_h, bte_l, fb_h, fb_l,
    sel_h, sel_l, zb, inn, qc, qf, tc, tf_h, tf_l, mi_h, mi_l,
    xhat, bhat, dinv, oh, xs_h, xs_l, ts_h, ts_l,
    cz, zz, gz, wf, ans, ap, vv,
    sx, sy, rx, ry, fz, s2, r2, s3, r3,
    lsem, ssem1, rsem1, ssemf, rsemf, ssem2, rsem2, ssem3, rsem3,
):
    px, py = lax.axis_index("px"), lax.axis_index("py")

    def peer(dx, dy):
        return (lax.rem(px + dx + nx, nx), lax.rem(py + dy + ny, ny))

    inside = {(1, 0): px < nx - 1, (-1, 0): px > 0, (0, 1): py < ny - 1, (0, -1): py > 0}

    def exists(dx, dy):
        if dx == 0 or dy == 0:
            return inside[(dx, dy)]
        return inside[(dx, 0)] & inside[(0, dy)]

    def unless(condition):
        return pl.when(jnp.logical_not(condition))

    barrier = pltpu.get_barrier_semaphore()
    greeted = 0
    for dx, dy in DIRS[4:]:
        greeted = greeted + jnp.where(exists(dx, dy), 1, 0)

        @pl.when(exists(dx, dy))
        def _():
            pl.semaphore_signal(barrier, inc=1, device_id=peer(dx, dy), device_id_type=MESH)

    local = []

    def load(src, dst):
        copy = pltpu.make_async_copy(src, dst, lsem.at[len(local)])
        copy.start()
        local.append(copy)

    load(tab_h, tab)
    load(coef_h, coef)
    load(ub_h, ub)
    load(mv_h, mv)
    load(xa.at[:, :, 0, :], xin)
    load(ba.at[:, :, 0, :], bin_)
    load(pe_h, pe)
    load(pm_h, pm)
    load(pinv_h, pinv)
    load(xx.at[:, 0, :, 1, 0, :], nfx.at[0, :, :, pl.ds(0, 256)])
    load(xx.at[:, 4, :, 0, 0, :], nfx.at[1, :, :, pl.ds(256, 256)])
    for x in range(2):
        load(xy.at[:, :, 0, :, x, 1, 0, :], nfy.at[0, :, :, :, pl.ds(256 * x, 128)])
        load(xy.at[:, :, 4, :, x, 0, 0, :], nfy.at[1, :, :, :, pl.ds(256 * x + 128, 128)])
    load(xz.at[:, :, 0, 0, :], nfz.at[0])
    load(xz.at[:, :, 4, 0, :], nfz.at[1])

    @unless(inside[(1, 0)])
    def _():
        nfx[0, :, :, 256:512] = jnp.zeros((4, 25, 256), F32)
        rx[1] = jnp.zeros((4, 25, 256), F32)

    @unless(inside[(-1, 0)])
    def _():
        nfx[1, :, :, 0:256] = jnp.zeros((4, 25, 256), F32)
        rx[0] = jnp.zeros((4, 25, 256), F32)

    @unless(inside[(0, 1)])
    def _():
        for x in range(2):
            nfy[0, :, :, :, 256 * x + 128 : 256 * x + 256] = jnp.zeros((4, 5, 5, 128), F32)
        ry[1] = jnp.zeros((4, 40, 256), F32)

    @unless(inside[(0, -1)])
    def _():
        for x in range(2):
            nfy[1, :, :, :, 256 * x : 256 * x + 128] = jnp.zeros((4, 5, 5, 128), F32)
        ry[0] = jnp.zeros((4, 40, 256), F32)

    for n, (dx, dy) in enumerate(DIRS):

        @unless(exists(-dx, -dy))
        def _():
            r2[n] = jnp.zeros((128, 128), F32)
            r3[n] = jnp.zeros((128, 128), F32)

    pl.semaphore_wait(barrier, greeted)

    sent = []

    def send(src, dst, ssem, rsem, dx, dy):
        copy = pltpu.make_async_remote_copy(
            src_ref=src, dst_ref=dst, send_sem=ssem, recv_sem=rsem, device_id=peer(dx, dy), device_id_type=MESH
        )

        @pl.when(exists(dx, dy))
        def _():
            copy.start()

        sent.append((copy, dx, dy))
        return sent[-1]

    def receive(copies):
        for copy, dx, dy in copies:

            @pl.when(exists(-dx, -dy))
            def _():
                copy.wait_recv()

    first = [
        send(xx.at[:, 4, :, 1, 0, :], nfx.at[1, :, :, pl.ds(0, 256)], ssem1.at[0], rsem1.at[0], 1, 0),
        send(xx.at[:, 0, :, 0, 0, :], nfx.at[0, :, :, pl.ds(256, 256)], ssem1.at[1], rsem1.at[1], -1, 0),
    ]
    for x in range(2):
        first.append(
            send(xy.at[:, :, 4, :, x, 1, 0, :], nfy.at[1, :, :, :, pl.ds(256 * x, 128)],
                 ssem1.at[2 + 2 * x], rsem1.at[2 + 2 * x], 0, 1)
        )
        first.append(
            send(xy.at[:, :, 0, :, x, 0, 0, :], nfy.at[0, :, :, :, pl.ds(256 * x + 128, 128)],
                 ssem1.at[3 + 2 * x], rsem1.at[3 + 2 * x], 0, -1)
        )

    for copy in local[0:4]:
        copy.wait()
    basis = [[ub[p, q] for q in range(5)] for p in range(5)]
    for weights in linear_values():
        basis.append([sum(float(weights[i]) * basis[i][q] for i in range(5)) for q in range(5)])
    spectrum = [mv[q] for q in range(5)]

    def mode_index(shape):
        row = iota(shape, 0)
        i = (row * 41) >> 10
        rest = row - 25 * i
        j = (rest * 13) >> 6
        return i, j, rest - 5 * j

    def block(start):
        modes = mode_index((128, 128))
        result = None
        for d in range(3):
            index = tab[d : d + 1, start : start + 128]
            hits = [index == p for p in range(7)]
            grown = jnp.zeros((128, 128), F32)
            for q in range(5):
                line = jnp.zeros((1, 128), F32)
                for p in range(7):
                    line = jnp.where(hits[p], basis[p][q], line)
                grown = jnp.where(modes[d] == q, line, grown)
            result = grown if result is None else result * grown
        return result

    nodes = block(0)
    bt_h[...], bt_l[...] = split(nodes)
    high, low = split(nodes.T)
    turn[...] = jnp.concatenate([high, high, low], axis=1)
    for part in range(2):
        faces = block(128 + 128 * part)
        span = pl.ds(128 * part, 128)
        bte_h[:, span], bte_l[:, span] = split(faces)
        fb_h[span, :], fb_l[span, :] = split(faces.T)
    for c in range(4):
        high, low = split(block(640 + 128 * c))
        sel_h[c] = jnp.concatenate([high, high], axis=1)
        sel_l[c] = low
    field = tab[3:4, 384:512]
    coarse_block = block(384)
    copy_of = iota((128, 128), 1)
    for f in range(4):
        part = jnp.where(field == f, coarse_block, 0.0)
        high, low = split(part)
        tc[pl.ds(128 * f, 128), :] = jnp.where(copy_of < 64, high.astype(F32), low.astype(F32)).astype(BF16)
        high, low = split(part.T[0:32])
        qc[0:32, pl.ds(128 * f, 128)] = high
        qc[32:64, pl.ds(128 * f, 128)] = low
    field = tab[3:4, 512:640]
    face_block = block(512)
    for f in range(4):
        part = jnp.where(field == f, face_block, 0.0)
        high, low = split(part)
        tf_h[pl.ds(128 * f, 128), :] = jnp.concatenate([high, high], axis=1)
        tf_l[pl.ds(128 * f, 128), :] = low
        high, low = split(part.T[0:96])
        qf[0:96, pl.ds(128 * f, 128)] = high
        qf[96:192, pl.ds(128 * f, 128)] = low

    modes = mode_index((128, 128))
    total = jnp.zeros((128, 128), F32)
    for d in range(3):
        for q in range(5):
            total = jnp.where(modes[d] == q, total + spectrum[q], total)

    def diagonal(c):
        return total * coef[c : c + 1, :] + 1.0

    for c in range(4):
        dinv[:, pl.ds(128 * c, 128)] = 1.0 / diagonal(c)

    local[4].wait()
    local[5].wait()
    for f in range(4):
        xhat[f] = mm3(bt_h[...], bt_l[...], rows_to(xin[f], 128))
        bhat[f] = mm3(bt_h[...], bt_l[...], rows_to(bin_[f], 128))

    local[6].wait()
    local[7].wait()
    elements = pe[...]
    alive = pm[...] != 0
    at_x = (elements >> 11) - 2 * px + 1
    at_y = ((elements >> 7) & 15) - 2 * py + 1
    at_z = elements & 127

    def least(v, most):
        return jnp.minimum(jnp.min(jnp.where(alive, v, most), axis=0, keepdims=True), most)

    low_x, low_y, low_z = least(at_x, 2), least(at_y, 2), least(at_z, 126)
    key = (low_x * 3 + low_y) * 128 + low_z
    place = (at_x - low_x) * 4 + (at_y - low_y) * 2 + (at_z - low_z)
    place = jnp.where(alive, place, 99)
    vertex = iota((128, LANES), 0)
    lowest = jnp.where(vertex == low_z, 1.0, 0.0).astype(BF16)
    zz[0:128, :] = lowest
    zz[128:256, :] = lowest
    for v in range(9):
        oh[pl.ds(128 * v, 128), :] = jnp.where(vertex + 128 * v == key, 1.0, 0.0).astype(BF16)

    local[8].wait()
    r = iota((256, 256), 0)
    source = (((r >> 1) & 3) * 8 + ((r >> 4) & 1) * 4 + ((r >> 3) & 1) * 2 + (r & 1)) * 8 + (r >> 5)
    order = jnp.where(iota((256, 256), 1) == source, 1.0, 0.0).astype(BF16)
    for piece, target in zip(split(pinv[...]), (mi_h, mi_l)):
        target[...] = dot_nt(dot(order, piece).astype(BF16), order).astype(BF16)

    for copy in local[9:]:
        copy.wait()

    none = jnp.zeros((32, 256), F32)
    gap = jnp.zeros((8, 128), F32)
    for f in range(4):
        parts = [
            jnp.concatenate([rows_to(nfx[0, f, :, 0:256], 32), none], axis=1),
            jnp.concatenate([none, rows_to(nfx[1, f, :, 256:512], 32)], axis=1),
        ]
        for i in range(5):
            near = [rows_to(nfy[0, f, i, :, 256 * x : 256 * x + 128], 8) for x in range(2)]
            parts.append(jnp.concatenate([near[0], gap, near[1], gap], axis=1))
        for i in range(5):
            near = [rows_to(nfy[1, f, i, :, 256 * x + 128 : 256 * x + 256], 8) for x in range(2)]
            parts.append(jnp.concatenate([gap, near[0], gap, near[1]], axis=1))
        parts.append(by_column(from_next, rows_to(nfz[0, f], 32)))
        parts.append(by_column(from_previous, rows_to(nfz[1, f], 32)))
        parts.append(jnp.zeros((48, LANES), F32))
        around = mm3(bte_h[...], bte_l[...], jnp.concatenate(parts, axis=0))
        x0 = xhat[f]
        zb[f] = 0.4 * (dinv[...] * (bhat[f] + 0.5 * around)) - 0.3 * x0
        diag = jnp.concatenate([diagonal(c) for c in range(4)], axis=1)
        rows = pl.ds(128 * f, 128)
        ts_h[rows, :], ts_l[rows, :] = split(bhat[f] - diag * x0)
    both = dot(qc[...], ts_h[...])
    inn[...] = 0.2 * (both[0:32] + both[32:64] + dot(qc[0:32, :], ts_l[...]))

    receive(first)

    for c in range(4):
        x, y = c // 2, c % 2
        lanes = slice(128 * c, 128 * c + 128)
        columns = []
        for f in range(4):
            parts = [rows_to(nfx[1 - x, f, :, lanes], 32)]
            parts += [rows_to(nfy[1 - y, f, i, :, lanes], 8) for i in range(5)]
            parts.append(jnp.zeros((56, 128), F32))
            columns.append(jnp.concatenate(parts, axis=0))
        high, low = split(jnp.concatenate(columns, axis=1))
        around = dot(sel_h[c], jnp.concatenate([high, low], axis=0)) + dot(sel_l[c], high)
        for f in range(4):
            z = zb[f, :, lanes] + 0.2 * (dinv[:, lanes] * around[:, 128 * f : 128 * f + 128])
            zb[f, :, lanes] = z
            rows = pl.ds(128 * f, 128)
            xs_h[rows, lanes], xs_l[rows, lanes] = split(z)

    inner = inn[...]
    both = dot(qf[...], xs_h[...])
    rim = both[0:96] + both[96:192] + dot(qf[0:96, :], xs_l[...])
    up_row = ((iota((32, 128), 0) & 1) == 1)

    def rim_of(start, size, c):
        return rim[start : start + size, 128 * c : 128 * c + 128]

    own = {}
    for x in range(2):
        for y in range(2):
            c = 2 * x + y
            v = inner[:, 128 * c : 128 * c + 128]
            faces = rim_of(64, 32, c)
            v = v + jnp.where(up_row, from_next(faces), from_previous(faces))
            v = add_a(v, 0, rim_of(0, 16, y)) if x == 1 else add_a(v, 1, rim_of(16, 16, 2 + y))
            v = add_b(v, 0, rim_of(32, 16, 2 * x)) if y == 1 else add_b(v, 1, rim_of(48, 16, 2 * x + 1))
            own[(x, y)] = v
    hx = {(1, y): rim_of(0, 16, 2 + y) for y in range(2)} | {(-1, y): rim_of(16, 16, y) for y in range(2)}
    hy = {(1, x): rim_of(32, 16, 2 * x + 1) for x in range(2)} | {(-1, x): rim_of(48, 16, 2 * x) for x in range(2)}

    def edge(d):
        return 1 if d == 1 else 0

    def exchange(blocks, sbuf, rbuf, ssem, rsem):
        copies = []
        for n, (dx, dy) in enumerate(DIRS):
            at = 0
            for v in blocks(dx, dy):
                sbuf[n, pl.ds(at, v.shape[0]), :] = v
                at += v.shape[0]
            copies.append(
                send(sbuf.at[n, pl.ds(0, at)], rbuf.at[n, pl.ds(0, at)], ssem.at[n], rsem.at[n], dx, dy)
            )
        return copies

    def residual_blocks(dx, dy):
        x, y = edge(dx), edge(dy)
        if dy == 0:
            return [own[(x, 0)], own[(x, 1)], hx[(dx, 0)], hx[(dx, 1)], hy[(1, x)], hy[(-1, x)]]
        if dx == 0:
            return [own[(0, y)], own[(1, y)], hy[(dy, 0)], hy[(dy, 1)], hx[(1, y)], hx[(-1, y)]]
        return [own[(x, y)], hx[(dx, y)], hy[(dy, x)]]

    second = exchange(residual_blocks, s2, r2, ssem2, rsem2)

    for f in range(4):
        rows = pl.ds(128 * f, 128)
        x1 = 2.0 * zb[f] + 0.8 * xhat[f]
        xhat[f] = x1
        xs_h[rows, :], xs_l[rows, :] = split(x1)
        for part in range(2):
            span = pl.ds(128 * part, 128)
            faces = (
                dot(fb_h[span, :], xs_h[rows, :])
                + dot(fb_h[span, :], xs_l[rows, :])
                + dot(fb_l[span, :], xs_h[rows, :])
            )
            fz[f, span, :] = faces
        sx[0, f] = fz[f, 0:25, 256:512]
        sx[1, f] = fz[f, 32:57, 0:256]
        for x in range(2):
            sy[0, f, :, pl.ds(128 * x, 128)] = fz[f, 64:104, 256 * x + 128 : 256 * x + 256]
            sy[1, f, :, pl.ds(128 * x, 128)] = fz[f, 104:144, 256 * x : 256 * x + 128]
    whole = [
        send(sy.at[0], ry.at[0], ssemf.at[2], rsemf.at[2], 0, 1),
        send(sy.at[1], ry.at[1], ssemf.at[3], rsemf.at[3], 0, -1),
    ]
    receive(second[6:])
    whole += [
        send(sx.at[0], rx.at[0], ssemf.at[0], rsemf.at[0], 1, 0),
        send(sx.at[1], rx.at[1], ssemf.at[1], rsemf.at[1], -1, 0),
    ]
    receive(second[:6])
    field_of = {}

    def put(at, v):
        field_of[at] = field_of[at] + v if at in field_of else v

    for at, v in own.items():
        put(at, v)
    late = []
    for y in range(2):
        late += [("a", 0, (2, y), hx[(1, y)]), ("a", 1, (-1, y), hx[(-1, y)])]
        late += [("b", 0, (y, 2), hy[(1, y)]), ("b", 1, (y, -1), hy[(-1, y)])]
    for n, (dx, dy) in enumerate(DIRS):
        x, y = edge(dx), edge(dy)
        side_a, side_b = (0 if dx == 1 else 1), (0 if dy == 1 else 1)
        if dy == 0:
            for t in range(2):
                put((x - 2 * dx, t), r2[n, 32 * t : 32 * t + 32, :])
                late.append(("a", side_a, (x - dx, t), r2[n, 64 + 16 * t : 80 + 16 * t, :]))
            late.append(("b", 0, (x - 2 * dx, 2), r2[n, 96:112, :]))
            late.append(("b", 1, (x - 2 * dx, -1), r2[n, 112:128, :]))
        elif dx == 0:
            for t in range(2):
                put((t, y - 2 * dy), r2[n, 32 * t : 32 * t + 32, :])
                late.append(("b", side_b, (t, y - dy), r2[n, 64 + 16 * t : 80 + 16 * t, :]))
            late.append(("a", 0, (2, y - 2 * dy), r2[n, 96:112, :]))
            late.append(("a", 1, (-1, y - 2 * dy), r2[n, 112:128, :]))
        else:
            put((x - 2 * dx, y - 2 * dy), r2[n, 0:32, :])
            late.append(("a", side_a, (x - dx, y - 2 * dy), r2[n, 32:48, :]))
            late.append(("b", side_b, (x - 2 * dx, y - dy), r2[n, 48:64, :]))
    for kind, side, at, v in late:
        field_of[at] = add_a(field_of[at], side, v) if kind == "a" else add_b(field_of[at], side, v)

    for (x, y), v in field_of.items():
        for z, value in enumerate((v, pltpu.roll(v, 127, 1))):
            rows = pl.ds(32 * (8 * (x + 1) + 2 * (y + 1) + z), 32)
            cz[rows, 0:128], cz[rows, 128:256] = split(value)
    halves = [pl.ds(256 * h, 256) for h in range(2)]

    def row_of(v, h):
        return jnp.broadcast_to(v[:, 256 * h : 256 * h + 256], (8, 256))

    def slots(h):
        return [row_of(place[t : t + 1], h) for t in range(8)]

    for half in halves:
        gz[:, half] = dot(cz[...], zz[:, half])
    for h, half in enumerate(halves):
        places = slots(h)
        in_x, in_y = row_of(low_x, h), row_of(low_y, h)
        x_one, x_two, y_one, y_two = in_x == 1, in_x == 2, in_y == 1, in_y == 2
        for t in range(4):

            def at(x, y, z):
                return gz[pl.ds(32 * (8 * x + 2 * y + z) + 8 * t, 8), half]

            cube = []
            for x in range(2):
                by_y = []
                for y in range(4):
                    by_y.append([
                        jnp.where(x_two, at(x + 2, y, z), jnp.where(x_one, at(x + 1, y, z), at(x, y, z)))
                        for z in range(2)
                    ])
                for y in range(2):
                    for z in range(2):
                        cube.append(jnp.where(y_two, by_y[y + 2][z], jnp.where(y_one, by_y[y + 1][z], by_y[y][z])))
            for slot in range(8):
                value = jnp.zeros((8, 256), F32)
                for p in range(8):
                    value = jnp.where(places[slot] == p, cube[p], value)
                wf[pl.ds(32 * slot + 8 * t, 8), half] = value
        wh, wl = split(wf[:, half])
        ans[:, half] = dot(mi_h[...], wh) + dot(mi_h[...], wl) + dot(mi_l[...], wh)
    for h, half in enumerate(halves):
        places = slots(h)
        for t in range(4):
            solved = [ans[pl.ds(32 * slot + 8 * t, 8), half] for slot in range(8)]
            for p in range(8):
                value = jnp.zeros((8, 256), F32)
                for slot in range(8):
                    value = jnp.where(places[slot] == p, solved[slot], value)
                wf[pl.ds(32 * p + 8 * t, 8), half] = value
        ap[0:256, half], ap[256:512, half] = split(wf[:, half])
    vv[...] = dot_nt(ap[pl.ds(0, 256), :], oh[...]) + dot_nt(ap[pl.ds(256, 256), :], oh[...])
    spread = {}
    for x in range(-1, 3):
        for y in range(-1, 3):
            sums = [None, None]
            for sx_, sy_ in ((0, 0), (0, 1), (1, 0), (1, 1)):
                vx, vy = x + 1 - sx_, y + 1 - sy_
                if 0 <= vx <= 2 and 0 <= vy <= 2:
                    for z in range(2):
                        p = sx_ * 4 + sy_ * 2 + z
                        v = vv[pl.ds(32 * p, 32), pl.ds(128 * (3 * vx + vy), 128)]
                        sums[z] = v if sums[z] is None else sums[z] + v
            spread[(x, y)] = sums[0] + pltpu.roll(sums[1], 1, 1)

    def correction_blocks(dx, dy):
        x, y = edge(dx), edge(dy)
        if dy == 0:
            return [
                spread[(x + dx, 0)], spread[(x + dx, 1)], a_half(spread[(x, 0)], x), a_half(spread[(x, 1)], x),
                b_half(spread[(x + dx, 2)], 0), b_half(spread[(x + dx, -1)], 1),
            ]
        if dx == 0:
            return [
                spread[(0, y + dy)], spread[(1, y + dy)], b_half(spread[(0, y)], y), b_half(spread[(1, y)], y),
                a_half(spread[(2, y + dy)], 0), a_half(spread[(-1, y + dy)], 1),
            ]
        return [spread[(x + dx, y + dy)], a_half(spread[(x, y + dy)], x), b_half(spread[(x + dx, y)], y)]

    third = exchange(correction_blocks, s3, r3, ssem3, rsem3)

    receive(whole)
    for f in range(4):
        x_up = jnp.concatenate([fz[f, 32:64, 256:512], rows_to(rx[1, f], 32)], axis=1)
        x_down = jnp.concatenate([rows_to(rx[0, f], 32), fz[f, 0:32, 0:256]], axis=1)
        y_up, y_down = [], []
        for x in range(2):
            y_up += [fz[f, 104:144, 256 * x + 128 : 256 * x + 256], ry[1, f, :, 128 * x : 128 * x + 128]]
            y_down += [ry[0, f, :, 128 * x : 128 * x + 128], fz[f, 64:104, 256 * x : 256 * x + 128]]
        parts = [
            x_up, x_down,
            jnp.concatenate(y_up, axis=1),
            jnp.concatenate(y_down, axis=1),
            by_column(from_next, fz[f, 176:208, :]),
            by_column(from_previous, fz[f, 144:176, :]),
            jnp.zeros((48, LANES), F32),
        ]
        around = mm3(bte_h[...], bte_l[...], jnp.concatenate(parts, axis=0))
        xhat[f] = 0.2 * xhat[f] + 0.8 * (dinv[...] * (bhat[f] + 0.5 * around))

    receive(third)
    fixed = {at: spread[at] for at in own}
    near_x = {(2, y): a_half(spread[(2, y)], 0) for y in range(2)} | {
        (-1, y): a_half(spread[(-1, y)], 1) for y in range(2)
    }
    near_y = {(x, 2): b_half(spread[(x, 2)], 0) for x in range(2)} | {
        (x, -1): b_half(spread[(x, -1)], 1) for x in range(2)
    }
    for n, (dx, dy) in enumerate(DIRS):
        x, y = edge(dx), edge(dy)
        if dy == 0:
            for t in range(2):
                fixed[(x - dx, t)] += r3[n, 32 * t : 32 * t + 32, :]
                near_x[(x - 2 * dx, t)] += r3[n, 64 + 16 * t : 80 + 16 * t, :]
            near_y[(x - dx, 2)] += r3[n, 96:112, :]
            near_y[(x - dx, -1)] += r3[n, 112:128, :]
        elif dx == 0:
            for t in range(2):
                fixed[(t, y - dy)] += r3[n, 32 * t : 32 * t + 32, :]
                near_y[(t, y - 2 * dy)] += r3[n, 64 + 16 * t : 80 + 16 * t, :]
            near_x[(2, y - dy)] += r3[n, 96:112, :]
            near_x[(-1, y - dy)] += r3[n, 112:128, :]
        else:
            fixed[(x - dx, y - dy)] += r3[n, 0:32, :]
            near_x[(x - 2 * dx, y - dy)] += r3[n, 32:48, :]
            near_y[(x - dx, y - 2 * dy)] += r3[n, 48:64, :]

    columns, rims = [], []
    for x in range(2):
        for y in range(2):
            v = fixed[(x, y)]
            columns.append(v)
            rims.append(
                jnp.concatenate(
                    [
                        a_half(fixed[(1, y)], 0) if x == 0 else near_x[(2, y)],
                        a_half(fixed[(0, y)], 1) if x == 1 else near_x[(-1, y)],
                        b_half(fixed[(x, 1)], 0) if y == 0 else near_y[(x, 2)],
                        b_half(fixed[(x, 0)], 1) if y == 1 else near_y[(x, -1)],
                        jnp.where(up_row, from_previous(v), from_next(v)),
                        jnp.zeros((32, 128), F32),
                    ],
                    axis=0,
                )
            )
    ch, cl = split(jnp.concatenate(columns, axis=1))
    stacked = jnp.concatenate([ch, cl, ch, jnp.zeros((32, LANES), BF16)], axis=0)
    rh, rl = split(jnp.concatenate(rims, axis=1))
    rims_both = jnp.concatenate([rh, rl], axis=0)
    for f in range(4):
        rows = pl.ds(128 * f, 128)
        direct = dot(tc[rows, :], stacked)
        coupled = dot(tf_h[rows, :], rims_both) + dot(tf_l[rows, :], rh)
        final = xhat[f] + 0.2 * direct + 0.4 * (dinv[...] * coupled)
        fin[f, 0:128, :], fin[f, 128:256, :] = split(final)
    for copy, dx, dy in sent:

        @pl.when(exists(dx, dy))
        def _():
            copy.wait_send()


def to_nodes(fin, turn, out, value, sem):
    copies = []
    for f in range(4):
        pieces = fin[f]
        nodes = dot(turn[:, 0:256], pieces) + dot(turn[:, 256:384], pieces[0:128])
        for c in range(4):
            value[pl.ds(500 * f + c, 125, stride=4), :] = nodes[0:125, 128 * c : 128 * c + 128]
        start, end = 500 * f // 8 * 8, 500 * (f + 1) // 8 * 8
        span = pl.ds(start, end - start)
        copies.append(pltpu.make_async_copy(value.at[span], out.at[span], sem.at[f]))
        copies[-1].start()
    for copy in copies:
        copy.wait()


def solution(mesh):
    nx, ny = mesh.shape["px"], mesh.shape["py"]
    table = column_table()

    def per_device(
        right_side, first_guess, coefficient, modal_basis, modal_values, patch_inverse, patch_elements, patch_mask
    ):
        hbm = pl.BlockSpec(memory_space=pltpu.HBM)

        def body(*refs):
            kernel(nx, ny, *refs)

        def f32(*shape):
            return pltpu.VMEM(shape, F32)

        def b16(*shape):
            return pltpu.VMEM(shape, BF16)

        def in_hbm(array):
            return pltpu.with_memory_space_constraint(array, pltpu.HBM)

        dma = pltpu.SemaphoreType.DMA
        fin, turn = pl.pallas_call(
            body,
            out_shape=(pltpu.VMEM((4, 256, 512), BF16), pltpu.VMEM((128, 384), BF16)),
            in_specs=[hbm] * 12,
            out_specs=(pl.BlockSpec(memory_space=pltpu.VMEM),) * 2,
            scratch_shapes=[
                pltpu.SMEM((5, 5), F32), pltpu.SMEM((5,), F32),
                f32(4, 125, 512), f32(4, 125, 512), f32(2, 4, 25, 512), f32(2, 4, 5, 5, 512), f32(2, 4, 25, 512),
                f32(4, 128), f32(256, 256), pltpu.VMEM((8, 512), jnp.int32), pltpu.VMEM((8, 512), jnp.int32),
                pltpu.VMEM((8, 1152), jnp.int32),
                b16(128, 128), b16(128, 128), b16(128, 256), b16(128, 256),
                b16(256, 128), b16(256, 128),
                b16(4, 128, 256), b16(4, 128, 128), f32(4, 128, 512), f32(32, 512), b16(64, 512), b16(192, 512),
                b16(512, 128), b16(512, 256), b16(512, 128), b16(256, 256), b16(256, 256),
                f32(4, 128, 512), f32(4, 128, 512), f32(128, 512), b16(1152, 512),
                b16(512, 512), b16(512, 512), b16(512, 512), b16(512, 512),
                b16(1024, 256), b16(256, 512), f32(1024, 512), f32(256, 512), f32(256, 512), b16(512, 512),
                f32(256, 1152),
                f32(2, 4, 25, 256), f32(2, 4, 40, 256), f32(2, 4, 25, 256), f32(2, 4, 40, 256), f32(4, 256, 512),
                f32(8, 128, 128), f32(8, 128, 128), f32(8, 128, 128), f32(8, 128, 128),
                dma((20,)), dma((6,)), dma((6,)), dma((4,)), dma((4,)), dma((8,)), dma((8,)), dma((8,)), dma((8,)),
            ],
            compiler_params=pltpu.CompilerParams(
                collective_id=0, has_side_effects=True, vmem_limit_bytes=60 * 1024 * 1024
            ),
        )(
            in_hbm(first_guess.reshape(4, 125, 1, 512)),
            in_hbm(first_guess.reshape(4, 5, 25, 2, 1, 256)),
            in_hbm(first_guess.reshape(4, 5, 5, 5, 2, 2, 1, 128)),
            in_hbm(first_guess.reshape(4, 25, 5, 1, 512)),
            in_hbm(right_side.reshape(4, 125, 1, 512)),
            in_hbm(coefficient.reshape(4, 128)),
            in_hbm(modal_basis),
            in_hbm(modal_values),
            in_hbm(patch_inverse),
            in_hbm(patch_elements.T),
            in_hbm(patch_mask.T),
            in_hbm(jnp.asarray(table)),
        )
        out = pl.pallas_call(
            to_nodes,
            out_shape=jax.ShapeDtypeStruct((2000, 128), F32),
            in_specs=[pl.BlockSpec(memory_space=pltpu.VMEM)] * 2,
            out_specs=pl.BlockSpec(memory_space=pl.ANY),
            scratch_shapes=[f32(2016, 128), dma((4,))],
            compiler_params=pltpu.CompilerParams(vmem_limit_bytes=16 * 1024 * 1024),
        )(fin, turn)
        return out.reshape(4, 5, 5, 5, 2, 2, 128)

    grid = P(None, None, None, None, "px", "py", None)
    rows = P(("px", "py"), None)
    return jax.shard_map(
        per_device,
        mesh=mesh,
        in_specs=(grid, grid, P("px", "py", None), P(), P(), P(), rows, rows),
        out_specs=grid,
        check_vma=False,
    )
```
